32 devices in a mesh: dp: 8 (over z, y), bn: 4 (over x, core).
Axes of the slice: x: 2, y: 2, z: 4, core: 2. Of those that a mesh axis runs over, the one named last changes fastest.
Arguments:
- images: bfloat16 [32, 38, 38, 512], P(('dp', 'bn')), may hold values from -6 to 6
- image_count: int32 [32], P(('dp', 'bn')), may hold values from 0 to 1, as said below
- image_size: int32 [32], P(('dp', 'bn')), may hold values from 16 to 19, as said below
- cotangent: bfloat16 [32, 19, 19, 1024], P(('dp', 'bn')), may hold values from -6 to 6
- stem_weight: bfloat16 [512, 3, 3, 1024], replicated, may hold values from -0.09375 to 0.09375
- split_main: bfloat16 [1024, 512], replicated, may hold values from -0.1875 to 0.1875
- split_side: bfloat16 [1024, 512], replicated, may hold values from -0.1875 to 0.1875
- block_reduce: bfloat16 [512, 512], replicated, may hold values from -0.25 to 0.25
- block_spatial: bfloat16 [512, 3, 3, 512], replicated, may hold values from -0.09375 to 0.09375
- block_transit: bfloat16 [512, 512], replicated, may hold values from -0.25 to 0.25
- merge_weight: bfloat16 [1024, 1024], replicated, may hold values from -0.1875 to 0.1875
- affines: float32 [3072, 2], replicated, may hold values from -0.5 to 1.5
Outputs:
- activations: float32 [32, 19, 19, 1024], P(('dp', 'bn'))
- image_grad: float32 [32, 38, 38, 512], P(('dp', 'bn'))
- grad_stem: float32 [512, 3, 3, 1024], P('dp')
- grad_main: float32 [1024, 512], P('dp')
- grad_side: float32 [1024, 512], P('dp')
- grad_reduce: float32 [512, 512], P('dp')
- grad_spatial: float32 [512, 3, 3, 512], P('dp')
- grad_transit: float32 [512, 512], P('dp')
- grad_merge: float32 [1024, 1024], P('dp')
- affine_grad: float32 [3072, 2], P('dp')
The draws below stay inside these ranges and needn't reach their ends.
Inputs may be any that keep to these rules, and one draw needn't show every extreme that they name: `image_count`: in each group of 4 devices that share a dp index, some device holds 1 images; other devices may hold none. A device's images fill its first slots. `image_size`: each slot's size is 16 or 19; an image of size s fills the first 2 s input rows and columns of its slot, and what lies outside is not read for any output.
All inputs are finite; a program needn't handle non-finite values.
Results may differ from the reference program's by a relative error of at most 0.015.
Values sent between devices are 32-bit elements; how exact they have to be, the bound alone decides.
A program may use at most 256 MiB of HBM per device.

```python
import jax
import jax.numpy as jnp
from jax import lax

CIN = 512
WIDTH = 1024
HALF = 512
GRID = 19
SLOTS = 1
IMAGES = 32
N_DP = 8
N_BN = 4


def draw_image_count(key, part):
    key = jax.random.fold_in(key, 1)
    first, second = jax.random.split(key)
    counts = jax.random.randint(first, (N_DP, N_BN), 0, SLOTS + 1)
    picked = jax.random.randint(second, (N_DP, 1), 0, N_BN)
    full = jnp.arange(N_BN, dtype=jnp.int32)[None, :] == picked
    return jnp.where(full, SLOTS, counts).reshape(N_DP * N_BN).astype(jnp.int32)


def draw_image_size(key, part):
    key = jax.random.fold_in(key, 2)
    first, second = jax.random.split(key)
    picks = jax.random.randint(first, (IMAGES,), 0, 2)
    spots = jax.random.randint(second, (2,), 0, IMAGES)
    picks = picks.at[spots[0]].set(0)
    picks = picks.at[spots[1]].set(1)
    return (GRID - 3 + 3 * picks).astype(jnp.int32)


def draw_affines(key, part):
    key = jax.random.fold_in(key, 3)
    first, second = jax.random.split(key)
    gains = jax.random.uniform(first, (3 * WIDTH,), jnp.float32, 0.5, 1.5)
    shifts = jax.random.uniform(second, (3 * WIDTH,), jnp.float32, -0.5, 0.5)
    return jnp.stack([gains, shifts], axis=1)


def block_levels(stream_key, dims, cuts, smallest, top_value):
    def one(dim, parts):
        steps = jax.random.uniform(jax.random.fold_in(jax.random.fold_in(stream_key, 6), dim), (parts,), jnp.float32, smallest / len(cuts), top_value / len(cuts))
        return jnp.repeat(jnp.exp(steps), dims[dim] // parts).reshape((-1,) + (1,) * (len(dims) - dim - 1))

    level = one(*cuts[0])
    for cut in cuts[1:]:
        level = level * one(*cut)
    return level


def scatter_about(rng, dims, scale, most, shards=(), held_as=jnp.bfloat16):
    factor_of = block_levels(rng, dims, shards, -0.22, 0.18) if shards else 1.0
    values = jax.random.normal(rng, dims, jnp.float32) * scale * factor_of
    return jnp.minimum(jnp.maximum(values, -most), most).astype(held_as)


def setup_inputs(seed: int = 0) -> dict:
    streams_of = jax.random.split(jax.random.key(seed), 13)
    images = scatter_about(streams_of[0], (IMAGES, 2 * GRID, 2 * GRID, CIN), 1.0, 6.0, ((0, 32),))
    image_count = draw_image_count(jax.random.fold_in(streams_of[12], 71), 0)
    image_size = draw_image_size(jax.random.fold_in(streams_of[12], 71), 0)
    cotangent = scatter_about(streams_of[3], (IMAGES, GRID, GRID, WIDTH), 1.0, 6.0, ((0, 32),))
    stem_weight = scatter_about(streams_of[4], (CIN, 3, 3, WIDTH), (9 * CIN) ** -0.5, 0.09375)
    split_main = scatter_about(streams_of[5], (WIDTH, HALF), WIDTH ** -0.5, 0.1875)
    split_side = scatter_about(streams_of[6], (WIDTH, HALF), WIDTH ** -0.5, 0.1875)
    block_reduce = scatter_about(streams_of[7], (HALF, HALF), HALF ** -0.5, 0.25)
    block_spatial = scatter_about(streams_of[8], (HALF, 3, 3, HALF), (9 * HALF) ** -0.5, 0.09375)
    block_transit = scatter_about(streams_of[9], (HALF, HALF), HALF ** -0.5, 0.25)
    merge_weight = scatter_about(streams_of[10], (WIDTH, WIDTH), WIDTH ** -0.5, 0.1875)
    affines = draw_affines(jax.random.fold_in(streams_of[12], 71), 0)
    return {"images": images, "image_count": image_count, "image_size": image_size, "cotangent": cotangent, "stem_weight": stem_weight, "split_main": split_main, "split_side": split_side, "block_reduce": block_reduce, "block_spatial": block_spatial, "block_transit": block_transit, "merge_weight": merge_weight, "affines": affines}


@jax.custom_vjp
def low(v):
    return lax.optimization_barrier(v.astype(jnp.bfloat16)).astype(jnp.float32)

@jax.custom_vjp
def low_back(v):
    return v

def low_keep(v):
    return (low(v), None)

def low_pass(kept, grad):
    return (grad,)

def back_keep(v):
    return (v, None)

def back_low(kept, grad):
    return (low(grad),)
low.defvjp(low_keep, low_pass)
low_back.defvjp(back_keep, back_low)
EPS = 1e-05

def mish(value):
    return value * jnp.tanh(jax.nn.softplus(value))

def conv_layer(field, weight, stride):
    return lax.conv_general_dilated(field, weight, (stride, stride), ((1, 1), (1, 1)), dimension_numbers=('NHWC', 'IHWO', 'NHWC'), precision=lax.Precision.HIGHEST)

def dense(field, weight):
    return jnp.einsum('nhwc,cd->nhwd', field, weight, precision=lax.Precision.HIGHEST)

def norm_act(values, mask, count, gain, shift):
    total = lax.optimization_barrier(jnp.sum(values * mask, axis=(0, 1, 2)))
    square = lax.optimization_barrier(jnp.sum(values * values * mask, axis=(0, 1, 2)))
    mean = total / count
    spread = square / count - mean * mean
    scaled = (values - mean) * lax.rsqrt(spread + EPS)
    return mish(scaled * gain + shift) * mask

def forward(weights, field, mask, count):
    stem_w, main_w, side_w, reduce_w, spatial_w, transit_w, merge_w, affines = weights
    half = main_w.shape[1]
    width = merge_w.shape[0]
    gains = affines[:, 0]
    shifts = affines[:, 1]
    cuts = (0, width, width + half, width + 2 * half, 2 * width + 2 * half)
    stem = low_back(conv_layer(field, stem_w, 2))
    stem_act = low(norm_act(stem, mask, count, gains[cuts[0]:cuts[1]], shifts[cuts[0]:cuts[1]]))
    main_path = low_back(dense(stem_act, main_w))
    side_path = low_back(dense(stem_act, side_w))
    reduce_pre = low_back(dense(low(main_path), reduce_w))
    reduce_act = low(norm_act(reduce_pre, mask, count, gains[cuts[1]:cuts[2]], shifts[cuts[1]:cuts[2]]))
    spatial = low_back(conv_layer(reduce_act, spatial_w, 1))
    residual = main_path + norm_act(spatial, mask, count, gains[cuts[2]:cuts[3]], shifts[cuts[2]:cuts[3]])
    transit = low(low_back(dense(low(residual), transit_w)))
    joined = jnp.concatenate([transit, low(side_path)], axis=-1)
    merged = low_back(dense(joined, merge_w))
    return norm_act(merged, mask, count, gains[cuts[3]:cuts[4]], shifts[cuts[3]:cuts[4]])

def reference(images, image_count, image_size, cotangent, stem_weight, split_main, split_side, block_reduce, block_spatial, block_transit, merge_weight, affines):
    grid = cotangent.shape[1]
    group = N_BN * SLOTS
    weights = (stem_weight.astype(jnp.float32), split_main.astype(jnp.float32), split_side.astype(jnp.float32), block_reduce.astype(jnp.float32), block_spatial.astype(jnp.float32), block_transit.astype(jnp.float32), merge_weight.astype(jnp.float32), affines.astype(jnp.float32))
    places = jnp.arange(grid, dtype=jnp.int32)
    slot_ids = jnp.arange(IMAGES, dtype=jnp.int32)
    present = slot_ids % SLOTS < image_count[slot_ids // SLOTS]
    sizes = image_size[:, None, None]
    inside = (places[None, :, None] < sizes) & (places[None, None, :] < sizes) & present[:, None, None]
    mask = inside.astype(jnp.float32)[..., None]

    def per_group(array):
        return array.reshape((N_DP, group) + array.shape[1:])

    def step(carry, item):
        field, local_mask, upstream = item
        count = jnp.sum(local_mask)

        def run(params, inputs):
            return forward(params, inputs, local_mask, count)
        output, back = jax.vjp(run, weights, field.astype(jnp.float32))
        weight_grads, field_grad = back(upstream.astype(jnp.float32))
        return (jax.tree.map(jnp.add, carry, weight_grads), (output, field_grad))
    zeros = jax.tree.map(jnp.zeros_like, weights)
    totals, (outputs, field_grads) = lax.scan(step, zeros, (per_group(images), per_group(mask), per_group(cotangent)))
    return (outputs.reshape(cotangent.shape), field_grads.reshape(images.shape), totals[0], totals[1], totals[2], totals[3], totals[4], totals[5], totals[6], totals[7])
```

```python
import functools

import jax
import jax.numpy as jnp
from jax import lax
from jax.experimental import pallas as pl
from jax.experimental.pallas import tpu as pltpu
from jax.sharding import PartitionSpec as P

EPS = 1e-05
F32 = jnp.float32
BF16 = jnp.bfloat16
MESH = pl.DeviceIdType.MESH
LEAD = 32
LANES = 128


def mish_parts(value):
    t = jnp.exp(-jnp.abs(value))
    positive = value >= 0
    t2 = t * t
    top = jnp.where(positive, 1.0 + 2.0 * t, t2 + 2.0 * t)
    inv = 1.0 / (top + jnp.where(positive, 2.0 * t2, 2.0))
    gate = top * inv
    slope = jnp.where(positive, t2, t) * (1.0 + t) * (4.0 * inv * inv)
    return value * gate, gate + value * slope


def dot(left, right):
    return jnp.dot(left, right, preferred_element_type=F32)


def dot_t(left, right):
    return lax.dot_general(left, right, (((1,), (1,)), ((), ())), preferred_element_type=F32)


def lane_tile(j, size=LANES):
    if isinstance(j, int):
        return pl.ds(j * size, size)
    return pl.ds(pl.multiple_of(j * size, size), size)


def share_order(n_dp):
    bits = [b for b in range(n_dp.bit_length() - 1)]
    if len(bits) < 2:
        return bits
    return [1, 0] + bits[:1:-1]


def share_place(share, n_dp):
    place = 0
    for bit in share_order(n_dp):
        place = 2 * place + (share >> bit) % 2
    return place


def flip(index, bit):
    low = lax.rem(index // (1 << bit), 2)
    return index + (1 - 2 * low) * (1 << bit), low


def chain_kernel(
    dims,
    count_ref, size_ref, images_ref, cot_ref, ws_hbm, wm_hbm, wsd_hbm, wr_hbm, w2_hbm, wt_hbm, wmg_hbm, aff_ref,
    act_ref, eo_hbm, ex_hbm, ao_hbm, ax_hbm, g0_ref, g2_ref,
    stem_low, joined, main_low, res_low, merge_in, tside, red_in, mside, sums_ref,
    ws, wms, wr, w2, wt, wmg, wsem,
    img_row, phases, taps, z0, d0, z1, d1, z2, d2, z3, i3, cot, main_path, apad, gpad, back, mask, stat,
    msg, heard, ssem, rsem, et, esem,
):
    grid, cin, width, half, n_dp, n_bn = dims
    pitch = grid + 1
    rows = z0.shape[0]
    share = cin // n_dp
    dp, bn = lax.axis_index("dp"), lax.axis_index("bn")
    others = [(dp, lax.rem(bn + k, n_bn)) for k in range(1, n_bn)]
    pair = (flip(dp, 1)[0], bn)
    act_bit = flip(dp, 1)[1]

    loads = [
        pltpu.make_async_copy(src, dst, wsem.at[k])
        for k, (src, dst) in enumerate(
            [(ws_hbm, ws), (wm_hbm, wms.at[:, pl.ds(0, half)]), (wsd_hbm, wms.at[:, pl.ds(half, half)]),
             (wr_hbm, wr), (w2_hbm, w2), (wt_hbm, wt), (wmg_hbm, wmg)]
        )
    ]
    for load in loads:
        load.start()

    barrier = pltpu.get_barrier_semaphore()
    for target in others + [pair]:
        pl.semaphore_signal(barrier, inc=1, device_id=target, device_id_type=MESH)

    places = lax.broadcasted_iota(jnp.int32, (rows, LANES), 0)
    row = (places * 3277) >> 16 if pitch == 20 else places // pitch
    col = places - row * pitch
    size = jnp.where(count_ref[0] > 0, size_ref[0], 0)
    mask[...] = jnp.where((row < size) & (col < size), 1.0, 0.0).astype(F32)

    for p in range(4):
        phases[p, 0:LEAD, :] = jnp.zeros((LEAD, cin), F32)
        tail = LEAD + pitch * grid
        phases[p, tail:, :] = jnp.zeros((phases.shape[1] - tail, cin), F32)
    for line in range(2 * grid):
        slot = line % 2
        value = images_ref[line].astype(F32)
        for k in range(cin // LANES):
            img_row[slot, k, 0 : 2 * grid, :] = value[:, k * LANES : (k + 1) * LANES]
        start = LEAD + pitch * (line // 2)
        for odd in range(2):
            p = 2 * (line % 2) + odd
            for k in range(cin // LANES):
                phases[p, start : start + grid, k * LANES : (k + 1) * LANES] = img_row[slot, k, pl.ds(odd, grid, stride=2), :]
            phases[p, start + grid : start + grid + 1, :] = jnp.zeros((1, cin), F32)

    for k in range(9):
        a, b = k // 3, k % 3
        p = 2 * (a != 1) + (b != 1)
        off = LEAD - pitch * (a == 0) - (b == 0)
        taps[:, k * cin : (k + 1) * cin] = phases[p, off : off + rows, :].astype(BF16)
    loads[0].wait()

    def put_sums(sync, j, first, second, tiles):
        msg[sync, pl.ds(j, 1), :] = first
        msg[sync, pl.ds(tiles + j, 1), :] = second

    def column_sums(sync, z, j, tiles):
        m = mask[...]
        zm = z * m
        put_sums(sync, j, jnp.sum(zm, axis=0, keepdims=True), jnp.sum(zm * z, axis=0, keepdims=True), tiles)

    def matmul_stats(sync, left, weight, out, cols):
        def body(n, _):
            z = dot(left[...], weight[:, lane_tile(n, 256)])
            out[:, lane_tile(n, 256)] = z
            for h in range(2):
                column_sums(sync, z[:, h * LANES : (h + 1) * LANES], 2 * n + h, cols // LANES)
            return 0
        lax.fori_loop(0, cols // 256, body, 0)

    def send(sync):
        heard[sync, bn] = msg[sync]
        copies = []
        for k, target in enumerate(others):
            copy = pltpu.make_async_remote_copy(
                src_ref=msg.at[sync], dst_ref=heard.at[sync, bn], send_sem=ssem.at[sync, k], recv_sem=rsem.at[sync, k],
                device_id=target, device_id_type=MESH,
            )
            copy.start()
            copies.append(copy)
        return copies

    def receive(sync, copies):
        for copy in copies:
            copy.wait()
        total = heard[sync, 0]
        for k in range(1, n_bn):
            total = total + heard[sync, k]
        return total

    def set_stat(slot, total, count, first_tile, tiles):
        mean = total[0:tiles] / count
        spread = total[tiles : 2 * tiles] / count - mean * mean
        stat[slot, 0, 0:tiles, :] = mean
        stat[slot, 1, 0:tiles, :] = lax.rsqrt(spread + EPS)
        for j in range(tiles):
            stat[slot, 2, j : j + 1, :] = aff_ref[2 * (first_tile + j) : 2 * (first_tile + j) + 1, :]
            stat[slot, 3, j : j + 1, :] = aff_ref[2 * (first_tile + j) + 1 : 2 * (first_tile + j) + 2, :]

    blocks = rows // LANES

    def per_tile(tiles, body):
        def step(j, _):
            body(j, lane_tile(j))
            return 0
        lax.fori_loop(0, tiles, step, 0)

    def normed(slot, z, j, cs, r):
        mean = stat[slot, 0, pl.ds(j, 1), :]
        inv = stat[slot, 1, pl.ds(j, 1), :]
        scaled = (z[r, cs] - mean) * inv
        return scaled, scaled * stat[slot, 2, pl.ds(j, 1), :] + stat[slot, 3, pl.ds(j, 1), :]

    def forward(slot, z, keep, tiles, put):
        def body(j, cs):
            for b in range(blocks):
                r = pl.ds(b * LANES, LANES)
                unused, before = normed(slot, z, j, cs, r)
                act, slope = mish_parts(before)
                keep[r, cs] = slope * mask[r, :]
                put(r, cs, act * mask[r, :])
        per_tile(tiles, body)

    def backward_sums(sync, slot, z, inner_ref, j, cs, upstream_of, tiles):
        first = jnp.zeros((1, LANES), F32)
        second = jnp.zeros((1, LANES), F32)
        for b in range(blocks):
            r = pl.ds(b * LANES, LANES)
            mean = stat[slot, 0, pl.ds(j, 1), :]
            inv = stat[slot, 1, pl.ds(j, 1), :]
            inner = inner_ref[r, cs] * upstream_of(r, cs)
            inner_ref[r, cs] = inner
            first = first + jnp.sum(inner, axis=0, keepdims=True)
            second = second + jnp.sum(inner * ((z[r, cs] - mean) * inv), axis=0, keepdims=True)
        put_sums(sync, j, first, second, tiles)

    def set_back(slot, total, count, first_tile, tiles):
        for j in range(tiles):
            sums_ref[2 * (first_tile + j) : 2 * (first_tile + j) + 1, :] = total[tiles + j : tiles + j + 1]
            sums_ref[2 * (first_tile + j) + 1 : 2 * (first_tile + j) + 2, :] = total[j : j + 1]
        stat[slot, 4, 0:tiles, :] = total[0:tiles] / count
        stat[slot, 5, 0:tiles, :] = total[tiles : 2 * tiles] / count

    def backward(slot, z, inner_ref, tiles, put):
        def body(j, cs):
            for b in range(blocks):
                r = pl.ds(b * LANES, LANES)
                mean = stat[slot, 0, pl.ds(j, 1), :]
                inv = stat[slot, 1, pl.ds(j, 1), :]
                scaled = (z[r, cs] - mean) * inv
                first = stat[slot, 4, pl.ds(j, 1), :]
                second = stat[slot, 5, pl.ds(j, 1), :]
                value = (inner_ref[r, cs] - mask[r, :] * (first + scaled * second)) * (inv * stat[slot, 2, pl.ds(j, 1), :])
                put(r, cs, value.astype(BF16))
        per_tile(tiles, body)

    wide_tiles, half_tiles = width // LANES, half // LANES
    t0, t1, t2, t3 = 0, wide_tiles, wide_tiles + half_tiles, wide_tiles + 2 * half_tiles

    matmul_stats(0, taps, ws, z0, width)
    msg[0, 2 * wide_tiles : 2 * wide_tiles + 8, :] = jnp.zeros((8, LANES), F32) + jnp.sum(mask[...], axis=0, keepdims=True)
    pl.semaphore_wait(barrier, n_bn)
    copies = send(0)

    def turn_phase(p, _):
        for k in range(cin // LANES):
            block = phases[p, LEAD : LEAD + rows, k * LANES : (k + 1) * LANES].T
            for s in range(k * LANES // share, (k + 1) * LANES // share):
                at = share_place(s, n_dp) * share
                inside = s * share - k * LANES
                et[p, at : at + share, :] = block[inside : inside + share, :]
        return 0
    lax.fori_loop(0, 4, turn_phase, 0)
    part = cin // 2
    mine = pl.ds(pl.multiple_of(act_bit * part, part), part)
    theirs = pl.ds(pl.multiple_of((1 - act_bit) * part, part), part)
    keep_e = pltpu.make_async_copy(et.at[0:4, mine, :], eo_hbm, esem.at[0])
    give_e = pltpu.make_async_remote_copy(
        src_ref=et.at[0:4, theirs, :], dst_ref=ex_hbm, send_sem=esem.at[1], recv_sem=esem.at[2],
        device_id=pair, device_id_type=MESH)
    keep_e.start()
    give_e.start()

    for r in range(grid):
        cot[r * pitch : r * pitch + grid, :] = cot_ref[r].astype(F32)
        cot[r * pitch + grid : (r + 1) * pitch, :] = jnp.zeros((1, width), F32)
    cot[grid * pitch :, :] = jnp.zeros((rows - grid * pitch, width), F32)
    apad[0:LEAD, :] = jnp.zeros((LEAD, half), F32)
    apad[LEAD + rows :, :] = jnp.zeros((LEAD, half), F32)
    gpad[0:LEAD, :] = jnp.zeros((LEAD, half), F32)
    gpad[LEAD + rows :, :] = jnp.zeros((LEAD, half), F32)

    total = receive(0, copies)
    count = total[2 * wide_tiles : 2 * wide_tiles + 1, 0:1]
    set_stat(0, total, count, t0, wide_tiles)

    def put_stem(r, cs, act):
        stem_low[r, cs] = act.astype(BF16)
    forward(0, z0, d0, wide_tiles, put_stem)
    loads[1].wait()
    loads[2].wait()
    for n in range(half // 256):
        y = dot(stem_low[...], wms[:, lane_tile(n, 256)])
        main_path[:, lane_tile(n, 256)] = y
        main_low[:, lane_tile(n, 256)] = y.astype(BF16)
    loads[3].wait()
    matmul_stats(1, main_low, wr, z1, half)
    copies = send(1)
    for n in range(half // 256):
        y = dot(stem_low[...], wms[:, lane_tile(half // 256 + n, 256)])
        joined[:, lane_tile(half // 256 + n, 256)] = y.astype(BF16)
    set_stat(1, receive(1, copies), count, t1, half_tiles)

    def put_reduce(r, cs, act):
        apad[pl.ds(LEAD + r.start, r.size), cs] = act.astype(BF16).astype(F32)
    forward(1, z1, d1, half_tiles, put_reduce)
    for k in range(9):
        off = LEAD + pitch * (k // 3 - 1) + k % 3 - 1
        taps[:, k * half : (k + 1) * half] = apad[off : off + rows, :].astype(BF16)
    loads[4].wait()
    matmul_stats(2, taps, w2, z2, half)
    copies = send(2)
    for k in range(half // LANES):
        block = apad[LEAD : LEAD + rows, k * LANES : (k + 1) * LANES].T
        for s in range(k * LANES // share, (k + 1) * LANES // share):
            at = share_place(s, n_dp) * share
            inside = s * share - k * LANES
            et[4, at : at + share, :] = block[inside : inside + share, :]
    keep_a = pltpu.make_async_copy(et.at[4, mine, :], ao_hbm, esem.at[3])
    give_a = pltpu.make_async_remote_copy(
        src_ref=et.at[4, theirs, :], dst_ref=ax_hbm, send_sem=esem.at[4], recv_sem=esem.at[5],
        device_id=pair, device_id_type=MESH)
    keep_a.start()
    give_a.start()
    set_stat(2, receive(2, copies), count, t2, half_tiles)

    def put_spatial(r, cs, act):
        res_low[r, cs] = (main_path[r, cs] + act).astype(BF16)
    forward(2, z2, d2, half_tiles, put_spatial)
    loads[5].wait()
    for n in range(half // 256):
        joined[:, lane_tile(n, 256)] = dot(res_low[...], wt[:, lane_tile(n, 256)]).astype(BF16)
    loads[6].wait()
    matmul_stats(3, joined, wmg, z3, width)
    set_stat(3, receive(3, send(3)), count, t3, wide_tiles)

    def merge_tile(j, cs):
        for b in range(blocks):
            r = pl.ds(b * LANES, LANES)
            unused, before = normed(3, z3, j, cs, r)
            act, slope = mish_parts(before)
            back[r, pl.ds(0, LANES)] = act * mask[r, :]
            i3[r, cs] = slope * mask[r, :]
        for line in range(grid):
            act_ref[pl.ds(line * grid * wide_tiles + j, grid, stride=wide_tiles), :] = back[line * pitch : line * pitch + grid, 0:LANES]
        backward_sums(4, 3, z3, i3, j, cs, lambda r, c: cot[r, c], wide_tiles)
    per_tile(wide_tiles, merge_tile)
    set_back(3, receive(4, send(4)), count, t3, wide_tiles)

    def put_merge(r, cs, value):
        merge_in[r, cs] = value
    backward(3, z3, i3, wide_tiles, put_merge)
    for n in range(width // 256):
        tside[:, lane_tile(n, 256)] = dot_t(merge_in[...], wmg[lane_tile(n, 256), :]).astype(BF16)
    for n in range(half // 256):
        back[:, lane_tile(n, 256)] = dot_t(tside[:, 0:half], wt[lane_tile(n, 256), :])

    def spatial_tile(j, cs):
        backward_sums(5, 2, z2, d2, j, cs, lambda r, c: back[r, c], half_tiles)
    per_tile(half_tiles, spatial_tile)
    set_back(2, receive(5, send(5)), count, t2, half_tiles)

    def put_spatial_in(r, cs, value):
        gpad[pl.ds(LEAD + r.start, r.size), cs] = value.astype(F32)
        g2_ref[r, cs] = value.astype(F32)
    backward(2, z2, d2, half_tiles, put_spatial_in)
    for k in range(9):
        off = LEAD - pitch * (k // 3 - 1) - (k % 3 - 1)
        taps[:, k * half : (k + 1) * half] = gpad[off : off + rows, :].astype(BF16)

    def reduce_columns(n, _):
        value = jnp.zeros((rows, 256), F32)
        for k in range(9):
            value = value + dot_t(taps[:, k * half : (k + 1) * half], w2[pl.ds(pl.multiple_of(k * half + n * 256, 256), 256), :])
        main_path[:, lane_tile(n, 256)] = value
        return 0
    lax.fori_loop(0, half // 256, reduce_columns, 0)

    def reduce_tile(j, cs):
        backward_sums(6, 1, z1, d1, j, cs, lambda r, c: main_path[r, c], half_tiles)
    per_tile(half_tiles, reduce_tile)
    copies = send(6)
    mside[:, half : 2 * half] = tside[:, half : 2 * half]
    set_back(1, receive(6, copies), count, t1, half_tiles)

    def put_reduce_in(r, cs, value):
        red_in[r, cs] = value
    backward(1, z1, d1, half_tiles, put_reduce_in)
    for n in range(half // 256):
        mside[:, lane_tile(n, 256)] = (back[:, lane_tile(n, 256)] + dot_t(red_in[...], wr[lane_tile(n, 256), :])).astype(BF16)

    def stem_columns(n, _):
        z3[:, lane_tile(n, 256)] = dot_t(mside[...], wms[lane_tile(n, 256), :])
        return 0
    lax.fori_loop(0, width // 256, stem_columns, 0)

    def stem_tile(j, cs):
        backward_sums(7, 0, z0, d0, j, cs, lambda r, c: z3[r, c], wide_tiles)
    per_tile(wide_tiles, stem_tile)
    set_back(0, receive(7, send(7)), count, t0, wide_tiles)

    def put_stem_in(r, cs, value):
        g0_ref[r, cs] = value.astype(F32)
    backward(0, z0, d0, wide_tiles, put_stem_in)
    keep_e.wait()
    keep_a.wait()
    give_e.wait()
    give_a.wait()


def chain(dims, count, size, images, cot, ws, wm, wsd, wr, w2, wt, wmg, aff):
    grid, cin, width, half, n_dp, n_bn = dims
    rows = -(-grid * (grid + 1) // LANES) * LANES
    sd = jax.ShapeDtypeStruct
    part = cin // 2
    tiles = width // LANES
    out = (
        sd((grid * grid * tiles, LANES), F32),
        sd((4, part, rows), F32), sd((4, part, rows), F32), sd((half // 2, rows), F32), sd((half // 2, rows), F32),
        sd((rows, width), F32), sd((rows, half), F32),
        sd((rows, width), BF16), sd((rows, 2 * half), BF16), sd((rows, half), BF16), sd((rows, half), BF16),
        sd((rows, width), BF16), sd((rows, 2 * half), BF16), sd((rows, half), BF16), sd((rows, 2 * half), BF16),
        sd(aff.shape, F32),
    )
    vm, any_ = pl.BlockSpec(memory_space=pltpu.VMEM), pl.BlockSpec(memory_space=pl.ANY)
    sm = pl.BlockSpec(memory_space=pltpu.SMEM)
    scratch = [
        pltpu.VMEM((9 * cin, width), BF16), pltpu.VMEM((width, 2 * half), BF16), pltpu.VMEM((half, half), BF16),
        pltpu.VMEM((9 * half, half), BF16), pltpu.VMEM((half, half), BF16), pltpu.VMEM((width, width), BF16),
        pltpu.SemaphoreType.DMA((7,)),
        pltpu.VMEM((2, cin // LANES, -(-2 * grid // 8) * 8, LANES), F32),
        pltpu.VMEM((4, LEAD + rows, cin), F32),
        pltpu.VMEM((rows, 9 * cin), BF16),
        pltpu.VMEM((rows, width), F32), pltpu.VMEM((rows, width), F32),
        pltpu.VMEM((rows, half), F32), pltpu.VMEM((rows, half), F32),
        pltpu.VMEM((rows, half), F32), pltpu.VMEM((rows, half), F32),
        pltpu.VMEM((rows, width), F32), pltpu.VMEM((rows, width), F32),
        pltpu.VMEM((rows, width), F32),
        pltpu.VMEM((rows, half), F32),
        pltpu.VMEM((LEAD + rows + LEAD, half), F32), pltpu.VMEM((LEAD + rows + LEAD, half), F32),
        pltpu.VMEM((rows, half), F32),
        pltpu.VMEM((rows, LANES), F32),
        pltpu.VMEM((4, 6, 8, LANES), F32),
        pltpu.VMEM((8, 3 * tiles, LANES), F32), pltpu.VMEM((8, n_bn, 3 * tiles, LANES), F32),
        pltpu.SemaphoreType.DMA((8, n_bn - 1)), pltpu.SemaphoreType.DMA((8, n_bn - 1)),
        pltpu.VMEM((5, cin, rows), F32), pltpu.SemaphoreType.DMA((6,)),
    ]
    return pl.pallas_call(
        functools.partial(chain_kernel, dims),
        out_shape=out,
        in_specs=[sm, sm, vm, vm] + [any_] * 7 + [vm],
        out_specs=(vm,) + (any_,) * 4 + (vm,) * 11,
        scratch_shapes=scratch,
        compiler_params=pltpu.CompilerParams(collective_id=0, has_side_effects=True, vmem_limit_bytes=63 * 2**20),
        name="chain",
    )(count, size, images, cot, ws, wm, wsd, wr, w2, wt, wmg, aff)


N_SPATIAL, N_STEM, N_DENSE = 5, 9, 5


def grads_kernel(
    dims,
    eo_hbm, ex_hbm, ao_hbm, ax_hbm, g0_hbm, g2_hbm,
    stem_hbm, joined_hbm, main_hbm, res_hbm, merge_hbm, tside_hbm, red_hbm, mside_hbm, sums_ref, ws_hbm,
    igrad_ref, out_hbm, total_ref, ec_hbm, ac_hbm,
    g0r, g2r, at_land, at_cat, et_land, et_cat, units, cuts_a, last_a, cuts_b, pair_b, cross_b, own_g, sums_in,
    load_sem, give_sem, take_sem, a_send, a_recv, b_send, b_recv, out_sem, s_send, s_recv,
):
    grid, cin, width, half, n_dp, n_bn = dims
    pitch = grid + 1
    rows = at_cat.shape[1] // 4
    share = cin // n_dp
    part = cin // 2
    dp, bn = lax.axis_index("dp"), lax.axis_index("bn")
    order = share_order(n_dp)
    order_a = order[1:]
    sib, core = flip(bn, 0)
    over, cross = flip(bn, 1)
    act_dp, act_bit = flip(dp, 1)
    partners = [(dp, sib), (dp, over), (act_dp, bn), (act_dp, sib)] + [(flip(dp, b)[0], bn) for b in order_a]
    bit_of = {b: flip(dp, b) for b in order}

    barrier = pltpu.get_barrier_semaphore()
    for target in partners:
        pl.semaphore_signal(barrier, inc=1, device_id=target, device_id_type=MESH)
    pl.semaphore_wait(barrier, len(partners))

    def remote(src, dst, send, recv, target):
        return pltpu.make_async_remote_copy(
            src_ref=src, dst_ref=dst, send_sem=send, recv_sem=recv, device_id=target, device_id_type=MESH)

    half2, half0 = half // 2, width // 2

    def cols(which, size):
        return pl.ds(pl.multiple_of(which * size, size), size)

    gives = []
    fields = ((g2_hbm, g2r, half2), (g0_hbm, g0r, half0))
    for f, (src, dst, size) in enumerate(fields):
        lead = LEAD if f == 0 else 0
        for k, (target, which) in enumerate((((dp, sib), 1 - core), ((act_dp, bn), core), ((act_dp, sib), 1 - core))):
            gives.append(remote(
                src.at[:, cols(which, size)], dst.at[k + 1, pl.ds(lead, rows)],
                give_sem.at[3 * f + k], take_sem.at[3 * f + k], target))
    forwards = [
        remote(ao_hbm, ac_hbm.at[0], give_sem.at[6], take_sem.at[6], (dp, sib)),
        remote(ax_hbm, ac_hbm.at[1], give_sem.at[7], take_sem.at[7], (dp, sib)),
        remote(eo_hbm, ec_hbm.at[0], give_sem.at[8], take_sem.at[8], (dp, sib)),
        remote(ex_hbm, ec_hbm.at[1], give_sem.at[9], take_sem.at[9], (dp, sib)),
    ]
    locals_ = [
        pltpu.make_async_copy(g2_hbm.at[:, cols(core, half2)], g2r.at[0, pl.ds(LEAD, rows)], load_sem.at[0]),
        pltpu.make_async_copy(g0_hbm.at[:, cols(core, half0)], g0r.at[0, pl.ds(0, rows)], load_sem.at[1]),
        pltpu.make_async_copy(g0_hbm, own_g.at[pl.ds(0, rows)], load_sem.at[2]),
        pltpu.make_async_copy(ao_hbm, at_land.at[0], load_sem.at[3]),
        pltpu.make_async_copy(ax_hbm, at_land.at[1], load_sem.at[4]),
    ]
    for k in (0, 1, 2):
        gives[k].start()
    forwards[0].start()
    forwards[1].start()
    for k in (3, 4, 5):
        gives[k].start()
    forwards[2].start()
    forwards[3].start()
    for load in locals_:
        load.start()

    def sums_step(k):
        return remote(total_ref if k else sums_ref, sums_in.at[k], s_send.at[k], s_recv.at[k], (bit_of[order[k]][0], bn))

    def sums_next(k):
        sums_step(k).wait()
        total_ref[...] = (total_ref[...] if k else sums_ref[...]) + sums_in[k]
        if k + 1 < len(order):
            sums_step(k + 1).start()
    sums_step(0).start()

    for k in range(4):
        g2r[k, 0:LEAD, :] = jnp.zeros((LEAD, half2), F32)
        g2r[k, LEAD + rows :, :] = jnp.zeros((LEAD, half2), F32)
        g0r[k, rows:, :] = jnp.zeros((LEAD, half0), F32)
    own_g[rows:, :] = jnp.zeros((LEAD, width), F32)

    n_b = len(order)

    def b_core(u, full):
        return remote(full.at[u % 2, :, cols(1 - core, half0)], pair_b.at[u], b_send.at[0, u], b_recv.at[0, u], (dp, sib))

    def b_cross(u):
        return remote(pair_b.at[u, :, cols(1 - cross, 256)], cross_b.at[u], b_send.at[1, u], b_recv.at[1, u], (dp, over))

    def b_step(u, i):
        src = cross_b if i == 0 else cuts_b[i - 1]
        size = cuts_b[i].shape[1]
        partner, bit = bit_of[order[i]]
        at = pl.ds(pl.multiple_of((1 - bit) * size, size), size)
        return remote(src.at[u, at], cuts_b[i].at[u], b_send.at[2 + i, u], b_recv.at[2 + i, u], (partner, bn))

    def add_rows(dst, src, size):
        n = min(size, 64)

        def body(k, _):
            r = pl.ds(pl.multiple_of(k * n, n), n)
            dst(r)
            return 0
        lax.fori_loop(0, size // n, body, 0)

    def b_after_core(u, full):
        b_core(u, full).wait()

        def add(r):
            pair_b[u, r, :] = pair_b[u, r, :] + full[u % 2, r, cols(core, half0)]
        add_rows(add, None, cin)
        b_cross(u).start()

    def b_after(u, i):
        if i == 0:
            b_cross(u).wait()

            def add(r):
                cross_b[u, r, :] = cross_b[u, r, :] + pair_b[u, r, cols(cross, 256)]
            add_rows(add, None, cin)
        else:
            b_step(u, i - 1).wait()
            src = cross_b if i == 1 else cuts_b[i - 2]
            dst = cuts_b[i - 1]
            size = dst.shape[1]
            bit = bit_of[order[i - 1]][1]

            def add(r):
                at = pl.ds(pl.multiple_of(bit * size + r.start, 8), r.size)
                dst[u, r, :] = dst[u, r, :] + src[u, at, :]
            add_rows(add, None, size)
        if i < n_b:
            b_step(u, i).start()

    def place(at):
        return cols(2 * core + at, 256)

    def gather_cross(u, src):
        mine = out_hbm.at[u, :, place(cross)]
        return (
            pltpu.make_async_copy(src, mine, out_sem.at[0, u]),
            remote(src, mine, out_sem.at[1, u], out_sem.at[2, u], (dp, over)),
        )

    def gather_core(u):
        both = out_hbm.at[u, :, cols(core, half0)]
        return remote(both, both, out_sem.at[3, u], out_sem.at[4, u], (dp, sib))

    def dense_phase(full, turned, r_merge, r_tside, r_red, r_mside, land):
        ins = ((joined_hbm, land, 2), (res_hbm, land, 1), (main_hbm, land, 1), (stem_hbm, land, 2))
        rights = [pltpu.make_async_copy(s, d, load_sem.at[5 + k]) for k, (s, d) in enumerate(
            ((merge_hbm, r_merge), (tside_hbm, r_tside), (red_hbm, r_red), (mside_hbm, r_mside)))]
        for load in rights:
            load.start()

        def turn(src, first, parts):
            size = parts * half
            load = pltpu.make_async_copy(src, land.at[:, pl.ds(0, size)], load_sem.at[9])
            load.start()
            load.wait()
            for k in range(size // LANES):
                block = land[:, k * LANES : (k + 1) * LANES].astype(F32).T
                for piece in range(LANES // share):
                    row = k * LANES + piece * share
                    s, h = (row // share) // parts, (row // share) % parts
                    at = share_place(s, n_dp) * share
                    turned[first + h, at : at + share, :] = block[piece * share : (piece + 1) * share].astype(BF16)

        def fill(u, left, right_ref, lo, hi):
            for n in range((hi - lo) // 256):
                full[u % 2, :, pl.ds(lo + n * 256, 256)] = dot(turned[left], right_ref[:, pl.ds(lo_of(right_ref, lo) + n * 256, 256)])

        def lo_of(ref, lo):
            return lo if ref.shape[1] >= width else 0

        turn(joined_hbm, 0, 2)
        rights[0].wait()
        fill(0, 0, r_merge, 0, width)
        b_core(0, full).start()
        fill(1, 1, r_merge, 0, width)
        b_core(1, full).start()
        turn(res_hbm, 2, 1)
        turn(main_hbm, 3, 1)
        b_after_core(0, full)
        rights[1].wait()
        rights[2].wait()
        fill(2, 2, r_tside, 0, half)
        fill(2, 3, r_red, half, 2 * half)
        b_core(2, full).start()
        b_after_core(1, full)
        turn(stem_hbm, 4, 2)
        rights[3].wait()
        fill(3, 4, r_mside, 0, width)
        b_core(3, full).start()
        b_after_core(2, full)
        fill(4, 5, r_mside, 0, width)
        b_core(4, full).start()
        b_after_core(3, full)
        b_after_core(4, full)

    pl.run_scoped(
        dense_phase, pltpu.VMEM((2, cin, width), F32), pltpu.VMEM((6, cin, rows), BF16),
        pltpu.VMEM((rows, width), BF16), pltpu.VMEM((rows, 2 * half), BF16), pltpu.VMEM((rows, half), BF16),
        pltpu.VMEM((rows, 2 * half), BF16), pltpu.VMEM((rows, width), BF16))

    n_a = len(order_a)
    n_units = N_SPATIAL + N_STEM

    def a_step(u, i):
        src = units.at[lax.rem(u, 3)] if i == 0 else cuts_a[i - 1].at[u]
        size = cuts_a[i].shape[1]
        partner, bit = bit_of[order_a[i]]
        at = pl.ds(pl.multiple_of((1 - bit) * size, size), size)
        return remote(src.at[at], cuts_a[i].at[u], a_send.at[i, u], a_recv.at[i, u], (partner, bn))

    def a_cross(u):
        return remote(cuts_a[-1].at[u, :, cols(1 - cross, 256)], last_a.at[u], a_send.at[n_a, u], a_recv.at[n_a, u], (dp, over))

    def a_after(u, i):
        if i < n_a:
            a_step(u, i).wait()
            dst = cuts_a[i]
            size = dst.shape[1]
            bit = bit_of[order_a[i]][1]

            def add(r):
                at = pl.ds(pl.multiple_of(bit * size + r.start, 8), r.size)
                own = units[lax.rem(u, 3), at, :] if i == 0 else cuts_a[i - 1][u, at, :]
                dst[u, r, :] = dst[u, r, :] + own
            add_rows(add, None, size)
            if i + 1 < n_a:
                a_step(u, i + 1).start()
            else:
                a_cross(u).start()
        elif i == n_a:
            a_cross(u).wait()
            last_a[u] = last_a[u] + cuts_a[-1][u, :, cols(cross, 256)]
            for copy in gather_cross(u, last_a.at[u]):
                copy.start()
        elif i == n_a + 1:
            for copy in gather_cross(u, last_a.at[u]):
                copy.wait()
            gather_core(u).start()
        else:
            gather_core(u).wait()

    n_stage = n_a + 3

    def advance(t, known):
        for i in range(n_stage):
            if isinstance(t, int):
                if 0 <= t - 1 - i < n_units:
                    a_after(t - 1 - i, i)
            elif i + 1 <= known:
                a_after(t - 1 - i, i)
            else:
                @pl.when(t - 1 - i >= 0)
                def _(i=i):
                    a_after(t - 1 - i, i)

    for load in locals_:
        load.wait()
    for k in (0, 1):
        forwards[k].wait()
        load = pltpu.make_async_copy(ac_hbm.at[k], at_land.at[2 + k], load_sem.at[10])
        load.start()
        load.wait()
    for k in (0, 1, 2):
        gives[k].wait()
    for slot, land in enumerate((0, 2, 1, 3)):
        at_cat[:, slot * rows : (slot + 1) * rows] = at_land[land].astype(BF16)
    sums_next(0)
    for u in range(N_SPATIAL):
        for h in range(2):
            k = 2 * u + h
            if k < 9:
                off = LEAD - pitch * (k // 3 - 1) - (k % 3 - 1)
                right = jnp.concatenate([g2r[s, off : off + rows, :].astype(BF16) for s in range(4)], axis=0)
                value = dot(at_cat[...], right)
            else:
                value = jnp.zeros((part, half2), F32)
            for x in range(2):
                units[u % 3, :, 256 * x + LANES * h : 256 * x + LANES * (h + 1)] = value[:, LANES * x : LANES * (x + 1)]
        a_step(u, 0).start()
        advance(u, 0)
    for u in range(N_DENSE):
        b_after(u, 0)
    sums_next(1)

    def stem_phase(shifted, own_shift, image, weight, wsem):
        def load_w(k):
            return pltpu.make_async_copy(
                ws_hbm.at[pl.ds(pl.multiple_of(k * cin, cin), cin)], weight.at[lax.rem(k, 2)], wsem.at[lax.rem(k, 2)])
        load_w(0).start()
        for k in (2, 3):
            forwards[k].wait()
        for p in range(4):
            pieces = [pltpu.make_async_copy(src, et_land.at[s], load_sem.at[11 + s]) for s, src in enumerate(
                (eo_hbm.at[p], ec_hbm.at[0, p], ex_hbm.at[p], ec_hbm.at[1, p]))]
            for piece in pieces:
                piece.start()
            for s, piece in enumerate(pieces):
                piece.wait()
                et_cat[p, :, s * rows : (s + 1) * rows] = et_land[s].astype(BF16)
            image[p] = jnp.zeros(image.shape[1:], F32)
        for sh, off in enumerate((0, 1, pitch, pitch + 1)):
            own_shift[sh] = own_g[off : off + rows, :].astype(BF16)
        for k in (3, 4, 5):
            gives[k].wait()
        for sh, off in enumerate((0, 1, pitch, pitch + 1)):
            for s in range(4):
                shifted[sh, s * rows : (s + 1) * rows, :] = g0r[s, off : off + rows, :].astype(BF16)

        def slot(k, _):
            a, b = k // 3, lax.rem(k, 3)
            p = 2 * jnp.where(a == 1, 0, 1) + jnp.where(b == 1, 0, 1)
            sh = 2 * jnp.where(a == 0, 1, 0) + jnp.where(b == 0, 1, 0)
            u = N_SPATIAL + k
            for n in range(half0 // 256):
                units[lax.rem(u, 3), :, n * 256 : (n + 1) * 256] = dot(et_cat[p], shifted[sh, :, n * 256 : (n + 1) * 256])
            a_step(u, 0).start()

            @pl.when(k < 8)
            def _():
                load_w(k + 1).start()
            load_w(k).wait()
            for n in range(cin // 256):
                c = slice(n * 256, (n + 1) * 256)
                image[p, :, c] = image[p, :, c] + dot_t(own_shift[sh], weight[lax.rem(k, 2), c, :])
            advance(u, N_SPATIAL)
            return 0

        lax.fori_loop(0, 3, slot, 0)
        for u in range(N_DENSE):
            b_after(u, 1)
        lax.fori_loop(3, 6, slot, 0)
        for u in range(N_DENSE):
            b_after(u, 2)
        lax.fori_loop(6, 9, slot, 0)

        def spread(p, _):
            pr, pc = p // 2, lax.rem(p, 2)
            for r in range(grid):
                for k in range(cin // LANES):
                    start = ((2 * r + pr) * 2 * grid + pc) * (cin // LANES) + k
                    igrad_ref[pl.ds(start, grid, stride=2 * cin // LANES), :] = image[p, r * pitch : r * pitch + grid, k * LANES : (k + 1) * LANES]
            return 0
        lax.fori_loop(0, 4, spread, 0)

    pl.run_scoped(
        stem_phase, pltpu.VMEM((4, 4 * rows, half0), BF16), pltpu.VMEM((4, rows, width), BF16),
        pltpu.VMEM((4, rows, cin), F32), pltpu.VMEM((2, cin, width), BF16), pltpu.SemaphoreType.DMA((2,)))

    for i in range(3, n_b + 1):
        for u in range(N_DENSE):
            b_after(u, i)
    for k in range(2, len(order)):
        sums_next(k)
    final = cuts_b[-1]
    for u in range(N_DENSE):
        for copy in gather_cross(n_units + u, final.at[u]):
            copy.start()
    for t in range(n_units, n_units + n_stage):
        advance(t, 0)
    for u in range(N_DENSE):
        for copy in gather_cross(n_units + u, final.at[u]):
            copy.wait()
        gather_core(n_units + u).start()
    for u in range(N_DENSE):
        gather_core(n_units + u).wait()


def grads(dims, eo, ex, ao, ax, g0, g2, stem_low, joined, main_low, res_low, merge_in, tside, red_in, mside, sums, ws):
    grid, cin, width, half, n_dp, n_bn = dims
    rows = g0.shape[0]
    share = cin // n_dp
    part = cin // 2
    n_units = N_SPATIAL + N_STEM
    sd = jax.ShapeDtypeStruct
    vm, any_ = pl.BlockSpec(memory_space=pltpu.VMEM), pl.BlockSpec(memory_space=pl.ANY)
    n_bits = len(share_order(n_dp))
    half0, half2 = width // 2, half // 2
    dma = pltpu.SemaphoreType.DMA
    scratch = [
        pltpu.VMEM((4, rows + LEAD, half0), F32), pltpu.VMEM((4, LEAD + rows + LEAD, half2), F32),
        pltpu.VMEM((4, part, rows), F32), pltpu.VMEM((part, 4 * rows), BF16),
        pltpu.VMEM((4, part, rows), F32), pltpu.VMEM((4, part, 4 * rows), BF16),
        pltpu.VMEM((3, part, half0), F32),
        [pltpu.VMEM((n_units, part >> (i + 1), half0), F32) for i in range(n_bits - 1)],
        pltpu.VMEM((n_units, share, 256), F32),
        [pltpu.VMEM((N_DENSE, cin >> (i + 1), 256), F32) for i in range(n_bits)],
        pltpu.VMEM((N_DENSE, cin, half0), F32), pltpu.VMEM((N_DENSE, cin, 256), F32),
        pltpu.VMEM((rows + LEAD, width), F32),
        pltpu.VMEM((n_bits,) + sums.shape, F32),
        dma((16,)), dma((10,)), dma((10,)),
        dma((n_bits, n_units)), dma((n_bits, n_units)), dma((n_bits + 2, N_DENSE)), dma((n_bits + 2, N_DENSE)),
        dma((5, n_units + N_DENSE)), dma((n_bits,)), dma((n_bits,)),
    ]
    out = (
        sd((4 * grid * grid * (cin // LANES), LANES), F32),
        sd((n_units + N_DENSE, share, width), F32),
        sd(sums.shape, F32),
        sd((2, 4, part, rows), F32), sd((2, part, rows), F32),
    )
    return pl.pallas_call(
        functools.partial(grads_kernel, dims),
        out_shape=out,
        in_specs=[any_] * 14 + [vm, any_],
        out_specs=(vm, any_, vm, any_, any_),
        scratch_shapes=scratch,
        compiler_params=pltpu.CompilerParams(collective_id=1, has_side_effects=True, vmem_limit_bytes=63 * 2**20),
        name="grads",
    )(eo, ex, ao, ax, g0, g2, stem_low, joined, main_low, res_low, merge_in, tside, red_in, mside, sums, ws)


def local(
    images, image_count, image_size, cotangent, stem_weight, split_main, split_side,
    block_reduce, block_spatial, block_transit, merge_weight, affines,
):
    n_dp, n_bn = lax.axis_size("dp"), lax.axis_size("bn")
    grid, cin = cotangent.shape[1], images.shape[3]
    width, half = merge_weight.shape[0], split_main.shape[1]
    share = cin // n_dp
    dims = (grid, cin, width, half, n_dp, n_bn)
    ws = stem_weight.transpose(1, 2, 0, 3).reshape(9 * cin, width)
    w2 = block_spatial.transpose(1, 2, 0, 3).reshape(9 * half, half)
    aff = affines.reshape(-1, LANES, 2).transpose(0, 2, 1).reshape(-1, LANES)
    act, *kept = chain(
        dims, image_count, image_size, images[0], cotangent[0], ws, split_main, split_side,
        block_reduce, w2, block_transit, merge_weight, aff)
    igrad, out, sums, unused, unused2 = grads(dims, *kept, ws)
    activations = act.reshape(1, grid, grid, width)
    image_grad = igrad.reshape(1, 2 * grid, 2 * grid, cin)
    grad_stem = out[N_SPATIAL : N_SPATIAL + N_STEM].reshape(3, 3, share, width).transpose(2, 0, 1, 3)
    spatial = out[:N_SPATIAL].reshape(N_SPATIAL, share, 4, 2, LANES).transpose(0, 3, 1, 2, 4)
    spatial = spatial.reshape(2 * N_SPATIAL, share, half)[:9]
    grad_spatial = spatial.reshape(3, 3, share, half).transpose(2, 0, 1, 3)
    dense = out[N_SPATIAL + N_STEM :]
    grad_merge = dense[0:2].transpose(0, 1, 2).reshape(2 * share, width)
    grad_transit, grad_reduce = dense[2, :, :half], dense[2, :, half:]
    split = dense[3:5].reshape(2 * share, width)
    grad_main, grad_side = split[:, :half], split[:, half:]
    mine = affines.shape[0] // n_dp
    whole = sums.reshape(-1, 2, LANES).transpose(0, 2, 1).reshape(-1, 2)
    affine_grad = lax.dynamic_slice_in_dim(whole, lax.axis_index("dp") * mine, mine, axis=0)
    return (activations, image_grad, grad_stem, grad_main, grad_side, grad_reduce, grad_spatial, grad_transit, grad_merge, affine_grad)


def solution(mesh):
    rows = P(("dp", "bn"), None, None, None)
    return jax.shard_map(
        local,
        mesh=mesh,
        in_specs=(rows, P(("dp", "bn")), P(("dp", "bn")), rows) + (P(),) * 8,
        out_specs=(
            rows, rows, P("dp", None, None, None), P("dp", None), P("dp", None), P("dp", None),
            P("dp", None, None, None), P("dp", None), P("dp", None), P("dp", None),
        ),
        check_vma=False,
    )
```

```python
import functools

import jax
import jax.numpy as jnp
from jax import lax
from jax.experimental import pallas as pl
from jax.experimental.pallas import tpu as pltpu
from jax.sharding import PartitionSpec as P

EPS = 1e-05
F32 = jnp.float32
BF16 = jnp.bfloat16
MESH = pl.DeviceIdType.MESH
LEAD = 32
LANES = 128


def mish_parts(value):
    t = jnp.exp(-jnp.abs(value))
    positive = value >= 0
    t2 = t * t
    top = jnp.where(positive, 1.0 + 2.0 * t, t2 + 2.0 * t)
    inv = 1.0 / (top + jnp.where(positive, 2.0 * t2, 2.0))
    gate = top * inv
    slope = jnp.where(positive, t2, t) * (1.0 + t) * (4.0 * inv * inv)
    return value * gate, gate + value * slope


def dot(left, right):
    return jnp.dot(left, right, preferred_element_type=F32)


def dot_t(left, right):
    return lax.dot_general(left, right, (((1,), (1,)), ((), ())), preferred_element_type=F32)


def lane_tile(j, size=LANES):
    if isinstance(j, int):
        return pl.ds(j * size, size)
    return pl.ds(pl.multiple_of(j * size, size), size)


def share_place(share, bits):
    place = 0
    for bit in bits:
        place = 2 * place + (share >> bit) % 2
    return place


def rest_bits(n_dp):
    return list(range(n_dp.bit_length() - 2, 1, -1))


def flip(index, bit):
    low = lax.rem(index // (1 << bit), 2)
    return index + (1 - 2 * low) * (1 << bit), low


def chain_kernel(
    dims,
    count_ref, size_ref, images_ref, cot_ref, ws_hbm, wm_hbm, wsd_hbm, wr_hbm, w2_hbm, wt_hbm, wmg_hbm, aff_ref,
    act_ref, eo_hbm, ex_hbm, ao_hbm, ax_hbm, g0_ref, g2_ref,
    stem_low, joined, main_low, res_low, merge_in, tside, red_in, mside, sums_ref,
    ws, wms, wr, w2, wt, wmg, wsem,
    img_row, phases, taps, z0, d0, z1, d1, z2, d2, z3, i3, cot, main_path, apad, gpad, back, mask, stat,
    msg, heard, ssem, rsem, et, esem,
):
    grid, cin, width, half, n_dp, n_bn = dims
    pitch = grid + 1
    rows = z0.shape[0]
    share = cin // n_dp
    dp, bn = lax.axis_index("dp"), lax.axis_index("bn")
    others = [(dp, lax.rem(bn + k, n_bn)) for k in range(1, n_bn)]
    pair, pair_bit = (flip(dp, 1)[0], bn), flip(dp, 1)[1]
    next_, next_bit = (flip(dp, 0)[0], bn), flip(dp, 0)[1]
    pair_bits, next_bits = [1, 0] + rest_bits(n_dp), [0, 1] + rest_bits(n_dp)

    loads = [
        pltpu.make_async_copy(src, dst, wsem.at[k])
        for k, (src, dst) in enumerate(
            [(ws_hbm, ws), (wm_hbm, wms.at[:, pl.ds(0, half)]), (wsd_hbm, wms.at[:, pl.ds(half, half)]),
             (wr_hbm, wr), (w2_hbm, w2), (wt_hbm, wt), (wmg_hbm, wmg)]
        )
    ]
    for load in loads:
        load.start()

    barrier = pltpu.get_barrier_semaphore()
    for target in others + [pair, next_]:
        pl.semaphore_signal(barrier, inc=1, device_id=target, device_id_type=MESH)

    places = lax.broadcasted_iota(jnp.int32, (rows, LANES), 0)
    row = (places * 3277) >> 16 if pitch == 20 else places // pitch
    col = places - row * pitch
    size = jnp.where(count_ref[0] > 0, size_ref[0], 0)
    mask[...] = jnp.where((row < size) & (col < size), 1.0, 0.0).astype(F32)

    for p in range(4):
        phases[p, 0:LEAD, :] = jnp.zeros((LEAD, cin), F32)
        tail = LEAD + pitch * grid
        phases[p, tail:, :] = jnp.zeros((phases.shape[1] - tail, cin), F32)
    for line in range(2 * grid):
        slot = line % 2
        value = images_ref[line].astype(F32)
        for k in range(cin // LANES):
            img_row[slot, k, 0 : 2 * grid, :] = value[:, k * LANES : (k + 1) * LANES]
        start = LEAD + pitch * (line // 2)
        for odd in range(2):
            p = 2 * (line % 2) + odd
            for k in range(cin // LANES):
                phases[p, start : start + grid, k * LANES : (k + 1) * LANES] = img_row[slot, k, pl.ds(odd, grid, stride=2), :]
            phases[p, start + grid : start + grid + 1, :] = jnp.zeros((1, cin), F32)

    for k in range(9):
        a, b = k // 3, k % 3
        p = 2 * (a != 1) + (b != 1)
        off = LEAD - pitch * (a == 0) - (b == 0)
        taps[:, k * cin : (k + 1) * cin] = phases[p, off : off + rows, :].astype(BF16)
    loads[0].wait()

    def put_sums(sync, j, first, second, tiles):
        msg[sync, pl.ds(j, 1), :] = first
        msg[sync, pl.ds(tiles + j, 1), :] = second

    def column_sums(sync, z, j, tiles):
        m = mask[...]
        zm = z * m
        put_sums(sync, j, jnp.sum(zm, axis=0, keepdims=True), jnp.sum(zm * z, axis=0, keepdims=True), tiles)

    def matmul_stats(sync, left, weight, out, cols):
        def body(n, _):
            z = dot(left[...], weight[:, lane_tile(n, 256)])
            out[:, lane_tile(n, 256)] = z
            for h in range(2):
                column_sums(sync, z[:, h * LANES : (h + 1) * LANES], 2 * n + h, cols // LANES)
            return 0
        lax.fori_loop(0, cols // 256, body, 0)

    def send(sync):
        heard[sync, bn] = msg[sync]
        copies = []
        for k, target in enumerate(others):
            copy = pltpu.make_async_remote_copy(
                src_ref=msg.at[sync], dst_ref=heard.at[sync, bn], send_sem=ssem.at[sync, k], recv_sem=rsem.at[sync, k],
                device_id=target, device_id_type=MESH,
            )
            copy.start()
            copies.append(copy)
        return copies

    def receive(sync, copies):
        for copy in copies:
            copy.wait()
        total = heard[sync, 0]
        for k in range(1, n_bn):
            total = total + heard[sync, k]
        return total

    def set_stat(slot, total, count, first_tile, tiles):
        mean = total[0:tiles] / count
        spread = total[tiles : 2 * tiles] / count - mean * mean
        stat[slot, 0, 0:tiles, :] = mean
        stat[slot, 1, 0:tiles, :] = lax.rsqrt(spread + EPS)
        for j in range(tiles):
            stat[slot, 2, j : j + 1, :] = aff_ref[2 * (first_tile + j) : 2 * (first_tile + j) + 1, :]
            stat[slot, 3, j : j + 1, :] = aff_ref[2 * (first_tile + j) + 1 : 2 * (first_tile + j) + 2, :]

    blocks = rows // LANES

    def per_tile(tiles, body):
        def step(j, _):
            body(j, lane_tile(j))
            return 0
        lax.fori_loop(0, tiles, step, 0)

    def normed(slot, z, j, cs, r):
        mean = stat[slot, 0, pl.ds(j, 1), :]
        inv = stat[slot, 1, pl.ds(j, 1), :]
        scaled = (z[r, cs] - mean) * inv
        return scaled, scaled * stat[slot, 2, pl.ds(j, 1), :] + stat[slot, 3, pl.ds(j, 1), :]

    def forward(slot, z, keep, tiles, put):
        def body(j, cs):
            for b in range(blocks):
                r = pl.ds(b * LANES, LANES)
                unused, before = normed(slot, z, j, cs, r)
                act, slope = mish_parts(before)
                keep[r, cs] = slope * mask[r, :]
                put(r, cs, act * mask[r, :])
        per_tile(tiles, body)

    def backward_sums(sync, slot, z, inner_ref, j, cs, upstream_of, tiles):
        first = jnp.zeros((1, LANES), F32)
        second = jnp.zeros((1, LANES), F32)
        for b in range(blocks):
            r = pl.ds(b * LANES, LANES)
            mean = stat[slot, 0, pl.ds(j, 1), :]
            inv = stat[slot, 1, pl.ds(j, 1), :]
            inner = inner_ref[r, cs] * upstream_of(r, cs)
            inner_ref[r, cs] = inner
            first = first + jnp.sum(inner, axis=0, keepdims=True)
            second = second + jnp.sum(inner * ((z[r, cs] - mean) * inv), axis=0, keepdims=True)
        put_sums(sync, j, first, second, tiles)

    def set_back(slot, total, count, first_tile, tiles):
        for j in range(tiles):
            sums_ref[2 * (first_tile + j) : 2 * (first_tile + j) + 1, :] = total[tiles + j : tiles + j + 1]
            sums_ref[2 * (first_tile + j) + 1 : 2 * (first_tile + j) + 2, :] = total[j : j + 1]
        stat[slot, 4, 0:tiles, :] = total[0:tiles] / count
        stat[slot, 5, 0:tiles, :] = total[tiles : 2 * tiles] / count

    def backward(slot, z, inner_ref, tiles, put):
        def body(j, cs):
            for b in range(blocks):
                r = pl.ds(b * LANES, LANES)
                mean = stat[slot, 0, pl.ds(j, 1), :]
                inv = stat[slot, 1, pl.ds(j, 1), :]
                scaled = (z[r, cs] - mean) * inv
                first = stat[slot, 4, pl.ds(j, 1), :]
                second = stat[slot, 5, pl.ds(j, 1), :]
                value = (inner_ref[r, cs] - mask[r, :] * (first + scaled * second)) * (inv * stat[slot, 2, pl.ds(j, 1), :])
                put(r, cs, value.astype(BF16))
        per_tile(tiles, body)

    wide_tiles, half_tiles = width // LANES, half // LANES
    t0, t1, t2, t3 = 0, wide_tiles, wide_tiles + half_tiles, wide_tiles + 2 * half_tiles

    matmul_stats(0, taps, ws, z0, width)
    msg[0, 2 * wide_tiles : 2 * wide_tiles + 8, :] = jnp.zeros((8, LANES), F32) + jnp.sum(mask[...], axis=0, keepdims=True)
    pl.semaphore_wait(barrier, n_bn + 1)
    copies = send(0)

    def turn_phase(p, _):
        for k in range(cin // LANES):
            block = phases[p, LEAD : LEAD + rows, k * LANES : (k + 1) * LANES].T
            for s in range(k * LANES // share, (k + 1) * LANES // share):
                at = share_place(s, pair_bits) * share
                inside = s * share - k * LANES
                et[p, at : at + share, :] = block[inside : inside + share, :]
        return 0
    lax.fori_loop(0, 4, turn_phase, 0)
    part = cin // 2
    mine = pl.ds(pl.multiple_of(pair_bit * part, part), part)
    theirs = pl.ds(pl.multiple_of((1 - pair_bit) * part, part), part)
    keep_e = pltpu.make_async_copy(et.at[0:4, mine, :], eo_hbm, esem.at[0])
    give_e = pltpu.make_async_remote_copy(
        src_ref=et.at[0:4, theirs, :], dst_ref=ex_hbm, send_sem=esem.at[1], recv_sem=esem.at[2],
        device_id=pair, device_id_type=MESH)
    keep_e.start()
    give_e.start()

    for r in range(grid):
        cot[r * pitch : r * pitch + grid, :] = cot_ref[r].astype(F32)
        cot[r * pitch + grid : (r + 1) * pitch, :] = jnp.zeros((1, width), F32)
    cot[grid * pitch :, :] = jnp.zeros((rows - grid * pitch, width), F32)
    apad[0:LEAD, :] = jnp.zeros((LEAD, half), F32)
    apad[LEAD + rows :, :] = jnp.zeros((LEAD, half), F32)
    gpad[0:LEAD, :] = jnp.zeros((LEAD, half), F32)
    gpad[LEAD + rows :, :] = jnp.zeros((LEAD, half), F32)

    total = receive(0, copies)
    count = total[2 * wide_tiles : 2 * wide_tiles + 1, 0:1]
    set_stat(0, total, count, t0, wide_tiles)

    def put_stem(r, cs, act):
        stem_low[r, cs] = act.astype(BF16)
    forward(0, z0, d0, wide_tiles, put_stem)
    loads[1].wait()
    loads[2].wait()
    for n in range(half // 256):
        y = dot(stem_low[...], wms[:, lane_tile(n, 256)])
        main_path[:, lane_tile(n, 256)] = y
        main_low[:, lane_tile(n, 256)] = y.astype(BF16)
    loads[3].wait()
    matmul_stats(1, main_low, wr, z1, half)
    copies = send(1)
    for n in range(half // 256):
        y = dot(stem_low[...], wms[:, lane_tile(half // 256 + n, 256)])
        joined[:, lane_tile(half // 256 + n, 256)] = y.astype(BF16)
    set_stat(1, receive(1, copies), count, t1, half_tiles)

    def put_reduce(r, cs, act):
        apad[pl.ds(LEAD + r.start, r.size), cs] = act.astype(BF16).astype(F32)
    forward(1, z1, d1, half_tiles, put_reduce)
    for k in range(9):
        off = LEAD + pitch * (k // 3 - 1) + k % 3 - 1
        taps[:, k * half : (k + 1) * half] = apad[off : off + rows, :].astype(BF16)
    loads[4].wait()
    matmul_stats(2, taps, w2, z2, half)
    copies = send(2)
    for k in range(half // LANES):
        block = apad[LEAD : LEAD + rows, k * LANES : (k + 1) * LANES].T
        for s in range(k * LANES // share, (k + 1) * LANES // share):
            at = share_place(s, next_bits) * share
            inside = s * share - k * LANES
            et[4, at : at + share, :] = block[inside : inside + share, :]
    mine_a = pl.ds(pl.multiple_of(next_bit * part, part), part)
    theirs_a = pl.ds(pl.multiple_of((1 - next_bit) * part, part), part)
    keep_a = pltpu.make_async_copy(et.at[4, mine_a, :], ao_hbm, esem.at[3])
    give_a = pltpu.make_async_remote_copy(
        src_ref=et.at[4, theirs_a, :], dst_ref=ax_hbm, send_sem=esem.at[4], recv_sem=esem.at[5],
        device_id=next_, device_id_type=MESH)
    keep_a.start()
    give_a.start()
    set_stat(2, receive(2, copies), count, t2, half_tiles)

    def put_spatial(r, cs, act):
        res_low[r, cs] = (main_path[r, cs] + act).astype(BF16)
    forward(2, z2, d2, half_tiles, put_spatial)
    loads[5].wait()
    for n in range(half // 256):
        joined[:, lane_tile(n, 256)] = dot(res_low[...], wt[:, lane_tile(n, 256)]).astype(BF16)
    loads[6].wait()
    matmul_stats(3, joined, wmg, z3, width)
    set_stat(3, receive(3, send(3)), count, t3, wide_tiles)

    def merge_tile(j, cs):
        for b in range(blocks):
            r = pl.ds(b * LANES, LANES)
            unused, before = normed(3, z3, j, cs, r)
            act, slope = mish_parts(before)
            back[r, pl.ds(0, LANES)] = act * mask[r, :]
            i3[r, cs] = slope * mask[r, :]
        for line in range(grid):
            act_ref[pl.ds(line * grid * wide_tiles + j, grid, stride=wide_tiles), :] = back[line * pitch : line * pitch + grid, 0:LANES]
        backward_sums(4, 3, z3, i3, j, cs, lambda r, c: cot[r, c], wide_tiles)
    per_tile(wide_tiles, merge_tile)
    set_back(3, receive(4, send(4)), count, t3, wide_tiles)

    def put_merge(r, cs, value):
        merge_in[r, cs] = value
    backward(3, z3, i3, wide_tiles, put_merge)
    for n in range(width // 256):
        tside[:, lane_tile(n, 256)] = dot_t(merge_in[...], wmg[lane_tile(n, 256), :]).astype(BF16)
    for n in range(half // 256):
        back[:, lane_tile(n, 256)] = dot_t(tside[:, 0:half], wt[lane_tile(n, 256), :])

    def spatial_tile(j, cs):
        backward_sums(5, 2, z2, d2, j, cs, lambda r, c: back[r, c], half_tiles)
    per_tile(half_tiles, spatial_tile)
    set_back(2, receive(5, send(5)), count, t2, half_tiles)

    def put_spatial_in(r, cs, value):
        gpad[pl.ds(LEAD + r.start, r.size), cs] = value.astype(F32)
        g2_ref[r, cs] = value.astype(F32)
    backward(2, z2, d2, half_tiles, put_spatial_in)
    for k in range(9):
        off = LEAD - pitch * (k // 3 - 1) - (k % 3 - 1)
        taps[:, k * half : (k + 1) * half] = gpad[off : off + rows, :].astype(BF16)

    def reduce_columns(n, _):
        value = jnp.zeros((rows, 256), F32)
        for k in range(9):
            value = value + dot_t(taps[:, k * half : (k + 1) * half], w2[pl.ds(pl.multiple_of(k * half + n * 256, 256), 256), :])
        main_path[:, lane_tile(n, 256)] = value
        return 0
    lax.fori_loop(0, half // 256, reduce_columns, 0)

    def reduce_tile(j, cs):
        backward_sums(6, 1, z1, d1, j, cs, lambda r, c: main_path[r, c], half_tiles)
    per_tile(half_tiles, reduce_tile)
    copies = send(6)
    mside[:, half : 2 * half] = tside[:, half : 2 * half]
    set_back(1, receive(6, copies), count, t1, half_tiles)

    def put_reduce_in(r, cs, value):
        red_in[r, cs] = value
    backward(1, z1, d1, half_tiles, put_reduce_in)
    for n in range(half // 256):
        mside[:, lane_tile(n, 256)] = (back[:, lane_tile(n, 256)] + dot_t(red_in[...], wr[lane_tile(n, 256), :])).astype(BF16)

    def stem_columns(n, _):
        z3[:, lane_tile(n, 256)] = dot_t(mside[...], wms[lane_tile(n, 256), :])
        return 0
    lax.fori_loop(0, width // 256, stem_columns, 0)

    def stem_tile(j, cs):
        backward_sums(7, 0, z0, d0, j, cs, lambda r, c: z3[r, c], wide_tiles)
    per_tile(wide_tiles, stem_tile)
    set_back(0, receive(7, send(7)), count, t0, wide_tiles)

    def put_stem_in(r, cs, value):
        g0_ref[r, cs] = value.astype(F32)
    backward(0, z0, d0, wide_tiles, put_stem_in)
    keep_e.wait()
    keep_a.wait()
    give_e.wait()
    give_a.wait()


def chain(dims, count, size, images, cot, ws, wm, wsd, wr, w2, wt, wmg, aff):
    grid, cin, width, half, n_dp, n_bn = dims
    rows = -(-grid * (grid + 1) // LANES) * LANES
    sd = jax.ShapeDtypeStruct
    part = cin // 2
    tiles = width // LANES
    out = (
        sd((grid * grid * tiles, LANES), F32),
        sd((4, part, rows), F32), sd((4, part, rows), F32), sd((half // 2, rows), F32), sd((half // 2, rows), F32),
        sd((rows, width), F32), sd((rows, half), F32),
        sd((rows, width), BF16), sd((rows, 2 * half), BF16), sd((rows, half), BF16), sd((rows, half), BF16),
        sd((rows, width), BF16), sd((rows, 2 * half), BF16), sd((rows, half), BF16), sd((rows, 2 * half), BF16),
        sd(aff.shape, F32),
    )
    vm, any_ = pl.BlockSpec(memory_space=pltpu.VMEM), pl.BlockSpec(memory_space=pl.ANY)
    sm = pl.BlockSpec(memory_space=pltpu.SMEM)
    scratch = [
        pltpu.VMEM((9 * cin, width), BF16), pltpu.VMEM((width, 2 * half), BF16), pltpu.VMEM((half, half), BF16),
        pltpu.VMEM((9 * half, half), BF16), pltpu.VMEM((half, half), BF16), pltpu.VMEM((width, width), BF16),
        pltpu.SemaphoreType.DMA((7,)),
        pltpu.VMEM((2, cin // LANES, -(-2 * grid // 8) * 8, LANES), F32),
        pltpu.VMEM((4, LEAD + rows, cin), F32),
        pltpu.VMEM((rows, 9 * cin), BF16),
        pltpu.VMEM((rows, width), F32), pltpu.VMEM((rows, width), F32),
        pltpu.VMEM((rows, half), F32), pltpu.VMEM((rows, half), F32),
        pltpu.VMEM((rows, half), F32), pltpu.VMEM((rows, half), F32),
        pltpu.VMEM((rows, width), F32), pltpu.VMEM((rows, width), F32),
        pltpu.VMEM((rows, width), F32),
        pltpu.VMEM((rows, half), F32),
        pltpu.VMEM((LEAD + rows + LEAD, half), F32), pltpu.VMEM((LEAD + rows + LEAD, half), F32),
        pltpu.VMEM((rows, half), F32),
        pltpu.VMEM((rows, LANES), F32),
        pltpu.VMEM((4, 6, 8, LANES), F32),
        pltpu.VMEM((8, 3 * tiles, LANES), F32), pltpu.VMEM((8, n_bn, 3 * tiles, LANES), F32),
        pltpu.SemaphoreType.DMA((8, n_bn - 1)), pltpu.SemaphoreType.DMA((8, n_bn - 1)),
        pltpu.VMEM((5, cin, rows), F32), pltpu.SemaphoreType.DMA((6,)),
    ]
    return pl.pallas_call(
        functools.partial(chain_kernel, dims),
        out_shape=out,
        in_specs=[sm, sm, vm, vm] + [any_] * 7 + [vm],
        out_specs=(vm,) + (any_,) * 4 + (vm,) * 11,
        scratch_shapes=scratch,
        compiler_params=pltpu.CompilerParams(collective_id=0, has_side_effects=True, vmem_limit_bytes=63 * 2**20),
        name="chain",
    )(count, size, images, cot, ws, wm, wsd, wr, w2, wt, wmg, aff)


TAPS = 9
UNITS = ["S%d" % k for k in range(5)] + ["T%d%d" % (k, h) for h in range(2) for k in range(TAPS)] + ["B%d" % k for k in range(6)]
ORDERS = {}
for order, names in (
    ("y12x", ["B0"]),
    ("y1x2", ["B1", "B3"]),
    ("xy21", ["B2", "B5"]),
    ("yx21", ["B4"]),
    ("x12", ["S0", "S1", "S2", "S3", "S4"]),
    ("xy2", ["T00", "T01", "T10", "T11", "T21", "T51"]),
    ("yx2", ["T20", "T31", "T40", "T41", "T50", "T60", "T61", "T70", "T71", "T80", "T81"]),
    ("y2x", ["T30"]),
):
    for name in names:
        ORDERS[name] = order
TOKENS = [
    "B2", "B5", "B2", "B4", "B5", "B0", "B1", "B3", "B2", "B4", "B0", "PS", "S1", "B1", "B2", "B3", "S2", "B5",
    "PT", "P0", "T10", "S1", "S3", "T00", "B4", "I", "S2", "I", "I", "T10", "I", "B2", "P1", "T01", "S1", "T21",
    "S3", "I", "S2", "B2", "B0", "T00", "S1", "T51", "I", "I", "S3", "S0", "S2", "B4", "I", "I", "T01", "B1",
    "T11", "B0", "B2", "S3", "T21", "S1", "B2", "T20", "S1", "S4", "T51", "B3", "B4", "T30", "T71", "B5", "S0",
    "T10", "S2", "B1", "T60", "S2", "T00", "T01", "T11", "B0", "T21", "S3", "T50", "S3", "B3", "T20", "S4", "B4",
    "T70", "T51", "B1", "B5", "T80", "B0", "T30", "B3", "S0", "T10", "T71", "T20", "T81", "T00", "B4", "T01",
    "T60", "B0", "B4", "T61", "T10", "T21", "B0", "T71", "T11", "T00", "T10", "T51", "T01", "T50", "S4", "T00",
    "T41", "T01", "T21", "B1", "T51", "T60", "T70", "T21", "B5", "T50", "T51", "T40", "T30", "B1", "T80", "T31",
    "B3", "B1", "T70", "B5", "T81", "T30", "S0", "B5", "T80", "T20", "B3", "T61", "T71", "T81", "B3", "T30",
    "T11", "T41", "S0", "T30", "S4", "T20", "T60", "S0", "T61", "T20", "T40", "T71", "T50", "T11", "T70", "T71",
    "T41", "T11", "T31", "S4", "T80", "T60", "T81", "S4", "T40", "T60", "T50", "T61", "T70", "T50", "T41", "T31",
    "T70", "T80", "T40", "T81", "T61", "T80", "T31", "T81", "T41", "T40", "T61", "T41", "T31", "T40", "T31"
]


class Unit:
    def __init__(self, name, dims):
        grid, cin, width, half, n_dp, n_bn = dims
        self.name, self.kind = name, name[0]
        order = ORDERS.get(name, {"S": "1x2", "T": "yx2", "B": "xy12"}[self.kind])
        self.steps = []
        for letter in order:
            self.steps += {"x": ["x"], "y": [0], "1": [1], "2": rest_bits(n_dp)}[letter]
        self.bits = [step for step in self.steps if step != "x"]
        narrow = name in ("S4", "B2", "B3") or self.kind == "T"
        rows, cols = (cin if self.kind == "B" else cin // 2), (width // 4 if narrow else width // 2)
        self.start = (rows, cols)
        self.pool = self.kind + ("n" if narrow and self.kind == "B" else "")
        self.shapes = [(rows, cols)] if self.kind == "B" else []
        for step in self.steps:
            rows, cols = (rows, cols // 2) if step == "x" else (rows // 2, cols)
            self.shapes.append((rows, cols))
        self.final = (rows, cols)
        self.n_moves = len(self.shapes)
        self.n_stages = self.n_moves + 3


def plan(dims):
    units = {name: Unit(name, dims) for name in UNITS}
    shapes, message = {}, 0
    for unit in units.values():
        unit.at = []
        for shape in unit.shapes:
            unit.at.append((shape, shapes.get(shape, 0)))
            shapes[shape] = shapes.get(shape, 0) + 1
        unit.message = message
        message += unit.n_moves + 3
    tokens = list(TOKENS)
    stage = {name: tokens.count(name) for name in UNITS}
    if not tokens:
        tokens = ["B%d" % k for k in range(6) for unused in range(2)] + ["PS"] + ["S%d" % k for k in range(5)] + ["PT", "P0", "P1"]
        tokens += [t for k in range(TAPS) for t in ("T%d0" % k, "T%d1" % k, "I")]
        stage = {name: tokens.count(name) for name in UNITS}
    while any(stage[name] < units[name].n_stages for name in UNITS):
        for name in UNITS:
            if stage[name] < units[name].n_stages:
                tokens.append(name)
                stage[name] += 1
    kinds = ("S", "T", "B", "Bn")
    seen, count, free = {}, {kind: 0 for kind in kinds}, {kind: [] for kind in kinds}
    for token in tokens:
        if token in units:
            unit = units[token]
            k = seen.get(token, 0)
            seen[token] = k + 1
            if k == 0:
                if not free[unit.pool]:
                    free[unit.pool].append(count[unit.pool])
                    count[unit.pool] += 1
                unit.slot = free[unit.pool].pop(0)
            elif k == 1:
                free[unit.pool].append(unit.slot)
    return units, shapes, message, tokens, count


def grads_kernel(
    dims,
    eo_hbm, ex_hbm, ao_hbm, ax_hbm, g0_hbm, g2_hbm,
    stem_hbm, joined_hbm, main_hbm, res_hbm, merge_hbm, tside_hbm, red_hbm, mside_hbm, sums_ref, ws_hbm,
    igrad_hbm, out_stem, out_spatial, out_merge, out_transit, out_reduce, out_split, total_ref,
    g0r, g2r, landed, own_g, sums_in, at_land, at_cat, et_land, spatial,
    load_sem, give_sem, take_sem, m_send, m_recv, keep_sem, s_send, s_recv,
):
    grid, cin, width, half, n_dp, n_bn = dims
    units, shapes, n_messages, tokens, pool = plan(dims)
    shape_list = list(shapes)
    pitch = grid + 1
    rows = own_g.shape[0] - LEAD
    share = cin // n_dp
    part = cin // 2
    quarter = width // 4
    dp, bn = lax.axis_index("dp"), lax.axis_index("bn")
    n_bits = n_dp.bit_length() - 1
    sib, core = flip(bn, 0)
    over, cross = flip(bn, 1)
    bit_of = [flip(dp, b) for b in range(n_bits)]
    sibling, across = (dp, sib), (dp, over)
    along = [(bit_of[b][0], bn) for b in range(n_bits)]
    next_sib, pair_sib = (bit_of[0][0], sib), (bit_of[1][0], sib)
    partners = [sibling, across, next_sib, pair_sib] + along

    barrier = pltpu.get_barrier_semaphore()
    for target in partners:
        pl.semaphore_signal(barrier, inc=1, device_id=target, device_id_type=MESH)
    pl.semaphore_wait(barrier, len(partners))

    def remote(src, dst, send, recv, target):
        return pltpu.make_async_remote_copy(
            src_ref=src, dst_ref=dst, send_sem=send, recv_sem=recv, device_id=target, device_id_type=MESH)

    def part_of(which, size):
        return pl.ds(pl.multiple_of(which * size, size), size)

    half2 = half // 2
    gives, locals_ = [], []
    for k, (target, which) in enumerate(((sibling, 1 - core), (along[0], core), (next_sib, 1 - core))):
        gives.append(remote(
            g2_hbm.at[:, part_of(which, half2)], g2r.at[k + 1, pl.ds(LEAD, rows)], give_sem.at[k], take_sem.at[k], target))
    for h in range(2):
        for k, (target, which) in enumerate(((sibling, 1 - core), (along[1], core), (pair_sib, 1 - core))):
            n = 3 + 3 * h + k
            gives.append(remote(
                g0_hbm.at[:, part_of(2 * which + h, quarter)], g0r.at[h, k + 1, pl.ds(0, rows)],
                give_sem.at[n], take_sem.at[n], target))
    forwards = [
        remote(land.at[n], land.at[n + 2], give_sem.at[9 + k], take_sem.at[9 + k], sibling)
        for k, (land, n) in enumerate(((at_land, 0), (at_land, 1), (et_land, 0), (et_land, 1)))
    ]
    own_parts = [
        pltpu.make_async_copy(src, land, load_sem.at[11 + k])
        for k, (src, land) in enumerate(
            ((ao_hbm, at_land.at[0]), (ax_hbm, at_land.at[1]), (eo_hbm, et_land.at[0]), (ex_hbm, et_land.at[1])))
    ]
    for load in own_parts:
        load.start()
    for n in range(3):
        gives[n].start()
    for n in (3, 4, 5):
        gives[n].start()
    for n in (6, 7, 8):
        gives[n].start()
    locals_ = [
        pltpu.make_async_copy(g2_hbm.at[:, part_of(core, half2)], g2r.at[0, pl.ds(LEAD, rows)], load_sem.at[0]),
        pltpu.make_async_copy(g0_hbm.at[:, part_of(2 * core, quarter)], g0r.at[0, 0, pl.ds(0, rows)], load_sem.at[1]),
        pltpu.make_async_copy(g0_hbm.at[:, part_of(2 * core + 1, quarter)], g0r.at[1, 0, pl.ds(0, rows)], load_sem.at[2]),
        pltpu.make_async_copy(g0_hbm, own_g.at[pl.ds(0, rows)], load_sem.at[3]),
    ]
    for load in locals_:
        load.start()
    for load, forward in zip(own_parts, forwards):
        load.wait()
        forward.start()

    def sums_step(k):
        return remote(total_ref if k else sums_ref, sums_in.at[k], s_send.at[k], s_recv.at[k], along[k])

    sums_done = []

    def sums_next():
        k = len(sums_done)
        if k < n_bits:
            sums_done.append(k)
            sums_step(k).wait()
            total_ref[...] = (total_ref[...] if k else sums_ref[...]) + sums_in[k]
            if k + 1 < n_bits:
                sums_step(k + 1).start()
    sums_step(0).start()

    for k in range(4):
        g2r[k, 0:LEAD, :] = jnp.zeros((LEAD, half2), F32)
        g2r[k, LEAD + rows :, :] = jnp.zeros((LEAD, half2), F32)
        for h in range(2):
            g0r[h, k, rows:, :] = jnp.zeros((LEAD, quarter), F32)
    own_g[rows:, :] = jnp.zeros((LEAD, width), F32)

    local = {}

    def landing(unit, k):
        shape, n = unit.at[k]
        return landed[shape_list.index(shape)].at[n]

    def source(unit, k):
        return local[unit.kind](unit) if k == 0 else landing(unit, k - 1)

    def move_of(unit, k):
        size_r, size_c = unit.shapes[k]
        step = "c" if unit.kind == "B" and k == 0 else unit.steps[k - (unit.kind == "B")]
        if step == "c":
            return sibling, (pl.ds(0, size_r), part_of(1 - core, size_c)), (None, part_of(core, size_c))
        if step == "x":
            return across, (pl.ds(0, size_r), part_of(1 - cross, size_c)), (None, part_of(cross, size_c))
        bit = bit_of[step][1]
        return along[step], (part_of(1 - bit, size_r), pl.ds(0, size_c)), (bit, pl.ds(0, size_c))

    def move(unit, k):
        target, gone, unused = move_of(unit, k)
        m = unit.message + k
        return remote(source(unit, k).at[gone[0], gone[1]], landing(unit, k), m_send.at[m], m_recv.at[m], target)

    def add_own(unit, k):
        unused, unused2, (bit, columns) = move_of(unit, k)
        size = unit.shapes[k][0]
        src, dst = source(unit, k), landing(unit, k)
        n = min(size, 64)

        def body(i, _):
            r = pl.ds(pl.multiple_of(i * n, n), n)
            own = r if bit is None else pl.ds(pl.multiple_of(bit * size + i * n, 8), n)
            dst[r, :] = dst[r, :] + src[own, columns]
            return 0
        lax.fori_loop(0, size // n, body, 0)

    def pieces(unit):
        name = unit.name
        cols = unit.final[1]
        k = int(name[1])
        at = 2 * core + cross
        if unit.kind == "T":
            h = int(name[2])
            base = pl.multiple_of(core * (width // 2) + h * quarter, quarter)
            mine = out_stem.at[k, :, pl.ds(pl.multiple_of(base + cross * cols, cols), cols)]
            return [(mine, 0)], out_stem.at[k, :, pl.ds(base, quarter)]
        if unit.kind == "S":
            mine = [(out_spatial.at[t, :, part_of(at, half // 4)], (t - 2 * k) * (half // 4)) for t in range(2 * k, min(2 * k + 2, TAPS))]
            return mine, out_spatial.at[pl.ds(2 * k, len(mine)), :, part_of(core, half2)]
        if k < 2:
            r = pl.ds(k * share, share)
            return [(out_merge.at[r, part_of(at, quarter)], 0)], out_merge.at[r, part_of(core, width // 2)]
        if k < 4:
            out = out_transit if k == 2 else out_reduce
            return [(out.at[:, part_of(at, half // 4)], 0)], out.at[:, part_of(core, half2)]
        r = pl.ds((k - 4) * share, share)
        return [(out_split.at[core, r, part_of(cross, half2)], 0)], out_split.at[core, r, :]

    def gather_cross(unit):
        m = unit.message + unit.n_moves
        copies = []
        mine, unused = pieces(unit)
        final = landing(unit, unit.n_moves - 1)
        for n, (place, col) in enumerate(mine):
            src = final.at[:, pl.ds(col, place.shape[-1])]
            copies.append(pltpu.make_async_copy(src, place, keep_sem.at[m + n]))
            copies.append(remote(src, place, m_send.at[m + n], m_recv.at[m + n], across))
        return copies

    def gather_core(unit):
        m = unit.message + unit.n_moves + 2
        both = pieces(unit)[1]
        return remote(both, both, m_send.at[m], m_recv.at[m], sibling)

    stage = {name: 0 for name in units}

    def advance(name, compute):
        unit = units[name]
        k = stage[name]
        stage[name] = k + 1
        if k == 0:
            compute(unit)
            move(unit, 0).start()
        elif k <= unit.n_moves:
            move(unit, k - 1).wait()
            add_own(unit, k - 1)
            if k < unit.n_moves:
                move(unit, k).start()
            else:
                for copy in gather_cross(unit):
                    copy.start()
        elif k == unit.n_moves + 1:
            for copy in gather_cross(unit):
                copy.wait()
            gather_core(unit).start()
        else:
            gather_core(unit).wait()

    local["S"] = lambda unit: spatial.at[unit.slot]

    def prepare_spatial():
        for n in range(2):
            forwards[n].wait()
        for k in range(3):
            gives[k].wait()
        locals_[0].wait()
        for slot, n in enumerate((0, 2, 1, 3)):
            at_cat[:, slot * rows : (slot + 1) * rows] = at_land[n].astype(BF16)
        sums_next()

    def compute_spatial(unit):
        k = int(unit.name[1])
        dst = local["S"](unit)
        c = unit.start[1] // 2
        for h in range(2):
            t = 2 * k + h
            if t < TAPS:
                off = LEAD - pitch * (t // 3 - 1) - (t % 3 - 1)
                right = jnp.concatenate([g2r[s, off : off + rows, :].astype(BF16) for s in range(4)], axis=0)
                value = dot(at_cat[...], right)
                for x in range(2):
                    dst[:, c * x + LANES * h : c * x + LANES * (h + 1)] = value[:, LANES * x : LANES * (x + 1)]

    cut = tokens.index("PT")

    def dense_phase(full, narrow, turned, r_merge, r_tside, r_red, r_mside, land):
        rights = [pltpu.make_async_copy(s, d, load_sem.at[5 + k]) for k, (s, d) in enumerate(
            ((merge_hbm, r_merge), (tside_hbm, r_tside), (red_hbm, r_red), (mside_hbm, r_mside)))]
        lefts = [(joined_hbm, 0, 2), (res_hbm, 2, 1), (main_hbm, 3, 1), (stem_hbm, 4, 2)]
        loads = [
            pltpu.make_async_copy(src, land.at[n % 2, :, pl.ds(0, parts * half)], load_sem.at[9 + n % 2])
            for n, (src, first, parts) in enumerate(lefts)]
        loads[0].start()
        for load in rights:
            load.start()
        loads[1].start()
        done = set()
        local["B"] = lambda unit: (full if unit.pool == "B" else narrow).at[unit.slot]

        def turn(n):
            src, first, parts = lefts[n]
            loads[n].wait()
            for k in range(parts * half // LANES):
                block = land[n % 2, :, k * LANES : (k + 1) * LANES].astype(F32).T
                for piece in range(LANES // share):
                    row = k * LANES + piece * share
                    s, h = (row // share) // parts, (row // share) % parts
                    at = share_place(s, units["B%d" % (first + h)].bits) * share
                    turned[first + h, at : at + share, :] = block[piece * share : (piece + 1) * share].astype(BF16)
            if n + 2 < len(loads):
                loads[n + 2].start()

        def compute(unit):
            if unit.kind == "S":
                return compute_spatial(unit)
            k = int(unit.name[1])
            for m in range({0: 0, 1: 0, 2: 1, 3: 2, 4: 3, 5: 3}[k] + 1):
                if m not in done:
                    turn(m)
                    done.add(m)
            right, r = [(r_merge, 0), (r_merge, 0), (r_tside, 1), (r_red, 2), (r_mside, 3), (r_mside, 3)][k]
            if ("right", r) not in done:
                rights[r].wait()
                done.add(("right", r))
            dst = local["B"](unit)
            for n in range(2 * unit.start[1] // 256):
                c = pl.ds(n * 256, 256)
                dst[:, c] = dot(turned[k], right[:, c])

        for token in tokens[:cut]:
            if token == "PS":
                prepare_spatial()
            elif token in units:
                advance(token, compute)
        for name in units:
            while units[name].kind == "B" and stage[name] < 2:
                advance(name, compute)

    pl.run_scoped(
        dense_phase,
        pltpu.VMEM((pool["B"], cin, width), F32), pltpu.VMEM((pool["Bn"], cin, half), F32), pltpu.VMEM((6, cin, rows), BF16),
        pltpu.VMEM((rows, width), BF16), pltpu.VMEM((rows, 2 * half), BF16), pltpu.VMEM((rows, half), BF16),
        pltpu.VMEM((rows, 2 * half), BF16), pltpu.VMEM((2, rows, width), BF16))

    def stem_phase(shifted, own_shift, image, weight, wsem, et_cat, blocks, igrad):
        local["T"] = lambda unit: blocks.at[unit.slot]
        offsets = (0, 1, pitch, pitch + 1)
        image_taps = [4, 3, 5, 1, 7, 0, 2, 6, 8]
        done = []

        def tap(k):
            a, b = k // 3, k % 3
            return 2 * (a != 1) + (b != 1), 2 * (a == 0) + (b == 0)

        def compute(unit):
            if unit.kind == "S":
                return compute_spatial(unit)
            p, sh = tap(int(unit.name[1]))
            local["T"](unit)[...] = dot(et_cat[p], shifted[int(unit.name[2]), sh])

        def image_step():
            k = image_taps[len(done)]
            p, sh = tap(k)
            if len(done) + 1 < TAPS:
                load_w_next = image_taps[len(done) + 1]
                pltpu.make_async_copy(
                    ws_hbm.at[pl.ds(load_w_next * cin, cin)], weight.at[(len(done) + 1) % 2], wsem.at[(len(done) + 1) % 2]).start()
            pltpu.make_async_copy(ws_hbm.at[pl.ds(k * cin, cin)], weight.at[len(done) % 2], wsem.at[len(done) % 2]).wait()
            first = k in (4, 3, 1, 0)
            for n in range(cin // 256):
                c = slice(n * 256, (n + 1) * 256)
                value = dot_t(own_shift[sh], weight[len(done) % 2, c, :])
                image[:, c] = value if first else image[:, c] + value
            done.append(k)
            if k in (4, 5, 7, 8):
                pr, pc = p // 2, p % 2

                def spread(r, _):
                    for n in range(cin // LANES):
                        start = ((2 * r + pr) * 2 * grid + pc) * (cin // LANES) + n
                        igrad[pl.ds(start, grid, stride=2 * cin // LANES), :] = line_of(r, n)
                    return 0

                def line_of(r, n):
                    return image[r * pitch : r * pitch + grid, n * LANES : (n + 1) * LANES]
                for r in range(grid):
                    spread(r, 0)
            if len(done) == TAPS:
                pltpu.make_async_copy(igrad, igrad_hbm, load_sem.at[15]).start()

        def run(token):
            if token == "PT":
                pltpu.make_async_copy(ws_hbm.at[pl.ds(image_taps[0] * cin, cin)], weight.at[0], wsem.at[0]).start()
                for n in (2, 3):
                    forwards[n].wait()

                for p in range(4):
                    for slot, n in enumerate((0, 2, 1, 3)):
                        et_cat[p, :, slot * rows : (slot + 1) * rows] = et_land[n, p].astype(BF16)
                locals_[3].wait()
                for sh, off in enumerate(offsets):
                    own_shift[sh] = own_g[off : off + rows, :].astype(BF16)
                sums_next()
            elif token in ("P0", "P1"):
                h = int(token[1])
                for k in range(3):
                    gives[3 + 3 * h + k].wait()
                locals_[1 + h].wait()
                for sh, off in enumerate(offsets):
                    for s in range(4):
                        shifted[h, sh, s * rows : (s + 1) * rows, :] = g0r[h, s, off : off + rows, :].astype(BF16)
                sums_next()
            elif token == "PS":
                prepare_spatial()
            elif token == "I":
                if len(done) < TAPS:
                    image_step()
            elif token in units:
                advance(token, compute)

        for token in tokens[cut:]:
            run(token)
        while len(done) < TAPS:
            image_step()
        for k in range(n_bits):
            sums_next()
        pltpu.make_async_copy(igrad, igrad_hbm, load_sem.at[15]).wait()

    pl.run_scoped(
        stem_phase,
        pltpu.VMEM((2, 4, 4 * rows, quarter), BF16), pltpu.VMEM((4, rows, width), BF16), pltpu.VMEM((rows, cin), F32),
        pltpu.VMEM((2, cin, width), BF16), pltpu.SemaphoreType.DMA((2,)),
        pltpu.VMEM((4, part, 4 * rows), BF16),
        pltpu.VMEM((pool["T"], part, quarter), F32), pltpu.VMEM((4 * grid * grid * (cin // LANES), LANES), F32))


def grads(dims, eo, ex, ao, ax, g0, g2, stem_low, joined, main_low, res_low, merge_in, tside, red_in, mside, sums, ws):
    grid, cin, width, half, n_dp, n_bn = dims
    units, shapes, n_messages, tokens, pool = plan(dims)
    rows = g0.shape[0]
    share = cin // n_dp
    part = cin // 2
    sd = jax.ShapeDtypeStruct
    vm, any_ = pl.BlockSpec(memory_space=pltpu.VMEM), pl.BlockSpec(memory_space=pl.ANY)
    n_bits = n_dp.bit_length() - 1
    dma = pltpu.SemaphoreType.DMA
    scratch = [
        pltpu.VMEM((2, 4, rows + LEAD, width // 4), F32), pltpu.VMEM((4, LEAD + rows + LEAD, half // 2), F32),
        [pltpu.VMEM((n,) + shape, F32) for shape, n in shapes.items()],
        pltpu.VMEM((rows + LEAD, width), F32),
        pltpu.VMEM((n_bits,) + sums.shape, F32),
        pltpu.VMEM((4, part, rows), F32), pltpu.VMEM((part, 4 * rows), BF16), pltpu.VMEM((4, 4, part, rows), F32),
        pltpu.VMEM((pool["S"], part, width // 2), F32),
        dma((16,)), dma((13,)), dma((13,)), dma((n_messages,)), dma((n_messages,)), dma((n_messages,)),
        dma((n_bits,)), dma((n_bits,)),
    ]
    out = (
        sd((4 * grid * grid * (cin // LANES), LANES), F32),
        sd((TAPS, share, width), F32), sd((TAPS, share, half), F32), sd((2 * share, width), F32),
        sd((share, half), F32), sd((share, half), F32), sd((2, 2 * share, half), F32),
        sd(sums.shape, F32),
    )
    return pl.pallas_call(
        functools.partial(grads_kernel, dims),
        out_shape=out,
        in_specs=[any_] * 14 + [vm, any_],
        out_specs=(any_,) + (vm,) * 7,
        scratch_shapes=scratch,
        compiler_params=pltpu.CompilerParams(collective_id=1, has_side_effects=True, vmem_limit_bytes=63 * 2**20),
        name="grads",
    )(eo, ex, ao, ax, g0, g2, stem_low, joined, main_low, res_low, merge_in, tside, red_in, mside, sums, ws)


def finish_kernel(parts, n, *refs):
    ins, outs = refs[:n], refs[n : n + len(parts)]
    held, sems = refs[n + len(parts) : n + 2 * len(parts)], refs[-2:]
    steps = []
    for k, (which, row) in enumerate(parts):
        src, dst, by = ins[which] if row is None else ins[which].at[row], outs[k], held[k]
        size = dst.shape[0]
        cuts = 4 if size % 32 == 0 or size >= 2048 else 1
        edge = [size // cuts // 8 * 8 * c for c in range(cuts)] + [size]
        for c in range(cuts):
            r = pl.ds(edge[c], edge[c + 1] - edge[c])
            at = len(steps)
            steps.append((
                pltpu.make_async_copy(src.at[r], by.at[r], sems[0].at[at]),
                pltpu.make_async_copy(by.at[r], dst.at[r], sems[1].at[at])))
    for step in steps:
        step[0].start()
    for step in steps:
        step[0].wait()
        step[1].start()
    for step in steps:
        step[1].wait()


def finish(arrays, parts):
    any_ = pl.BlockSpec(memory_space=pl.ANY)
    shapes = [arrays[which].shape if row is None else arrays[which].shape[1:] for which, row in parts]
    return pl.pallas_call(
        functools.partial(finish_kernel, parts, len(arrays)),
        out_shape=tuple(jax.ShapeDtypeStruct(shape, F32) for shape in shapes),
        in_specs=[any_] * len(arrays),
        out_specs=(any_,) * len(parts),
        scratch_shapes=[pltpu.VMEM(shape, F32) for shape in shapes] + [pltpu.SemaphoreType.DMA((4 * len(parts),))] * 2,
        compiler_params=pltpu.CompilerParams(vmem_limit_bytes=63 * 2**20),
        name="finish",
    )(*arrays)


def local(
    images, image_count, image_size, cotangent, stem_weight, split_main, split_side,
    block_reduce, block_spatial, block_transit, merge_weight, affines,
):
    n_dp, n_bn = lax.axis_size("dp"), lax.axis_size("bn")
    grid, cin = cotangent.shape[1], images.shape[3]
    width, half = merge_weight.shape[0], split_main.shape[1]
    share = cin // n_dp
    dims = (grid, cin, width, half, n_dp, n_bn)
    ws = stem_weight.transpose(1, 2, 0, 3).reshape(9 * cin, width)
    w2 = block_spatial.transpose(1, 2, 0, 3).reshape(9 * half, half)
    aff = affines.reshape(-1, LANES, 2).transpose(0, 2, 1).reshape(-1, LANES)
    act, *kept = chain(
        dims, image_count, image_size, images[0], cotangent[0], ws, split_main, split_side,
        block_reduce, w2, block_transit, merge_weight, aff)
    igrad, stem, spatial, merge, transit, reduce, split, sums = grads(dims, *kept, ws)
    act, igrad, stem, spatial, grad_merge, grad_transit, grad_reduce, grad_main, grad_side = finish(
        [act, igrad, stem, spatial, merge, transit, reduce, split], [(k, None) for k in range(7)] + [(7, 0), (7, 1)])
    activations = act.reshape(1, grid, grid, width)
    image_grad = igrad.reshape(1, 2 * grid, 2 * grid, cin)
    grad_stem = stem.reshape(3, 3, share, width).transpose(2, 0, 1, 3)
    grad_spatial = spatial.reshape(3, 3, share, half).transpose(2, 0, 1, 3)
    mine = affines.shape[0] // n_dp
    whole = sums.reshape(-1, 2, LANES).transpose(0, 2, 1).reshape(-1, 2)
    affine_grad = lax.dynamic_slice_in_dim(whole, lax.axis_index("dp") * mine, mine, axis=0)
    return (activations, image_grad, grad_stem, grad_main, grad_side, grad_reduce, grad_spatial, grad_transit, grad_merge, affine_grad)


def solution(mesh):
    rows = P(("dp", "bn"), None, None, None)
    return jax.shard_map(
        local,
        mesh=mesh,
        in_specs=(rows, P(("dp", "bn")), P(("dp", "bn")), rows) + (P(),) * 8,
        out_specs=(
            rows, rows, P("dp", None, None, None), P("dp", None), P("dp", None), P("dp", None),
            P("dp", None, None, None), P("dp", None), P("dp", None), P("dp", None),
        ),
        check_vma=False,
    )
```

```python
import functools

import jax
import jax.numpy as jnp
from jax import lax
from jax.experimental import pallas as pl
from jax.experimental.pallas import tpu as pltpu
from jax.sharding import PartitionSpec as P

EPS = 1e-05
F32 = jnp.float32
BF16 = jnp.bfloat16
MESH = pl.DeviceIdType.MESH
LEAD = 32
LANES = 128
TAPS = 9
UNITS = ["S%d" % k for k in range(5)] + ["T%d%d" % (k, h) for h in range(2) for k in range(5)] + ["B%d" % k for k in range(6)]
ORDERS = {}
for order, names in (
    ("1xy2", ["B0"]),
    ("xy21", ["B1", "B5"]),
    ("x1y2", ["B2"]),
    ("y12x", ["B3"]),
    ("yx21", ["B4"]),
    ("x12", ["S0", "S1", "S2"]),
    ("12x", ["S3"]),
    ("1x2", ["S4"]),
    ("yx2", ["T00", "T01", "T11", "T21", "T30", "T41"]),
    ("y2x", ["T10"]),
    ("xy2", ["T20", "T31", "T40"]),
):
    for name in names:
        ORDERS[name] = order
TOKENS = [
    "sync0", "sync1", "sync2", "sync3", "sync4", "sync5", "B0", "B2", "sync6", "B0", "B1", "sync7", "B1", "end",
    "B3", "B5", "B0", "B5", "B4", "B1", "B4", "B3", "B2", "FW", "PS", "B0", "PT", "S2", "P0", "B1", "I", "B4",
    "T10", "S1", "T00", "B3", "B0", "I", "B2", "T30", "I", "T40", "B5", "B1", "B4", "B3", "T20", "S2", "I", "P1",
    "T00", "B0", "T10", "T31", "B1", "T11", "S3", "T41", "T40", "B5", "S2", "B4", "T21", "T10", "I", "T30", "B3",
    "I", "S1", "B2", "T41", "T11", "S3", "T00", "T01", "S4", "B4", "T31", "T21", "T30", "T40", "B2", "T41", "S0",
    "B5", "T01", "S1", "B4", "S4", "S2", "T21", "S3", "T01", "T11", "B0", "T10", "T00", "S1", "T20", "B5", "T31",
    "S0", "B2", "I", "T01", "I", "B3", "T10", "T30", "T41", "T20", "S4", "S3", "B2", "S1", "T11", "I", "S0",
    "T31", "T40", "T21", "B3", "T41", "S2", "T30", "S4", "S3", "T00", "T20", "T11", "S1", "B4", "S2", "B3", "T30",
    "B1", "B2", "B5", "S0", "B0", "T10", "T40", "T40", "T31", "T21", "T41", "S4", "T01", "T11", "T20", "S0", "B5",
    "T01", "T20", "S3", "T31", "T21", "S4", "B1", "T00", "S0"
]


def mish_parts(value):
    t = jnp.exp(-jnp.abs(value))
    positive = value >= 0
    t2 = t * t
    top = jnp.where(positive, 1.0 + 2.0 * t, t2 + 2.0 * t)
    inv = 1.0 / (top + jnp.where(positive, 2.0 * t2, 2.0))
    gate = top * inv
    slope = jnp.where(positive, t2, t) * (1.0 + t) * (4.0 * inv * inv)
    return value * gate, gate + value * slope


def dot(left, right):
    return jnp.dot(left, right, preferred_element_type=F32)


def dot_t(left, right):
    return lax.dot_general(left, right, (((1,), (1,)), ((), ())), preferred_element_type=F32)


def lane_tile(j, size=LANES):
    if isinstance(j, int):
        return pl.ds(j * size, size)
    return pl.ds(pl.multiple_of(j * size, size), size)


def share_place(share, bits):
    place = 0
    for bit in bits:
        place = 2 * place + (share >> bit) % 2
    return place


def rest_bits(n_dp):
    return list(range(n_dp.bit_length() - 2, 1, -1))


def flip(index, bit):
    low = lax.rem(index // (1 << bit), 2)
    return index + (1 - 2 * low) * (1 << bit), low


class Unit:
    def __init__(self, name, dims):
        grid, cin, width, half, n_dp, n_bn = dims
        self.name, self.kind = name, name[0]
        order = ORDERS.get(name, {"S": "1x2", "T": "yx2", "B": "xy12"}[self.kind])
        self.steps = []
        for letter in order:
            self.steps += {"x": ["x"], "y": [0], "1": [1], "2": rest_bits(n_dp)}[letter]
        self.bits = [step for step in self.steps if step != "x"]
        narrow = name in ("S4", "T40", "T41", "B2", "B3")
        rows, cols = (cin if self.kind == "B" else cin // 2), (width // 4 if narrow else width // 2)
        self.start = (rows, cols)
        self.pool = self.kind + ("n" if narrow and self.kind == "B" else "")
        self.shapes = [(rows, cols)] if self.kind == "B" else []
        for step in self.steps:
            rows, cols = (rows, cols // 2) if step == "x" else (rows // 2, cols)
            self.shapes.append((rows, cols))
        self.final = (rows, cols)
        self.n_moves = len(self.shapes)
        self.n_stages = self.n_moves + 3


def plan(dims):
    units = {name: Unit(name, dims) for name in UNITS}
    shapes, finals, message = {}, {}, 0
    for unit in units.values():
        unit.at = []
        for shape in unit.shapes:
            unit.at.append((shape, shapes.get(shape, 0)))
            shapes[shape] = shapes.get(shape, 0) + 1
        unit.across = (unit.final, finals.get(unit.final, 0))
        finals[unit.final] = finals.get(unit.final, 0) + 1
        unit.message = message
        message += unit.n_moves + 5
    fills, now = {k: [] for k in range(9)}, 8
    for token in TOKENS or ["B%d" % k for k in range(6) for unused in range(2)] + ["FW", "PS", "PT", "P0", "P1"]:
        if token[:4] == "sync":
            now = int(token[4:])
        elif token == "end":
            now = 8
        else:
            fills[now].append(token)
    stage = {name: sum(fill.count(name) for fill in fills.values()) for name in UNITS}
    while any(stage[name] < units[name].n_stages for name in UNITS):
        for name in UNITS:
            if stage[name] < units[name].n_stages:
                fills[8].append(name)
                stage[name] += 1
    kinds = ("S", "T", "B", "Bn")
    seen, count, free = {}, {kind: 0 for kind in kinds}, {kind: [] for kind in kinds}
    for k in range(9):
        for token in fills[k]:
            if token in units:
                unit = units[token]
                n = seen.get(token, 0)
                seen[token] = n + 1
                if n == 0:
                    if not free[unit.pool]:
                        free[unit.pool].append(count[unit.pool])
                        count[unit.pool] += 1
                    unit.slot = free[unit.pool].pop(0)
                elif n == 1:
                    free[unit.pool].append(unit.slot)
    return units, shapes, finals, message, fills, count


def fused_kernel(
    dims,
    count_ref, size_ref, images_hbm, cot_hbm, ws_hbm, wm_hbm, wsd_hbm, wr_hbm, w2_hbm, wt_hbm, wmg_hbm, aff_ref,
    act_hbm, igrad_hbm, out_stem, out_spatial, out_merge, out_transit, out_reduce, out_split, total_ref,
    eo_hbm, ex_hbm, ec_hbm, ao_hbm, ax_hbm, ac_hbm, g2_hbm, g0_hbm,
    landed, across_land, own_g, own_g2, mask, stat, msg, heard, sums_ref, sums_in,
    wsem, ssem, rsem, local_sem, give_sem, take_sem, m_send, m_recv, keep_sem, s_send, s_recv,
):
    grid, cin, width, half, n_dp, n_bn = dims
    units, shapes, finals, n_messages, fills, pool = plan(dims)
    shape_list, final_list = list(shapes), list(finals)
    pitch = grid + 1
    rows = own_g.shape[0] - LEAD
    blocks = rows // LANES
    share = cin // n_dp
    part = cin // 2
    quarter = width // 4
    half2 = half // 2
    n_bits = n_dp.bit_length() - 1
    wide_tiles, half_tiles = width // LANES, half // LANES
    t0, t1, t2, t3 = 0, wide_tiles, wide_tiles + half_tiles, wide_tiles + 2 * half_tiles

    dp, bn = lax.axis_index("dp"), lax.axis_index("bn")
    others = [(dp, lax.rem(bn + k, n_bn)) for k in range(1, n_bn)]
    sib, core = flip(bn, 0)
    over, cross = flip(bn, 1)
    bit_of = [flip(dp, b) for b in range(n_bits)]
    sibling, across = (dp, sib), (dp, over)
    along = [(bit_of[b][0], bn) for b in range(n_bits)]
    next_sib, pair_sib = (bit_of[0][0], sib), (bit_of[1][0], sib)
    partners = others + along + [next_sib, pair_sib]

    def remote(src, dst, send, recv, target):
        return pltpu.make_async_remote_copy(
            src_ref=src, dst_ref=dst, send_sem=send, recv_sem=recv, device_id=target, device_id_type=MESH)

    def part_of(which, size):
        return pl.ds(pl.multiple_of(which * size, size), size)

    barrier = pltpu.get_barrier_semaphore()
    for target in partners:
        pl.semaphore_signal(barrier, inc=1, device_id=target, device_id_type=MESH)

    places = lax.broadcasted_iota(jnp.int32, (rows, LANES), 0)
    row = (places * 3277) >> 16 if pitch == 20 else places // pitch
    col = places - row * pitch
    size = jnp.where(count_ref[0] > 0, size_ref[0], 0)
    mask[...] = jnp.where((row < size) & (col < size), 1.0, 0.0).astype(F32)
    own_g[rows:, :] = jnp.zeros((LEAD, width), F32)

    def put_sums(sync, j, first, second, tiles):
        msg[sync, pl.ds(j, 1), :] = first
        msg[sync, pl.ds(tiles + j, 1), :] = second

    def column_sums(sync, z, j, tiles):
        zm = z * mask[...]
        put_sums(sync, j, jnp.sum(zm, axis=0, keepdims=True), jnp.sum(zm * z, axis=0, keepdims=True), tiles)

    def matmul_stats(sync, left, weight, out, cols, ready=lambda n: None):
        def body(n, _):
            ready(n)
            z = dot(left[...], weight[:, lane_tile(n, 256)])
            out[:, lane_tile(n, 256)] = z
            for h in range(2):
                column_sums(sync, z[:, h * LANES : (h + 1) * LANES], 2 * n + h, cols // LANES)
            return 0
        lax.fori_loop(0, cols // 256, body, 0)

    def greet(sync):
        return [
            remote(msg.at[sync], heard.at[sync, bn], ssem.at[sync, k], rsem.at[sync, k], target)
            for k, target in enumerate(others)]

    def send(sync):
        heard[sync, bn] = msg[sync]
        for copy in greet(sync):
            copy.start()

    def receive(sync):
        for copy in greet(sync):
            copy.wait()
        total = heard[sync, 0]
        for k in range(1, n_bn):
            total = total + heard[sync, k]
        return total

    def set_stat(slot, total, count, first_tile, tiles):
        mean = total[0:tiles] / count
        spread = total[tiles : 2 * tiles] / count - mean * mean
        stat[slot, 0, 0:tiles, :] = mean
        stat[slot, 1, 0:tiles, :] = lax.rsqrt(spread + EPS)
        for j in range(tiles):
            stat[slot, 2, j : j + 1, :] = aff_ref[2 * (first_tile + j) : 2 * (first_tile + j) + 1, :]
            stat[slot, 3, j : j + 1, :] = aff_ref[2 * (first_tile + j) + 1 : 2 * (first_tile + j) + 2, :]

    def per_tile(tiles, body):
        def step(j, _):
            body(j, lane_tile(j))
            return 0
        lax.fori_loop(0, tiles, step, 0)

    def normed(slot, z, j, cs, r):
        scaled = (z[r, cs] - stat[slot, 0, pl.ds(j, 1), :]) * stat[slot, 1, pl.ds(j, 1), :]
        return scaled, scaled * stat[slot, 2, pl.ds(j, 1), :] + stat[slot, 3, pl.ds(j, 1), :]

    def forward(slot, z, keep, tiles, put):
        def body(j, cs):
            for b in range(blocks):
                r = pl.ds(b * LANES, LANES)
                unused, before = normed(slot, z, j, cs, r)
                act, slope = mish_parts(before)
                keep[r, cs] = slope * mask[r, :]
                put(r, cs, act * mask[r, :])
        per_tile(tiles, body)

    def backward_sums(sync, slot, z, inner_ref, j, cs, upstream, tiles):
        first = jnp.zeros((1, LANES), F32)
        second = jnp.zeros((1, LANES), F32)
        for b in range(blocks):
            r = pl.ds(b * LANES, LANES)
            inner = inner_ref[r, cs] * upstream[r, cs]
            inner_ref[r, cs] = inner
            scaled = (z[r, cs] - stat[slot, 0, pl.ds(j, 1), :]) * stat[slot, 1, pl.ds(j, 1), :]
            first = first + jnp.sum(inner, axis=0, keepdims=True)
            second = second + jnp.sum(inner * scaled, axis=0, keepdims=True)
        put_sums(sync, j, first, second, tiles)

    def set_back(slot, total, count, first_tile, tiles):
        for j in range(tiles):
            sums_ref[2 * (first_tile + j) : 2 * (first_tile + j) + 1, :] = total[tiles + j : tiles + j + 1]
            sums_ref[2 * (first_tile + j) + 1 : 2 * (first_tile + j) + 2, :] = total[j : j + 1]
        stat[slot, 4, 0:tiles, :] = total[0:tiles] / count
        stat[slot, 5, 0:tiles, :] = total[tiles : 2 * tiles] / count

    def backward(slot, z, inner_ref, tiles, put):
        def body(j, cs):
            for b in range(blocks):
                r = pl.ds(b * LANES, LANES)
                inv = stat[slot, 1, pl.ds(j, 1), :]
                scaled = (z[r, cs] - stat[slot, 0, pl.ds(j, 1), :]) * inv
                pull = mask[r, :] * (stat[slot, 4, pl.ds(j, 1), :] + scaled * stat[slot, 5, pl.ds(j, 1), :])
                value = (inner_ref[r, cs] - pull) * (inv * stat[slot, 2, pl.ds(j, 1), :])
                put(r, cs, value.astype(BF16))
        per_tile(tiles, body)

    local = {}
    stage = {name: 0 for name in units}

    def landing(unit, k):
        shape, n = unit.at[k]
        return landed[shape_list.index(shape)].at[n]

    def source(unit, k):
        return local[unit.pool](unit.slot) if k == 0 else landing(unit, k - 1)

    def move_of(unit, k):
        size_r, size_c = unit.shapes[k]
        step = "c" if unit.kind == "B" and k == 0 else unit.steps[k - (unit.kind == "B")]
        if step == "c":
            return sibling, (pl.ds(0, size_r), part_of(1 - core, size_c)), (None, part_of(core, size_c))
        if step == "x":
            return across, (pl.ds(0, size_r), part_of(1 - cross, size_c)), (None, part_of(cross, size_c))
        bit = bit_of[step][1]
        return along[step], (part_of(1 - bit, size_r), pl.ds(0, size_c)), (bit, pl.ds(0, size_c))

    def move(unit, k):
        target, gone, unused = move_of(unit, k)
        m = unit.message + k
        return remote(source(unit, k).at[gone[0], gone[1]], landing(unit, k), m_send.at[m], m_recv.at[m], target)

    def add_own(unit, k):
        unused, unused2, (bit, columns) = move_of(unit, k)
        size = unit.shapes[k][0]
        src, dst = source(unit, k), landing(unit, k)
        n = min(size, 64)

        def body(i, _):
            r = pl.ds(pl.multiple_of(i * n, n), n)
            own = r if bit is None else pl.ds(pl.multiple_of(bit * size + i * n, 8), n)
            dst[r, :] = dst[r, :] + src[own, columns]
            return 0
        lax.fori_loop(0, size // n, body, 0)

    def pieces(unit, cross_at):
        k = int(unit.name[1])
        at = 2 * core + cross_at
        taps_of = range(2 * k, min(2 * k + 2, TAPS))
        if unit.kind == "T":
            col = part_of(4 * core + 2 * int(unit.name[2]) + cross_at, LANES)
            return [(out_stem.at[t, :, col], (t - 2 * k) * LANES) for t in taps_of]
        if unit.kind == "S":
            return [(out_spatial.at[t, :, part_of(at, half // 4)], (t - 2 * k) * (half // 4)) for t in taps_of]
        if k < 2:
            return [(out_merge.at[pl.ds(k * share, share), part_of(at, quarter)], 0)]
        if k < 4:
            return [((out_transit if k == 2 else out_reduce).at[:, part_of(at, half // 4)], 0)]
        return [(out_split.at[core, pl.ds((k - 4) * share, share), part_of(cross_at, half2)], 0)]

    def arrival(unit):
        shape, n = unit.across
        return across_land[final_list.index(shape)].at[n]

    def give_across(unit):
        m = unit.message + unit.n_moves
        return remote(landing(unit, unit.n_moves - 1), arrival(unit), m_send.at[m], m_recv.at[m], across)

    def spread_piece(unit, mine):
        block = landing(unit, unit.n_moves - 1) if mine else arrival(unit)
        m = unit.message + unit.n_moves + (1 if mine else 3)
        copies = []
        for n, (place, first) in enumerate(pieces(unit, cross if mine else 1 - cross)):
            src = block.at[:, pl.ds(first, place.shape[-1])]
            copies.append(pltpu.make_async_copy(src, place, keep_sem.at[m + n]))
            copies.append(remote(src, place, m_send.at[m + n], m_recv.at[m + n], sibling))
        return copies

    def advance(name, compute):
        unit = units[name]
        k = stage[name]
        stage[name] = k + 1
        if k == 0:
            compute(unit)
            move(unit, 0).start()
        elif k <= unit.n_moves:
            move(unit, k - 1).wait()
            add_own(unit, k - 1)
            if k < unit.n_moves:
                move(unit, k).start()
            else:
                give_across(unit).start()
                for copy in spread_piece(unit, True):
                    copy.start()
        elif k == unit.n_moves + 1:
            give_across(unit).wait()
            for copy in spread_piece(unit, False):
                copy.start()
        else:
            for copy in spread_piece(unit, True) + spread_piece(unit, False):
                copy.wait()

    next_bit, pair_bit = bit_of[0][1], bit_of[1][1]
    next_bits, pair_bits = [0, 1] + rest_bits(n_dp), [1, 0] + rest_bits(n_dp)

    def field_gives(src, dst, which_of, size, first, targets):
        return [
            remote(src.at[pl.ds(0, rows), part_of(which_of(which), size)], dst.at[k], give_sem.at[first + k], take_sem.at[first + k], target)
            for k, (target, which) in enumerate(targets)]
    gives2 = field_gives(own_g2, g2_hbm, lambda w: w, half2, 0, ((sibling, 1 - core), (along[0], core), (next_sib, 1 - core)))
    gives0 = [
        field_gives(own_g, g0_hbm.at[h], lambda w, h=h: 2 * w + h, quarter, 3 + 3 * h,
                    ((sibling, 1 - core), (along[1], core), (pair_sib, 1 - core)))
        for h in range(2)]

    forwards = [
        remote(ax_hbm, ac_hbm.at[1], give_sem.at[14], take_sem.at[14], sibling),
        remote(ex_hbm, ec_hbm.at[1], give_sem.at[15], take_sem.at[15], sibling)]

    def turned_block(block, k, dst, bits, parts=1):
        for piece in range(LANES // share):
            at_row = k * LANES + piece * share
            s, h = (at_row // share) // parts, (at_row // share) % parts
            at = share_place(s, bits[h]) * share
            dst(h, pl.ds(at, share), block[piece * share : (piece + 1) * share])

    def chain_phase(wms, wr, w2, wt, wmg, taps, z0, d0, stem_low, et):
        smalls = [
            pltpu.make_async_copy(src, dst, wsem.at[2 + k])
            for k, (src, dst) in enumerate(
                [(wm_hbm, wms.at[:, pl.ds(0, half)]), (wsd_hbm, wms.at[:, pl.ds(half, half)]),
                 (wr_hbm, wr), (w2_hbm, w2), (wt_hbm, wt), (wmg_hbm, wmg)])
        ]

        def first_phase(ws, images, phases, img_row):
            load_i = pltpu.make_async_copy(images_hbm, images, wsem.at[0])

            def load_w(n):
                block = lane_tile(n, 256)
                return pltpu.make_async_copy(ws_hbm.at[:, block], ws.at[:, block], wsem.at[8 + n])
            load_i.start()
            for n in range(width // 256):
                load_w(n).start()
            for p in range(4):
                phases[p, 0:LEAD, :] = jnp.zeros((LEAD, cin), F32)
                tail = LEAD + pitch * grid
                phases[p, tail:, :] = jnp.zeros((phases.shape[1] - tail, cin), F32)
            load_i.wait()
            for line in range(2 * grid):
                slot = line % 2
                value = images[line].astype(F32)
                for k in range(cin // LANES):
                    img_row[slot, k, 0 : 2 * grid, :] = value[:, k * LANES : (k + 1) * LANES]
                start = LEAD + pitch * (line // 2)
                for odd in range(2):
                    p = 2 * (line % 2) + odd
                    for k in range(cin // LANES):
                        phases[p, start : start + grid, k * LANES : (k + 1) * LANES] = img_row[slot, k, pl.ds(odd, grid, stride=2), :]
                    phases[p, start + grid : start + grid + 1, :] = jnp.zeros((1, cin), F32)
            for k in range(TAPS):
                a, b = k // 3, k % 3
                p = 2 * (a != 1) + (b != 1)
                off = LEAD - pitch * (a == 0) - (b == 0)
                taps[:, k * cin : (k + 1) * cin] = phases[p, off : off + rows, :].astype(BF16)
            for load in smalls:
                load.start()
            matmul_stats(0, taps, ws, z0, width, lambda n: load_w(n).wait())
            msg[0, 2 * wide_tiles : 2 * wide_tiles + 8, :] = jnp.zeros((8, LANES), F32) + jnp.sum(mask[...], axis=0, keepdims=True)
            pl.semaphore_wait(barrier, len(partners))
            send(0)

            def turn_phase(p, _):
                for k in range(cin // LANES):
                    block = phases[p, LEAD : LEAD + rows, k * LANES : (k + 1) * LANES].T

                    def put(h, r, value):
                        et[p, r, :] = value
                    turned_block(block, k, put, [pair_bits])
                return 0
            lax.fori_loop(0, 4, turn_phase, 0)

        pl.run_scoped(
            first_phase, pltpu.VMEM((TAPS * cin, width), BF16), pltpu.VMEM((2 * grid, 2 * grid, cin), BF16),
            pltpu.VMEM((4, LEAD + rows, cin), F32), pltpu.VMEM((2, cin // LANES, -(-2 * grid // 8) * 8, LANES), F32))
        keep_e = pltpu.make_async_copy(et.at[0:4, part_of(pair_bit, part), :], eo_hbm, local_sem.at[0])
        give_e = remote(et.at[0:4, part_of(1 - pair_bit, part), :], ex_hbm, give_sem.at[9], take_sem.at[9], along[1])
        keep_e.start()
        give_e.start()
        own_e = [
            remote(et.at[pl.ds(2 * h, 2), part_of(pair_bit, part), :], ec_hbm.at[0, pl.ds(2 * h, 2)],
                   give_sem.at[11 + h], take_sem.at[11 + h], sibling)
            for h in range(2)]

        def rest_phase(
            z1, d1, z2, d2, wide, narrow, main_path, apad, gpad, back, joined, main_low, res_low, mside, turned, act, cot_in, tile,
        ):
            z3 = own_g.at[pl.ds(0, rows)]
            i3, cot = wide.at[0, pl.ds(0, rows)], wide.at[1, pl.ds(0, rows)]
            merge_in, tside, red_in = stem_low, joined, main_low
            local["B"] = lambda slot: wide.at[slot]
            local["Bn"] = lambda slot: narrow.at[slot]
            load_cot = pltpu.make_async_copy(cot_hbm, cot_in, local_sem.at[1])
            load_cot.start()
            for ref in (apad, gpad):
                ref[0:LEAD, :] = jnp.zeros((LEAD, half), F32)
                ref[LEAD + rows :, :] = jnp.zeros((LEAD, half), F32)

            def turn(src, first, parts):
                for k in range(parts * half // LANES):
                    block = src[:, k * LANES : (k + 1) * LANES].astype(F32).T

                    def put(h, r, value):
                        turned[first + h, r, :] = value.astype(BF16)
                    turned_block(block, k, put, [units["B%d" % (first + h)].bits for h in range(parts)], parts)

            def compute(unit):
                k = int(unit.name[1])
                right = [merge_in, merge_in, tside, red_in, mside, mside][k]
                dst = local[unit.pool](unit.slot)
                for n in range(2 * unit.start[1] // 256):
                    dst[:, pl.ds(n * 256, 256)] = dot(turned[k], right[:, pl.ds(n * 256, 256)])

            def fill(sync):
                for token in fills[sync]:
                    advance(token, compute)

            total = receive(0)
            count = total[2 * wide_tiles : 2 * wide_tiles + 1, 0:1]
            set_stat(0, total, count, t0, wide_tiles)

            def put_stem(r, cs, value):
                stem_low[r, cs] = value.astype(BF16)
            forward(0, z0, d0, wide_tiles, put_stem)
            smalls[0].wait()
            smalls[1].wait()
            for n in range(half // 256):
                y = dot(stem_low[...], wms[:, lane_tile(n, 256)])
                main_path[:, lane_tile(n, 256)] = y
                main_low[:, lane_tile(n, 256)] = y.astype(BF16)
            smalls[2].wait()
            matmul_stats(1, main_low, wr, z1, half)
            send(1)
            own_e[0].start()
            for n in range(half // 256):
                y = dot(stem_low[...], wms[:, lane_tile(half // 256 + n, 256)])
                joined[:, lane_tile(half // 256 + n, 256)] = y.astype(BF16)
            turn(stem_low, 4, 2)
            set_stat(1, receive(1), count, t1, half_tiles)

            def put_reduce(r, cs, value):
                apad[pl.ds(LEAD + r.start, r.size), cs] = value.astype(BF16).astype(F32)
            forward(1, z1, d1, half_tiles, put_reduce)
            for k in range(TAPS):
                off = LEAD + pitch * (k // 3 - 1) + k % 3 - 1
                taps[:, k * half : (k + 1) * half] = apad[off : off + rows, :].astype(BF16)
            smalls[3].wait()
            matmul_stats(2, taps, w2, z2, half)
            send(2)
            own_e[1].start()
            for k in range(half // LANES):
                def put_a(h, r, value):
                    et[4, r, :] = value
                turned_block(apad[LEAD : LEAD + rows, k * LANES : (k + 1) * LANES].T, k, put_a, [next_bits])
            keep_a = pltpu.make_async_copy(et.at[4, part_of(next_bit, part), :], ao_hbm, local_sem.at[2])
            give_a = remote(et.at[4, part_of(1 - next_bit, part), :], ax_hbm, give_sem.at[10], take_sem.at[10], along[0])
            own_a = remote(et.at[4, part_of(next_bit, part), :], ac_hbm.at[0], give_sem.at[13], take_sem.at[13], sibling)
            keep_a.start()
            give_a.start()
            turn(main_low, 3, 1)
            load_cot.wait()
            for r in range(grid):
                cot[r * pitch : r * pitch + grid, :] = cot_in[r].astype(F32)
                cot[r * pitch + grid : (r + 1) * pitch, :] = jnp.zeros((1, width), F32)
            cot[grid * pitch :, :] = jnp.zeros((rows - grid * pitch, width), F32)
            set_stat(2, receive(2), count, t2, half_tiles)

            def put_spatial(r, cs, value):
                res_low[r, cs] = (main_path[r, cs] + value).astype(BF16)
            forward(2, z2, d2, half_tiles, put_spatial)
            smalls[4].wait()
            for n in range(half // 256):
                joined[:, lane_tile(n, 256)] = dot(res_low[...], wt[:, lane_tile(n, 256)]).astype(BF16)
            smalls[5].wait()
            matmul_stats(3, joined, wmg, z3, width)
            send(3)
            own_a.start()
            turn(joined, 0, 2)
            set_stat(3, receive(3), count, t3, wide_tiles)

            def merge_tile(j, cs):
                for b in range(blocks):
                    r = pl.ds(b * LANES, LANES)
                    unused, before = normed(3, z3, j, cs, r)
                    value, slope = mish_parts(before)
                    tile[r, :] = value * mask[r, :]
                    i3[r, cs] = slope * mask[r, :]
                backward_sums(4, 3, z3, i3, j, cs, cot, wide_tiles)
                cot[:, cs] = tile[...]
            per_tile(wide_tiles, merge_tile)
            send(4)

            def act_tile(j, cs):
                for line in range(grid):
                    act[pl.ds(line * grid * wide_tiles + j, grid, stride=wide_tiles), :] = cot[line * pitch : line * pitch + grid, cs]
            per_tile(wide_tiles, act_tile)
            store_act = pltpu.make_async_copy(act, act_hbm, local_sem.at[3])
            store_act.start()
            turn(res_low, 2, 1)
            fill(4)
            set_back(3, receive(4), count, t3, wide_tiles)

            def put_merge(r, cs, value):
                merge_in[r, cs] = value
            backward(3, z3, i3, wide_tiles, put_merge)
            for n in range(width // 256):
                tside[:, lane_tile(n, 256)] = dot_t(merge_in[...], wmg[lane_tile(n, 256), :]).astype(BF16)
            for n in range(half // 256):
                back[:, lane_tile(n, 256)] = dot_t(tside[:, 0:half], wt[lane_tile(n, 256), :])

            def spatial_tile(j, cs):
                backward_sums(5, 2, z2, d2, j, cs, back, half_tiles)
            per_tile(half_tiles, spatial_tile)
            send(5)
            fill(5)
            set_back(2, receive(5), count, t2, half_tiles)

            def put_spatial_in(r, cs, value):
                gpad[pl.ds(LEAD + r.start, r.size), cs] = value.astype(F32)
                own_g2[r, cs] = value.astype(F32)
            backward(2, z2, d2, half_tiles, put_spatial_in)
            for give in gives2:
                give.start()
            for k in range(TAPS):
                off = LEAD - pitch * (k // 3 - 1) - (k % 3 - 1)
                taps[:, k * half : (k + 1) * half] = gpad[off : off + rows, :].astype(BF16)

            def reduce_columns(n, _):
                value = jnp.zeros((rows, 256), F32)
                for k in range(TAPS):
                    value = value + dot_t(taps[:, k * half : (k + 1) * half], w2[pl.ds(pl.multiple_of(k * half + n * 256, 256), 256), :])
                main_path[:, lane_tile(n, 256)] = value
                return 0
            lax.fori_loop(0, half // 256, reduce_columns, 0)

            def reduce_tile(j, cs):
                backward_sums(6, 1, z1, d1, j, cs, main_path, half_tiles)
            per_tile(half_tiles, reduce_tile)
            send(6)
            mside[:, half : 2 * half] = tside[:, half : 2 * half]
            fill(6)
            set_back(1, receive(6), count, t1, half_tiles)

            def put_reduce_in(r, cs, value):
                red_in[r, cs] = value
            backward(1, z1, d1, half_tiles, put_reduce_in)
            for n in range(half // 256):
                mside[:, lane_tile(n, 256)] = (back[:, lane_tile(n, 256)] + dot_t(red_in[...], wr[lane_tile(n, 256), :])).astype(BF16)

            def stem_columns(n, _):
                z3[:, lane_tile(n, 256)] = dot_t(mside[...], wms[lane_tile(n, 256), :])
                return 0
            lax.fori_loop(0, width // 256, stem_columns, 0)

            def stem_tile(j, cs):
                backward_sums(7, 0, z0, d0, j, cs, z3, wide_tiles)
            per_tile(wide_tiles, stem_tile)
            send(7)
            fill(7)
            set_back(0, receive(7), count, t0, wide_tiles)

            def put_stem_in(r, cs, value):
                own_g[r, cs] = value.astype(F32)
            backward(0, z0, d0, wide_tiles, put_stem_in)
            for gives in gives0:
                for give in gives:
                    give.start()
            while any(units[name].kind == "B" and stage[name] < 2 for name in units) or "FW" in fills[8]:
                token = fills[8].pop(0)
                if token == "FW":
                    give_e.wait()
                    give_a.wait()
                    for forward_copy in forwards:
                        forward_copy.start()
                else:
                    advance(token, compute)
            for copy in own_e + [own_a, keep_e, keep_a, store_act]:
                copy.wait()

        pl.run_scoped(
            rest_phase,
            pltpu.VMEM((rows, half), F32), pltpu.VMEM((rows, half), F32), pltpu.VMEM((rows, half), F32), pltpu.VMEM((rows, half), F32),
            pltpu.VMEM((max(2, pool["B"]), cin, width), F32), pltpu.VMEM((pool["Bn"], cin, half), F32),
            pltpu.VMEM((rows, half), F32), pltpu.VMEM((LEAD + rows + LEAD, half), F32), pltpu.VMEM((LEAD + rows + LEAD, half), F32),
            pltpu.VMEM((rows, half), F32), pltpu.VMEM((rows, 2 * half), BF16), pltpu.VMEM((rows, half), BF16),
            pltpu.VMEM((rows, half), BF16), pltpu.VMEM((rows, 2 * half), BF16), pltpu.VMEM((6, cin, rows), BF16),
            pltpu.VMEM((grid * grid * wide_tiles, LANES), F32), pltpu.VMEM((grid, grid, width), BF16), pltpu.VMEM((rows, LANES), F32))

    pl.run_scoped(
        chain_phase,
        pltpu.VMEM((width, 2 * half), BF16), pltpu.VMEM((half, half), BF16), pltpu.VMEM((TAPS * half, half), BF16),
        pltpu.VMEM((half, half), BF16), pltpu.VMEM((width, width), BF16), pltpu.VMEM((rows, TAPS * cin), BF16),
        pltpu.VMEM((rows, width), F32), pltpu.VMEM((rows, width), F32), pltpu.VMEM((rows, width), BF16),
        pltpu.VMEM((5, cin, rows), F32))

    def last_phase(g2r, g0r, at_land, at_cat, spatial, et_land, et_cat, shifted, own_shift, image, weight, stem_blocks, igrad):
        local["S"] = lambda slot: spatial.at[slot]
        local["T"] = lambda slot: stem_blocks.at[slot]
        offsets = (0, 1, pitch, pitch + 1)
        image_taps = [4, 3, 5, 1, 7, 0, 2, 6, 8]
        done = []
        sums_done = []

        def load_weight(n):
            k = image_taps[n]
            return pltpu.make_async_copy(ws_hbm.at[pl.ds(k * cin, cin)], weight.at[n % 2], wsem.at[n % 2])
        load_weight(0).start()
        own_parts = [
            pltpu.make_async_copy(src, dst, local_sem.at[9 + k])
            for k, (src, dst) in enumerate(
                ((ao_hbm, at_land.at[0]), (ax_hbm, at_land.at[1]), (eo_hbm, et_land.at[0]), (ex_hbm, et_land.at[1])))]
        for load in own_parts:
            load.start()

        def sums_step(k):
            return remote(total_ref if k else sums_ref, sums_in.at[k], s_send.at[k], s_recv.at[k], along[k])

        def sums_next():
            k = len(sums_done)
            if k < n_bits:
                sums_done.append(k)
                sums_step(k).wait()
                total_ref[...] = (total_ref[...] if k else sums_ref[...]) + sums_in[k]
                if k + 1 < n_bits:
                    sums_step(k + 1).start()
        sums_step(0).start()
        for k in range(4):
            g2r[k, 0:LEAD, :] = jnp.zeros((LEAD, half2), F32)
            g2r[k, LEAD + rows :, :] = jnp.zeros((LEAD, half2), F32)
            for h in range(2):
                g0r[h, k, rows:, :] = jnp.zeros((LEAD, quarter), F32)

        def tap(k):
            a, b = k // 3, k % 3
            return 2 * (a != 1) + (b != 1), 2 * (a == 0) + (b == 0)

        def fetch(pairs, first):
            loads = [pltpu.make_async_copy(src, dst, local_sem.at[first + k]) for k, (src, dst) in enumerate(pairs)]
            for load in loads:
                load.start()
            for load in loads:
                load.wait()

        def compute(unit):
            k = int(unit.name[1])
            c = unit.start[1] // 2
            dst = local[unit.pool](unit.slot)
            for h in range(2):
                t = 2 * k + h
                if t == TAPS:
                    continue
                if unit.kind == "T":
                    p, sh = tap(t)
                    value = dot(et_cat[p], shifted[int(unit.name[2]), sh])
                else:
                    off = LEAD - pitch * (t // 3 - 1) - (t % 3 - 1)
                    right = jnp.concatenate([g2r[s, off : off + rows, :].astype(BF16) for s in range(4)], axis=0)
                    value = dot(at_cat[...], right)
                for x in range(2):
                    dst[:, c * x + LANES * h : c * x + LANES * (h + 1)] = value[:, LANES * x : LANES * (x + 1)]

        def image_step():
            n = len(done)
            k = image_taps[n]
            p, sh = tap(k)
            if n + 1 < TAPS:
                load_weight(n + 1).start()
            load_weight(n).wait()
            for m in range(cin // 256):
                c = slice(m * 256, (m + 1) * 256)
                value = dot_t(own_shift[sh], weight[n % 2, c, :])
                image[:, c] = value if k in (4, 3, 1, 0) else image[:, c] + value
            done.append(k)
            if k in (4, 5, 7, 8):
                for r in range(grid):
                    for m in range(cin // LANES):
                        start = ((2 * r + p // 2) * 2 * grid + p % 2) * (cin // LANES) + m
                        igrad[pl.ds(start, grid, stride=2 * cin // LANES), :] = image[r * pitch : r * pitch + grid, m * LANES : (m + 1) * LANES]
            if len(done) == TAPS:
                pltpu.make_async_copy(igrad, igrad_hbm, local_sem.at[8]).start()

        for token in fills[8]:
            if token == "PS":
                forwards[0].wait()
                own_parts[0].wait()
                own_parts[1].wait()
                for give in gives2:
                    give.wait()
                fetch([(ac_hbm.at[0], at_land.at[2]), (ac_hbm.at[1], at_land.at[3])]
                      + [(g2_hbm.at[s], g2r.at[s + 1, pl.ds(LEAD, rows)]) for s in range(3)]
                      + [(own_g2.at[:, part_of(core, half2)], g2r.at[0, pl.ds(LEAD, rows)])], 0)
                for slot, n in enumerate((0, 2, 1, 3)):
                    at_cat[:, slot * rows : (slot + 1) * rows] = at_land[n].astype(BF16)
                sums_next()
            elif token == "PT":
                forwards[1].wait()
                own_parts[2].wait()
                own_parts[3].wait()
                fetch([(ec_hbm.at[0], et_land.at[2]), (ec_hbm.at[1], et_land.at[3])], 0)
                for p in range(4):
                    for slot, n in enumerate((0, 2, 1, 3)):
                        et_cat[p, :, slot * rows : (slot + 1) * rows] = et_land[n, p].astype(BF16)
                for sh, off in enumerate(offsets):
                    own_shift[sh] = own_g[off : off + rows, :].astype(BF16)
                sums_next()
            elif token in ("P0", "P1"):
                h = int(token[1])
                for give in gives0[h]:
                    give.wait()
                fetch([(g0_hbm.at[h, s], g0r.at[h, s + 1, pl.ds(0, rows)]) for s in range(3)]
                      + [(own_g.at[pl.ds(0, rows), part_of(2 * core + h, quarter)], g0r.at[h, 0, pl.ds(0, rows)])], 0)
                for sh, off in enumerate(offsets):
                    for s in range(4):
                        shifted[h, sh, s * rows : (s + 1) * rows, :] = g0r[h, s, off : off + rows, :].astype(BF16)
                sums_next()
            elif token == "I":
                if len(done) < TAPS:
                    image_step()
            elif token in units:
                advance(token, compute)
        while len(done) < TAPS:
            image_step()
        for k in range(n_bits):
            sums_next()
        pltpu.make_async_copy(igrad, igrad_hbm, local_sem.at[8]).wait()

    pl.run_scoped(
        last_phase,
        pltpu.VMEM((4, LEAD + rows + LEAD, half2), F32), pltpu.VMEM((2, 4, rows + LEAD, quarter), F32),
        pltpu.VMEM((4, part, rows), F32), pltpu.VMEM((part, 4 * rows), BF16), pltpu.VMEM((pool["S"], part, width // 2), F32),
        pltpu.VMEM((4, 4, part, rows), F32), pltpu.VMEM((4, part, 4 * rows), BF16),
        pltpu.VMEM((2, 4, 4 * rows, quarter), BF16), pltpu.VMEM((4, rows, width), BF16), pltpu.VMEM((rows, cin), F32),
        pltpu.VMEM((2, cin, width), BF16), pltpu.VMEM((pool["T"], part, width // 2), F32),
        pltpu.VMEM((4 * grid * grid * (cin // LANES), LANES), F32))


def fused(dims, count, size, images, cot, ws, wm, wsd, wr, w2, wt, wmg, aff):
    grid, cin, width, half, n_dp, n_bn = dims
    units, shapes, finals, n_messages, fills, pool = plan(dims)
    rows = -(-grid * (grid + 1) // LANES) * LANES
    share, part = cin // n_dp, cin // 2
    tiles = width // LANES
    n_bits = n_dp.bit_length() - 1
    sd, dma = jax.ShapeDtypeStruct, pltpu.SemaphoreType.DMA
    vm, any_, sm = (pl.BlockSpec(memory_space=space) for space in (pltpu.VMEM, pl.ANY, pltpu.SMEM))
    out = (
        sd((grid * grid * tiles, LANES), F32), sd((4 * grid * grid * (cin // LANES), LANES), F32),
        sd((TAPS, share, width), F32), sd((TAPS, share, half), F32), sd((2 * share, width), F32),
        sd((share, half), F32), sd((share, half), F32), sd((2, 2 * share, half), F32), sd(aff.shape, F32),
        sd((4, part, rows), F32), sd((4, part, rows), F32), sd((2, 4, part, rows), F32),
        sd((part, rows), F32), sd((part, rows), F32), sd((2, part, rows), F32),
        sd((3, rows, half // 2), F32), sd((2, 3, rows, width // 4), F32),
    )
    scratch = [
        [pltpu.VMEM((n,) + shape, F32) for shape, n in shapes.items()],
        [pltpu.VMEM((n,) + shape, F32) for shape, n in finals.items()],
        pltpu.VMEM((rows + LEAD, width), F32), pltpu.VMEM((rows, half), F32),
        pltpu.VMEM((rows, LANES), F32), pltpu.VMEM((4, 6, 8, LANES), F32),
        pltpu.VMEM((8, 3 * tiles, LANES), F32), pltpu.VMEM((8, n_bn, 3 * tiles, LANES), F32),
        pltpu.VMEM(aff.shape, F32), pltpu.VMEM((n_bits,) + aff.shape, F32),
        dma((8 + width // 256,)), dma((8, n_bn - 1)), dma((8, n_bn - 1)), dma((16,)), dma((16,)), dma((16,)),
        dma((n_messages,)), dma((n_messages,)), dma((n_messages,)), dma((n_bits,)), dma((n_bits,)),
    ]
    return pl.pallas_call(
        functools.partial(fused_kernel, dims),
        out_shape=out,
        in_specs=[sm, sm] + [any_] * 9 + [vm],
        out_specs=(any_,) * 8 + (vm,) + (any_,) * 8,
        scratch_shapes=scratch,
        compiler_params=pltpu.CompilerParams(collective_id=0, has_side_effects=True, vmem_limit_bytes=64 * 2**20 - 65536),
        name="section",
    )(count, size, images, cot, ws, wm, wsd, wr, w2, wt, wmg, aff)


def finish_kernel(parts, n, tiles, sums_hbm, *refs):
    ins, outs, affine_hbm = refs[:n], refs[n : n + len(parts)], refs[n + len(parts)]
    held, (sums, affine, sem_a), sems = refs[n + len(parts) + 1 : n + 2 * len(parts) + 1], refs[-5:-2], refs[-2:]
    load_sums = pltpu.make_async_copy(sums_hbm, sums, sem_a.at[0])
    store_affine = pltpu.make_async_copy(affine, affine_hbm, sem_a.at[1])
    load_sums.start()
    steps = []
    for k, (which, row) in enumerate(parts):
        src, dst, by = ins[which] if row is None else ins[which].at[row], outs[k], held[k]
        size = dst.shape[0]
        cuts = 4 if size % 32 == 0 or size >= 2048 else 1
        edge = [size // cuts // 8 * 8 * c for c in range(cuts)] + [size]
        for c in range(cuts):
            r = pl.ds(edge[c], edge[c + 1] - edge[c])
            at = len(steps)
            steps.append((
                pltpu.make_async_copy(src.at[r], by.at[r], sems[0].at[at]),
                pltpu.make_async_copy(by.at[r], dst.at[r], sems[1].at[at])))
    for step in steps:
        step[0].start()
    load_sums.wait()
    first = 2 * tiles * lax.axis_index("dp")
    for t in range(affine.shape[0]):
        for c in range(2):
            affine[t, c : c + 1, :] = sums[pl.ds(first + 2 * t + c, 1), :]
    store_affine.start()
    for step in steps:
        step[0].wait()
        step[1].start()
    for step in steps:
        step[1].wait()
    store_affine.wait()


def finish(sums, tiles, arrays, parts):
    any_ = pl.BlockSpec(memory_space=pl.ANY)
    affine = (max(1, tiles), 2, LANES)
    shapes = [arrays[which].shape if row is None else arrays[which].shape[1:] for which, row in parts]
    return pl.pallas_call(
        functools.partial(finish_kernel, parts, len(arrays), tiles),
        out_shape=tuple(jax.ShapeDtypeStruct(shape, F32) for shape in shapes + [affine]),
        in_specs=[any_] * (len(arrays) + 1),
        out_specs=(any_,) * (len(parts) + 1),
        scratch_shapes=[pltpu.VMEM(shape, F32) for shape in shapes + [sums.shape, affine]] + [pltpu.SemaphoreType.DMA((2,))] + [pltpu.SemaphoreType.DMA((4 * len(parts),))] * 2,
        compiler_params=pltpu.CompilerParams(vmem_limit_bytes=63 * 2**20),
        name="finish",
    )(sums, *arrays)


def local(
    images, image_count, image_size, cotangent, stem_weight, split_main, split_side,
    block_reduce, block_spatial, block_transit, merge_weight, affines,
):
    n_dp, n_bn = lax.axis_size("dp"), lax.axis_size("bn")
    grid, cin = cotangent.shape[1], images.shape[3]
    width, half = merge_weight.shape[0], split_main.shape[1]
    share = cin // n_dp
    dims = (grid, cin, width, half, n_dp, n_bn)
    ws = stem_weight.transpose(1, 2, 0, 3).reshape(9 * cin, width)
    w2 = block_spatial.transpose(1, 2, 0, 3).reshape(9 * half, half)
    aff = affines.reshape(-1, LANES, 2).transpose(0, 2, 1).reshape(-1, LANES)
    act, igrad, stem, spatial, merge, transit, reduce, split, sums, *unused = fused(
        dims, image_count, image_size, images[0], cotangent[0], ws, split_main, split_side,
        block_reduce, w2, block_transit, merge_weight, aff)
    mine = affines.shape[0] // n_dp
    act, igrad, stem, spatial, grad_merge, grad_transit, grad_reduce, grad_main, grad_side, affine = finish(
        sums, mine // LANES, [act, igrad, stem, spatial, merge, transit, reduce, split], [(k, None) for k in range(7)] + [(7, 0), (7, 1)])
    activations = act.reshape(1, grid, grid, width)
    image_grad = igrad.reshape(1, 2 * grid, 2 * grid, cin)
    grad_stem = stem.reshape(3, 3, share, width).transpose(2, 0, 1, 3)
    grad_spatial = spatial.reshape(3, 3, share, half).transpose(2, 0, 1, 3)
    if mine % LANES == 0:
        affine_grad = affine.transpose(0, 2, 1).reshape(mine, 2)
    else:
        whole = sums.reshape(-1, 2, LANES).transpose(0, 2, 1).reshape(-1, 2)
        affine_grad = lax.dynamic_slice_in_dim(whole, lax.axis_index("dp") * mine, mine, axis=0)
    return (activations, image_grad, grad_stem, grad_main, grad_side, grad_reduce, grad_spatial, grad_transit, grad_merge, affine_grad)


def solution(mesh):
    rows = P(("dp", "bn"), None, None, None)
    return jax.shard_map(
        local,
        mesh=mesh,
        in_specs=(rows, P(("dp", "bn")), P(("dp", "bn")), rows) + (P(),) * 8,
        out_specs=(
            rows, rows, P("dp", None, None, None), P("dp", None), P("dp", None), P("dp", None),
            P("dp", None, None, None), P("dp", None), P("dp", None), P("dp", None),
        ),
        check_vma=False,
    )
```

```python
import functools

import jax
import jax.numpy as jnp
from jax import lax
from jax.experimental import pallas as pl
from jax.experimental.pallas import tpu as pltpu
from jax.sharding import PartitionSpec as P

EPS = 1e-05
F32 = jnp.float32
BF16 = jnp.bfloat16
MESH = pl.DeviceIdType.MESH
LEAD = 32
LANES = 128
TAPS = 9
UNITS = ["S%d" % k for k in range(5)] + ["T%d%d" % (k, h) for h in range(2) for k in range(5)] + ["B%d" % k for k in range(6)]
ORDERS = {}
for order, names in (
    ("1xy2", ["B0"]),
    ("xy21", ["B1", "B5"]),
    ("x1y2", ["B2"]),
    ("y12x", ["B3"]),
    ("yx21", ["B4"]),
    ("x12", ["S0", "S1", "S3"]),
    ("12x", ["S2"]),
    ("1x2", ["S4"]),
    ("yx2", ["T00", "T11", "T21", "T30", "T31", "T41"]),
    ("xy2", ["T01", "T20", "T40"]),
    ("y2x", ["T10"]),
):
    for name in names:
        ORDERS[name] = order
TOKENS = [
    "sync0", "sync1", "sync2", "sync3", "sync4", "sync5", "B0", "sync6", "B0", "B1", "sync7", "B1", "end", "B2",
    "B3", "B5", "B0", "B5", "B4", "B1", "B4", "B3", "B2", "FW", "PS", "B0", "S3", "PT", "I", "P0", "T10", "B4",
    "T40", "B1", "I", "T00", "B3", "S1", "B0", "T30", "B2", "I", "I", "B5", "I", "B1", "B4", "B3", "I", "S3",
    "T20", "P1", "T00", "T10", "T01", "B0", "T11", "T41", "S2", "B3", "B5", "S3", "T10", "T40", "T21", "B4", "I",
    "T30", "B1", "B2", "S1", "T41", "T00", "T11", "S2", "T31", "S4", "B4", "T01", "T21", "T30", "B2", "B3", "T41",
    "S0", "B5", "T31", "T11", "B3", "T40", "S2", "S4", "T20", "S1", "T21", "S3", "T31", "T41", "B2", "B0", "T11",
    "T00", "B5", "S1", "S0", "T01", "S4", "S2", "T31", "T10", "B1", "B4", "T20", "T30", "T00", "I", "S1", "T21",
    "T01", "S0", "I", "T11", "T40", "B0", "S3", "B5", "S4", "T10", "T20", "S0", "S2", "B3", "T01", "B2", "T41",
    "T40", "T01", "T21", "S2", "T30", "T20", "T31", "S4", "S0", "S3", "T11", "T40", "T20", "B4", "T31", "T30",
    "T21", "T10", "T41", "S0", "T00", "S4", "B2", "B1", "S1", "B5"
]


def mish_parts(value):
    t = jnp.exp(-jnp.abs(value))
    positive = value >= 0
    t2 = t * t
    top = jnp.where(positive, 1.0 + 2.0 * t, t2 + 2.0 * t)
    inv = 1.0 / (top + jnp.where(positive, 2.0 * t2, 2.0))
    gate = top * inv
    slope = jnp.where(positive, t2, t) * (1.0 + t) * (4.0 * inv * inv)
    return value * gate, gate + value * slope


def dot(left, right):
    return jnp.dot(left, right, preferred_element_type=F32)


def dot_t(left, right):
    return lax.dot_general(left, right, (((1,), (1,)), ((), ())), preferred_element_type=F32)


def lane_tile(j, size=LANES):
    if isinstance(j, int):
        return pl.ds(j * size, size)
    return pl.ds(pl.multiple_of(j * size, size), size)


def share_place(share, bits):
    place = 0
    for bit in bits:
        place = 2 * place + (share >> bit) % 2
    return place


def rest_bits(n_dp):
    return list(range(n_dp.bit_length() - 2, 1, -1))


def flip(index, bit):
    low = lax.rem(index // (1 << bit), 2)
    return index + (1 - 2 * low) * (1 << bit), low


class Unit:
    def __init__(self, name, dims):
        grid, cin, width, half, n_dp, n_bn = dims
        self.name, self.kind = name, name[0]
        order = ORDERS.get(name, {"S": "1x2", "T": "yx2", "B": "xy12"}[self.kind])
        self.steps = []
        for letter in order:
            self.steps += {"x": ["x"], "y": [0], "1": [1], "2": rest_bits(n_dp)}[letter]
        self.bits = [step for step in self.steps if step != "x"]
        narrow = name in ("S4", "T40", "T41", "B2", "B3")
        rows, cols = (cin if self.kind == "B" else cin // 2), (width // 4 if narrow else width // 2)
        self.start = (rows, cols)
        self.pool = self.kind + ("n" if narrow and self.kind == "B" else "")
        self.shapes = [(rows, cols)] if self.kind == "B" else []
        for step in self.steps:
            rows, cols = (rows, cols // 2) if step == "x" else (rows // 2, cols)
            self.shapes.append((rows, cols))
        self.final = (rows, cols)
        self.n_moves = len(self.shapes)
        self.n_stages = self.n_moves + 3


def plan(dims):
    units = {name: Unit(name, dims) for name in UNITS}
    shapes, finals, message = {}, {}, 0
    for unit in units.values():
        unit.at = []
        for shape in unit.shapes:
            unit.at.append((shape, shapes.get(shape, 0)))
            shapes[shape] = shapes.get(shape, 0) + 1
        unit.across = (unit.final, finals.get(unit.final, 0))
        finals[unit.final] = finals.get(unit.final, 0) + 1
        unit.message = message
        message += unit.n_moves + 5
    fills, now = {k: [] for k in range(9)}, 8
    for token in TOKENS or ["B%d" % k for k in range(6) for unused in range(2)] + ["FW", "PS", "PT", "P0", "P1"]:
        if token[:4] == "sync":
            now = int(token[4:])
        elif token == "end":
            now = 8
        else:
            fills[now].append(token)
    stage = {name: sum(fill.count(name) for fill in fills.values()) for name in UNITS}
    while any(stage[name] < units[name].n_stages for name in UNITS):
        for name in UNITS:
            if stage[name] < units[name].n_stages:
                fills[8].append(name)
                stage[name] += 1
    kinds = ("S", "T", "B", "Bn")
    seen, count, free = {}, {kind: 0 for kind in kinds}, {kind: [] for kind in kinds}
    for k in range(9):
        for token in fills[k]:
            if token in units:
                unit = units[token]
                n = seen.get(token, 0)
                seen[token] = n + 1
                if n == 0:
                    if not free[unit.pool]:
                        free[unit.pool].append(count[unit.pool])
                        count[unit.pool] += 1
                    unit.slot = free[unit.pool].pop(0)
                elif n == 1:
                    free[unit.pool].append(unit.slot)
    return units, shapes, finals, message, fills, count


def fused_kernel(
    dims,
    count_ref, size_ref, images_hbm, cot_hbm, ws_hbm, wm_hbm, wsd_hbm, wr_hbm, w2_hbm, wt_hbm, wmg_hbm, aff_ref,
    act_hbm, igrad_hbm, out_stem, out_spatial, out_merge, out_transit, out_reduce, out_split, total_ref,
    eo_hbm, ex_hbm, ec_hbm, ao_hbm, ax_hbm, ac_hbm, g2_hbm, g0_hbm,
    landed, across_land, own_g, own_g2, mask, stat, msg, heard, sums_ref, sums_in,
    wsem, ssem, rsem, local_sem, give_sem, take_sem, m_send, m_recv, keep_sem, s_send, s_recv,
):
    grid, cin, width, half, n_dp, n_bn = dims
    units, shapes, finals, n_messages, fills, pool = plan(dims)
    shape_list, final_list = list(shapes), list(finals)
    pitch = grid + 1
    rows = own_g.shape[0] - LEAD
    blocks = rows // LANES
    share = cin // n_dp
    part = cin // 2
    quarter = width // 4
    half2 = half // 2
    n_bits = n_dp.bit_length() - 1
    wide_tiles, half_tiles = width // LANES, half // LANES
    t0, t1, t2, t3 = 0, wide_tiles, wide_tiles + half_tiles, wide_tiles + 2 * half_tiles

    dp, bn = lax.axis_index("dp"), lax.axis_index("bn")
    others = [(dp, lax.rem(bn + k, n_bn)) for k in range(1, n_bn)]
    sib, core = flip(bn, 0)
    over, cross = flip(bn, 1)
    bit_of = [flip(dp, b) for b in range(n_bits)]
    sibling, across = (dp, sib), (dp, over)
    along = [(bit_of[b][0], bn) for b in range(n_bits)]
    next_sib, pair_sib = (bit_of[0][0], sib), (bit_of[1][0], sib)
    partners = others + along + [next_sib, pair_sib]

    def remote(src, dst, send, recv, target):
        return pltpu.make_async_remote_copy(
            src_ref=src, dst_ref=dst, send_sem=send, recv_sem=recv, device_id=target, device_id_type=MESH)

    def part_of(which, size):
        return pl.ds(pl.multiple_of(which * size, size), size)

    barrier = pltpu.get_barrier_semaphore()
    for target in partners:
        pl.semaphore_signal(barrier, inc=1, device_id=target, device_id_type=MESH)

    places = lax.broadcasted_iota(jnp.int32, (rows, LANES), 0)
    row = (places * 3277) >> 16 if pitch == 20 else places // pitch
    col = places - row * pitch
    size = jnp.where(count_ref[0] > 0, size_ref[0], 0)
    mask[...] = jnp.where((row < size) & (col < size), 1.0, 0.0).astype(F32)
    own_g[rows:, :] = jnp.zeros((LEAD, width), F32)

    norms = ((0, t0, wide_tiles), (1, t1, half_tiles), (2, t2, half_tiles), (3, t3, wide_tiles))

    def put_sums(sync, j, first, second, tiles):
        msg[sync, pl.ds(j, 1), :] = first
        msg[sync, pl.ds(tiles + j, 1), :] = second

    def column_sums(sync, z, j, tiles):
        zm = z * mask[...]
        put_sums(sync, j, jnp.sum(zm, axis=0, keepdims=True), jnp.sum(zm * z, axis=0, keepdims=True), tiles)

    def matmul_stats(sync, left, weight, out, cols, ready=lambda n: None):
        def body(n, _):
            ready(n)
            z = dot(left[...], weight[:, lane_tile(n, 256)])
            out[:, lane_tile(n, 256)] = z
            for h in range(2):
                column_sums(sync, z[:, h * LANES : (h + 1) * LANES], 2 * n + h, cols // LANES)
            return 0
        lax.fori_loop(0, cols // 256, body, 0)

    lines = [pl.ds(0, n) for n in (
        2 * wide_tiles + 8, 2 * half_tiles, 2 * half_tiles, 2 * wide_tiles, 2 * wide_tiles, 2 * half_tiles, 2 * half_tiles, 2 * wide_tiles)]

    def greet(sync):
        return [
            remote(msg.at[sync, lines[sync]], heard.at[sync, bn, lines[sync]], ssem.at[sync, k], rsem.at[sync, k], target)
            for k, target in enumerate(others)]

    def send(sync):
        heard[sync, bn, lines[sync], :] = msg[sync, lines[sync], :]
        for copy in greet(sync):
            copy.start()

    def receive(sync):
        for copy in greet(sync):
            copy.wait()
        total = heard[sync, 0, lines[sync], :]
        for k in range(1, n_bn):
            total = total + heard[sync, k, lines[sync], :]
        return total

    def set_stat(slot, total, count, first_tile, tiles):
        mean = total[0:tiles] / count
        spread = total[tiles : 2 * tiles] / count - mean * mean
        stat[slot, 0, 0:tiles, :] = mean
        stat[slot, 1, 0:tiles, :] = lax.rsqrt(spread + EPS)

    def set_affine(slot, first_tile, tiles):
        for j in range(tiles):
            stat[slot, 2, j : j + 1, :] = aff_ref[2 * (first_tile + j) : 2 * (first_tile + j) + 1, :]
            stat[slot, 3, j : j + 1, :] = aff_ref[2 * (first_tile + j) + 1 : 2 * (first_tile + j) + 2, :]

    def per_tile(tiles, body):
        def step(j, _):
            body(j, lane_tile(j))
            return 0
        lax.fori_loop(0, tiles, step, 0)

    def normed(slot, z, j, cs, r):
        scaled = (z[r, cs] - stat[slot, 0, pl.ds(j, 1), :]) * stat[slot, 1, pl.ds(j, 1), :]
        return scaled, scaled * stat[slot, 2, pl.ds(j, 1), :] + stat[slot, 3, pl.ds(j, 1), :]

    def forward(slot, z, keep, tiles, put):
        def body(j, cs):
            for b in range(blocks):
                r = pl.ds(b * LANES, LANES)
                unused, before = normed(slot, z, j, cs, r)
                act, slope = mish_parts(before)
                keep[r, cs] = slope * mask[r, :]
                put(r, cs, act * mask[r, :])
        per_tile(tiles, body)

    def backward_sums(sync, slot, z, inner_ref, j, cs, upstream, tiles):
        first = jnp.zeros((1, LANES), F32)
        second = jnp.zeros((1, LANES), F32)
        for b in range(blocks):
            r = pl.ds(b * LANES, LANES)
            inner = inner_ref[r, cs] * upstream[r, cs]
            inner_ref[r, cs] = inner
            scaled = (z[r, cs] - stat[slot, 0, pl.ds(j, 1), :]) * stat[slot, 1, pl.ds(j, 1), :]
            first = first + jnp.sum(inner, axis=0, keepdims=True)
            second = second + jnp.sum(inner * scaled, axis=0, keepdims=True)
        put_sums(sync, j, first, second, tiles)

    def set_back(slot, total, count, first_tile, tiles):
        stat[slot, 4, 0:tiles, :] = total[0:tiles] / count
        stat[slot, 5, 0:tiles, :] = total[tiles : 2 * tiles] / count
        stat[slot, 6, 0:tiles, :] = total[tiles : 2 * tiles]
        stat[slot, 7, 0:tiles, :] = total[0:tiles]

    def put_affine(slot, first_tile, tiles):
        for j in range(tiles):
            for c in range(2):
                at = 2 * (first_tile + j) + c
                sums_ref[at : at + 1, :] = stat[slot, 6 + c, j : j + 1, :]

    def backward(slot, z, inner_ref, tiles, put):
        def body(j, cs):
            for b in range(blocks):
                r = pl.ds(b * LANES, LANES)
                inv = stat[slot, 1, pl.ds(j, 1), :]
                scaled = (z[r, cs] - stat[slot, 0, pl.ds(j, 1), :]) * inv
                pull = mask[r, :] * (stat[slot, 4, pl.ds(j, 1), :] + scaled * stat[slot, 5, pl.ds(j, 1), :])
                value = (inner_ref[r, cs] - pull) * (inv * stat[slot, 2, pl.ds(j, 1), :])
                put(r, cs, value.astype(BF16))
        per_tile(tiles, body)

    local = {}
    stage = {name: 0 for name in units}

    def landing(unit, k):
        shape, n = unit.at[k]
        return landed[shape_list.index(shape)].at[n]

    def source(unit, k):
        return local[unit.pool](unit.slot) if k == 0 else landing(unit, k - 1)

    def move_of(unit, k):
        size_r, size_c = unit.shapes[k]
        step = "c" if unit.kind == "B" and k == 0 else unit.steps[k - (unit.kind == "B")]
        if step == "c":
            return sibling, (pl.ds(0, size_r), part_of(1 - core, size_c)), (None, part_of(core, size_c))
        if step == "x":
            return across, (pl.ds(0, size_r), part_of(1 - cross, size_c)), (None, part_of(cross, size_c))
        bit = bit_of[step][1]
        return along[step], (part_of(1 - bit, size_r), pl.ds(0, size_c)), (bit, pl.ds(0, size_c))

    def move(unit, k):
        target, gone, unused = move_of(unit, k)
        m = unit.message + k
        return remote(source(unit, k).at[gone[0], gone[1]], landing(unit, k), m_send.at[m], m_recv.at[m], target)

    def add_own(unit, k):
        unused, unused2, (bit, columns) = move_of(unit, k)
        size = unit.shapes[k][0]
        src, dst = source(unit, k), landing(unit, k)
        n = min(size, 64)

        def body(i, _):
            r = pl.ds(pl.multiple_of(i * n, n), n)
            own = r if bit is None else pl.ds(pl.multiple_of(bit * size + i * n, 8), n)
            dst[r, :] = dst[r, :] + src[own, columns]
            return 0
        lax.fori_loop(0, size // n, body, 0)

    def pieces(unit, cross_at):
        k = int(unit.name[1])
        at = 2 * core + cross_at
        taps_of = range(2 * k, min(2 * k + 2, TAPS))
        if unit.kind == "T":
            col = part_of(4 * core + 2 * int(unit.name[2]) + cross_at, LANES)
            return [(out_stem.at[t, :, col], (t - 2 * k) * LANES) for t in taps_of]
        if unit.kind == "S":
            return [(out_spatial.at[t, :, part_of(at, half // 4)], (t - 2 * k) * (half // 4)) for t in taps_of]
        if k < 2:
            return [(out_merge.at[pl.ds(k * share, share), part_of(at, quarter)], 0)]
        if k < 4:
            return [((out_transit if k == 2 else out_reduce).at[:, part_of(at, half // 4)], 0)]
        return [(out_split.at[core, pl.ds((k - 4) * share, share), part_of(cross_at, half2)], 0)]

    def arrival(unit):
        shape, n = unit.across
        return across_land[final_list.index(shape)].at[n]

    def give_across(unit):
        m = unit.message + unit.n_moves
        return remote(landing(unit, unit.n_moves - 1), arrival(unit), m_send.at[m], m_recv.at[m], across)

    def spread_piece(unit, mine):
        block = landing(unit, unit.n_moves - 1) if mine else arrival(unit)
        m = unit.message + unit.n_moves + (1 if mine else 3)
        copies = []
        for n, (place, first) in enumerate(pieces(unit, cross if mine else 1 - cross)):
            src = block.at[:, pl.ds(first, place.shape[-1])]
            copies.append(pltpu.make_async_copy(src, place, keep_sem.at[m + n]))
            copies.append(remote(src, place, m_send.at[m + n], m_recv.at[m + n], sibling))
        return copies

    def advance(name, compute):
        unit = units[name]
        k = stage[name]
        stage[name] = k + 1
        if k == 0:
            compute(unit)
            move(unit, 0).start()
        elif k <= unit.n_moves:
            move(unit, k - 1).wait()
            add_own(unit, k - 1)
            if k < unit.n_moves:
                move(unit, k).start()
            else:
                give_across(unit).start()
                for copy in spread_piece(unit, True):
                    copy.start()
        elif k == unit.n_moves + 1:
            give_across(unit).wait()
            for copy in spread_piece(unit, False):
                copy.start()
        else:
            for copy in spread_piece(unit, True) + spread_piece(unit, False):
                copy.wait()

    next_bit, pair_bit = bit_of[0][1], bit_of[1][1]
    next_bits, pair_bits = [0, 1] + rest_bits(n_dp), [1, 0] + rest_bits(n_dp)

    def field_gives(src, dst, which_of, size, first, targets):
        return [
            remote(src.at[pl.ds(0, rows), part_of(which_of(which), size)], dst.at[k], give_sem.at[first + k], take_sem.at[first + k], target)
            for k, (target, which) in enumerate(targets)]
    gives2 = field_gives(own_g2, g2_hbm, lambda w: w, half2, 0, ((sibling, 1 - core), (along[0], core), (next_sib, 1 - core)))
    gives0 = [
        field_gives(own_g, g0_hbm.at[h], lambda w, h=h: 2 * w + h, quarter, 3 + 3 * h,
                    ((sibling, 1 - core), (along[1], core), (pair_sib, 1 - core)))
        for h in range(2)]

    forwards = [
        remote(ax_hbm, ac_hbm.at[1], give_sem.at[14], take_sem.at[14], sibling),
        remote(ex_hbm, ec_hbm.at[1], give_sem.at[15], take_sem.at[15], sibling)]

    def turned_block(block, k, dst, bits, parts=1):
        for piece in range(LANES // share):
            at_row = k * LANES + piece * share
            s, h = (at_row // share) // parts, (at_row // share) % parts
            at = share_place(s, bits[h]) * share
            dst(h, pl.ds(at, share), block[piece * share : (piece + 1) * share])

    def chain_phase(wms, wr, w2, wt, wmg, taps, z0, d0, stem_low, et):
        smalls = [
            pltpu.make_async_copy(src, dst, wsem.at[2 + k])
            for k, (src, dst) in enumerate(
                [(wm_hbm, wms.at[:, pl.ds(0, half)]), (wsd_hbm, wms.at[:, pl.ds(half, half)]),
                 (wr_hbm, wr), (w2_hbm, w2), (wt_hbm, wt), (wmg_hbm, wmg)])
        ]

        def first_phase(ws, images, phases, img_row):
            load_i = pltpu.make_async_copy(images_hbm, images, wsem.at[0])

            def load_w(n):
                block = lane_tile(n, 256)
                return pltpu.make_async_copy(ws_hbm.at[:, block], ws.at[:, block], wsem.at[8 + n])
            load_i.start()
            for n in range(width // 256):
                load_w(n).start()
            for p in range(4):
                phases[p, 0:LEAD, :] = jnp.zeros((LEAD, cin), F32)
                tail = LEAD + pitch * grid
                phases[p, tail:, :] = jnp.zeros((phases.shape[1] - tail, cin), F32)
            for norm in norms:
                set_affine(*norm)
            load_i.wait()
            for line in range(2 * grid):
                slot = line % 2
                value = images[line].astype(F32)
                for k in range(cin // LANES):
                    img_row[slot, k, 0 : 2 * grid, :] = value[:, k * LANES : (k + 1) * LANES]
                start = LEAD + pitch * (line // 2)
                for odd in range(2):
                    p = 2 * (line % 2) + odd
                    for k in range(cin // LANES):
                        phases[p, start : start + grid, k * LANES : (k + 1) * LANES] = img_row[slot, k, pl.ds(odd, grid, stride=2), :]
                    phases[p, start + grid : start + grid + 1, :] = jnp.zeros((1, cin), F32)
            for k in range(TAPS):
                a, b = k // 3, k % 3
                p = 2 * (a != 1) + (b != 1)
                off = LEAD - pitch * (a == 0) - (b == 0)
                taps[:, k * cin : (k + 1) * cin] = phases[p, off : off + rows, :].astype(BF16)
            for load in smalls:
                load.start()
            matmul_stats(0, taps, ws, z0, width, lambda n: load_w(n).wait())
            msg[0, 2 * wide_tiles : 2 * wide_tiles + 8, :] = jnp.zeros((8, LANES), F32) + jnp.sum(mask[...], axis=0, keepdims=True)
            pl.semaphore_wait(barrier, len(partners))
            send(0)

            def turn_phase(p, _):
                for k in range(cin // LANES):
                    block = phases[p, LEAD : LEAD + rows, k * LANES : (k + 1) * LANES].T

                    def put(h, r, value):
                        et[p, r, :] = value
                    turned_block(block, k, put, [pair_bits])
                return 0
            lax.fori_loop(0, 4, turn_phase, 0)

        pl.run_scoped(
            first_phase, pltpu.VMEM((TAPS * cin, width), BF16), pltpu.VMEM((2 * grid, 2 * grid, cin), BF16),
            pltpu.VMEM((4, LEAD + rows, cin), F32), pltpu.VMEM((2, cin // LANES, -(-2 * grid // 8) * 8, LANES), F32))
        keep_e = pltpu.make_async_copy(et.at[0:4, part_of(pair_bit, part), :], eo_hbm, local_sem.at[0])
        give_e = remote(et.at[0:4, part_of(1 - pair_bit, part), :], ex_hbm, give_sem.at[9], take_sem.at[9], along[1])
        keep_e.start()
        give_e.start()
        own_e = [
            remote(et.at[pl.ds(2 * h, 2), part_of(pair_bit, part), :], ec_hbm.at[0, pl.ds(2 * h, 2)],
                   give_sem.at[11 + h], take_sem.at[11 + h], sibling)
            for h in range(2)]

        def rest_phase(
            z1, d1, z2, d2, wide, narrow, main_path, apad, gpad, back, joined, main_low, res_low, mside, turned, act, cot_in, tile,
        ):
            z3 = own_g.at[pl.ds(0, rows)]
            i3, cot = wide.at[0, pl.ds(0, rows)], wide.at[1, pl.ds(0, rows)]
            merge_in, tside, red_in = stem_low, joined, main_low
            local["B"] = lambda slot: wide.at[slot]
            local["Bn"] = lambda slot: narrow.at[slot]
            load_cot = pltpu.make_async_copy(cot_hbm, cot_in, local_sem.at[1])
            load_cot.start()
            for ref in (apad, gpad):
                ref[0:LEAD, :] = jnp.zeros((LEAD, half), F32)
                ref[LEAD + rows :, :] = jnp.zeros((LEAD, half), F32)

            def turn(src, first, parts):
                for k in range(parts * half // LANES):
                    block = src[:, k * LANES : (k + 1) * LANES].astype(F32).T

                    def put(h, r, value):
                        turned[first + h, r, :] = value.astype(BF16)
                    turned_block(block, k, put, [units["B%d" % (first + h)].bits for h in range(parts)], parts)

            def compute(unit):
                k = int(unit.name[1])
                right = [merge_in, merge_in, tside, red_in, mside, mside][k]
                dst = local[unit.pool](unit.slot)
                for n in range(2 * unit.start[1] // 256):
                    dst[:, pl.ds(n * 256, 256)] = dot(turned[k], right[:, pl.ds(n * 256, 256)])

            def fill(sync):
                for token in fills[sync]:
                    advance(token, compute)

            total = receive(0)
            count = total[2 * wide_tiles : 2 * wide_tiles + 1, 0:1]
            set_stat(0, total, count, t0, wide_tiles)

            def put_stem(r, cs, value):
                stem_low[r, cs] = value.astype(BF16)
            forward(0, z0, d0, wide_tiles, put_stem)
            smalls[0].wait()
            smalls[1].wait()
            for n in range(half // 256):
                y = dot(stem_low[...], wms[:, lane_tile(n, 256)])
                main_path[:, lane_tile(n, 256)] = y
                main_low[:, lane_tile(n, 256)] = y.astype(BF16)
            smalls[2].wait()
            matmul_stats(1, main_low, wr, z1, half)
            send(1)
            own_e[0].start()
            for n in range(half // 256):
                y = dot(stem_low[...], wms[:, lane_tile(half // 256 + n, 256)])
                joined[:, lane_tile(half // 256 + n, 256)] = y.astype(BF16)
            turn(stem_low, 4, 2)
            set_stat(1, receive(1), count, t1, half_tiles)

            def put_reduce(r, cs, value):
                apad[pl.ds(LEAD + r.start, r.size), cs] = value.astype(BF16).astype(F32)
            forward(1, z1, d1, half_tiles, put_reduce)
            for k in range(TAPS):
                off = LEAD + pitch * (k // 3 - 1) + k % 3 - 1
                taps[:, k * half : (k + 1) * half] = apad[off : off + rows, :].astype(BF16)
            smalls[3].wait()
            matmul_stats(2, taps, w2, z2, half)
            send(2)
            own_e[1].start()
            for k in range(half // LANES):
                def put_a(h, r, value):
                    et[4, r, :] = value
                turned_block(apad[LEAD : LEAD + rows, k * LANES : (k + 1) * LANES].T, k, put_a, [next_bits])
            keep_a = pltpu.make_async_copy(et.at[4, part_of(next_bit, part), :], ao_hbm, local_sem.at[2])
            give_a = remote(et.at[4, part_of(1 - next_bit, part), :], ax_hbm, give_sem.at[10], take_sem.at[10], along[0])
            own_a = remote(et.at[4, part_of(next_bit, part), :], ac_hbm.at[0], give_sem.at[13], take_sem.at[13], sibling)
            keep_a.start()
            give_a.start()
            turn(main_low, 3, 1)
            load_cot.wait()
            for r in range(grid):
                cot[r * pitch : r * pitch + grid, :] = cot_in[r].astype(F32)
                cot[r * pitch + grid : (r + 1) * pitch, :] = jnp.zeros((1, width), F32)
            cot[grid * pitch :, :] = jnp.zeros((rows - grid * pitch, width), F32)
            set_stat(2, receive(2), count, t2, half_tiles)

            def put_spatial(r, cs, value):
                res_low[r, cs] = (main_path[r, cs] + value).astype(BF16)
            forward(2, z2, d2, half_tiles, put_spatial)
            smalls[4].wait()
            for n in range(half // 256):
                joined[:, lane_tile(n, 256)] = dot(res_low[...], wt[:, lane_tile(n, 256)]).astype(BF16)
            smalls[5].wait()
            matmul_stats(3, joined, wmg, z3, width)
            send(3)
            own_a.start()
            turn(joined, 0, 2)
            set_stat(3, receive(3), count, t3, wide_tiles)

            def merge_tile(j, cs):
                for b in range(blocks):
                    r = pl.ds(b * LANES, LANES)
                    unused, before = normed(3, z3, j, cs, r)
                    value, slope = mish_parts(before)
                    tile[r, :] = value * mask[r, :]
                    i3[r, cs] = slope * mask[r, :]
                backward_sums(4, 3, z3, i3, j, cs, cot, wide_tiles)
                cot[:, cs] = tile[...]
            per_tile(wide_tiles, merge_tile)
            send(4)

            def act_tile(j, cs):
                for line in range(grid):
                    act[pl.ds(line * grid * wide_tiles + j, grid, stride=wide_tiles), :] = cot[line * pitch : line * pitch + grid, cs]
            per_tile(wide_tiles, act_tile)
            store_act = pltpu.make_async_copy(act, act_hbm, local_sem.at[3])
            store_act.start()
            turn(res_low, 2, 1)
            fill(4)
            set_back(3, receive(4), count, t3, wide_tiles)

            def put_merge(r, cs, value):
                merge_in[r, cs] = value
            backward(3, z3, i3, wide_tiles, put_merge)
            for n in range(width // 256):
                tside[:, lane_tile(n, 256)] = dot_t(merge_in[...], wmg[lane_tile(n, 256), :]).astype(BF16)
            for n in range(half // 256):
                back[:, lane_tile(n, 256)] = dot_t(tside[:, 0:half], wt[lane_tile(n, 256), :])

            def spatial_tile(j, cs):
                backward_sums(5, 2, z2, d2, j, cs, back, half_tiles)
            per_tile(half_tiles, spatial_tile)
            send(5)
            fill(5)
            set_back(2, receive(5), count, t2, half_tiles)

            def put_spatial_in(r, cs, value):
                gpad[pl.ds(LEAD + r.start, r.size), cs] = value.astype(F32)
                own_g2[r, cs] = value.astype(F32)
            backward(2, z2, d2, half_tiles, put_spatial_in)
            for give in gives2:
                give.start()
            for k in range(TAPS):
                off = LEAD - pitch * (k // 3 - 1) - (k % 3 - 1)
                taps[:, k * half : (k + 1) * half] = gpad[off : off + rows, :].astype(BF16)

            def reduce_columns(n, _):
                value = jnp.zeros((rows, 256), F32)
                for k in range(TAPS):
                    value = value + dot_t(taps[:, k * half : (k + 1) * half], w2[pl.ds(pl.multiple_of(k * half + n * 256, 256), 256), :])
                main_path[:, lane_tile(n, 256)] = value
                return 0
            lax.fori_loop(0, half // 256, reduce_columns, 0)

            def reduce_tile(j, cs):
                backward_sums(6, 1, z1, d1, j, cs, main_path, half_tiles)
            per_tile(half_tiles, reduce_tile)
            send(6)
            mside[:, half : 2 * half] = tside[:, half : 2 * half]
            fill(6)
            set_back(1, receive(6), count, t1, half_tiles)

            def put_reduce_in(r, cs, value):
                red_in[r, cs] = value
            backward(1, z1, d1, half_tiles, put_reduce_in)
            for n in range(half // 256):
                mside[:, lane_tile(n, 256)] = (back[:, lane_tile(n, 256)] + dot_t(red_in[...], wr[lane_tile(n, 256), :])).astype(BF16)

            def stem_columns(n, _):
                z3[:, lane_tile(n, 256)] = dot_t(mside[...], wms[lane_tile(n, 256), :])
                return 0
            lax.fori_loop(0, width // 256, stem_columns, 0)

            def stem_tile(j, cs):
                backward_sums(7, 0, z0, d0, j, cs, z3, wide_tiles)
            per_tile(wide_tiles, stem_tile)
            send(7)
            fill(7)
            set_back(0, receive(7), count, t0, wide_tiles)

            def put_stem_in(r, cs, value):
                own_g[r, cs] = value.astype(F32)
            backward(0, z0, d0, wide_tiles, put_stem_in)
            for gives in gives0:
                for give in gives:
                    give.start()
            while any(units[name].kind == "B" and stage[name] < 2 for name in units) or "FW" in fills[8]:
                token = fills[8].pop(0)
                if token == "FW":
                    give_e.wait()
                    give_a.wait()
                    for forward_copy in forwards:
                        forward_copy.start()
                else:
                    advance(token, compute)
            for norm in norms:
                put_affine(*norm)
            for copy in own_e + [own_a, keep_e, keep_a, store_act]:
                copy.wait()

        pl.run_scoped(
            rest_phase,
            pltpu.VMEM((rows, half), F32), pltpu.VMEM((rows, half), F32), pltpu.VMEM((rows, half), F32), pltpu.VMEM((rows, half), F32),
            pltpu.VMEM((max(2, pool["B"]), cin, width), F32), pltpu.VMEM((pool["Bn"], cin, half), F32),
            pltpu.VMEM((rows, half), F32), pltpu.VMEM((LEAD + rows + LEAD, half), F32), pltpu.VMEM((LEAD + rows + LEAD, half), F32),
            pltpu.VMEM((rows, half), F32), pltpu.VMEM((rows, 2 * half), BF16), pltpu.VMEM((rows, half), BF16),
            pltpu.VMEM((rows, half), BF16), pltpu.VMEM((rows, 2 * half), BF16), pltpu.VMEM((6, cin, rows), BF16),
            pltpu.VMEM((grid * grid * wide_tiles, LANES), F32), pltpu.VMEM((grid, grid, width), BF16), pltpu.VMEM((rows, LANES), F32))

    pl.run_scoped(
        chain_phase,
        pltpu.VMEM((width, 2 * half), BF16), pltpu.VMEM((half, half), BF16), pltpu.VMEM((TAPS * half, half), BF16),
        pltpu.VMEM((half, half), BF16), pltpu.VMEM((width, width), BF16), pltpu.VMEM((rows, TAPS * cin), BF16),
        pltpu.VMEM((rows, width), F32), pltpu.VMEM((rows, width), F32), pltpu.VMEM((rows, width), BF16),
        pltpu.VMEM((5, cin, rows), F32))

    def last_phase(g2r, g0r, at_land, at_cat, spatial, et_land, et_cat, shifted, own_shift, image, weight, stem_blocks, igrad):
        local["S"] = lambda slot: spatial.at[slot]
        local["T"] = lambda slot: stem_blocks.at[slot]
        offsets = (0, 1, pitch, pitch + 1)
        image_taps = [4, 3, 5, 1, 7, 0, 2, 6, 8]
        done = []
        sums_done = []

        def load_weight(n):
            k = image_taps[n]
            return pltpu.make_async_copy(ws_hbm.at[pl.ds(k * cin, cin)], weight.at[n % 2], wsem.at[n % 2])
        load_weight(0).start()
        own_parts = [
            pltpu.make_async_copy(src, dst, local_sem.at[9 + k])
            for k, (src, dst) in enumerate(
                ((ao_hbm, at_land.at[0]), (ax_hbm, at_land.at[1]), (eo_hbm, et_land.at[0]), (ex_hbm, et_land.at[1])))]
        for load in own_parts:
            load.start()

        def sums_step(k):
            return remote(total_ref if k else sums_ref, sums_in.at[k], s_send.at[k], s_recv.at[k], along[k])

        def sums_next():
            k = len(sums_done)
            if k < n_bits:
                sums_done.append(k)
                sums_step(k).wait()
                total_ref[...] = (total_ref[...] if k else sums_ref[...]) + sums_in[k]
                if k + 1 < n_bits:
                    sums_step(k + 1).start()
        sums_step(0).start()
        for k in range(4):
            g2r[k, 0:LEAD, :] = jnp.zeros((LEAD, half2), F32)
            g2r[k, LEAD + rows :, :] = jnp.zeros((LEAD, half2), F32)
            for h in range(2):
                g0r[h, k, rows:, :] = jnp.zeros((LEAD, quarter), F32)

        def tap(k):
            a, b = k // 3, k % 3
            return 2 * (a != 1) + (b != 1), 2 * (a == 0) + (b == 0)

        def fetch(pairs, first):
            loads = [pltpu.make_async_copy(src, dst, local_sem.at[first + k]) for k, (src, dst) in enumerate(pairs)]
            for load in loads:
                load.start()
            for load in loads:
                load.wait()

        def compute(unit):
            k = int(unit.name[1])
            c = unit.start[1] // 2
            dst = local[unit.pool](unit.slot)
            for h in range(2):
                t = 2 * k + h
                if t == TAPS:
                    continue
                if unit.kind == "T":
                    p, sh = tap(t)
                    value = dot(et_cat[p], shifted[int(unit.name[2]), sh])
                else:
                    off = LEAD - pitch * (t // 3 - 1) - (t % 3 - 1)
                    right = jnp.concatenate([g2r[s, off : off + rows, :].astype(BF16) for s in range(4)], axis=0)
                    value = dot(at_cat[...], right)
                for x in range(2):
                    dst[:, c * x + LANES * h : c * x + LANES * (h + 1)] = value[:, LANES * x : LANES * (x + 1)]

        def image_step():
            n = len(done)
            k = image_taps[n]
            p, sh = tap(k)
            if n + 1 < TAPS:
                load_weight(n + 1).start()
            load_weight(n).wait()
            for m in range(cin // 256):
                c = slice(m * 256, (m + 1) * 256)
                value = dot_t(own_shift[sh], weight[n % 2, c, :])
                image[:, c] = value if k in (4, 3, 1, 0) else image[:, c] + value
            done.append(k)
            if k in (4, 5, 7, 8):
                for r in range(grid):
                    for m in range(cin // LANES):
                        start = ((2 * r + p // 2) * 2 * grid + p % 2) * (cin // LANES) + m
                        igrad[pl.ds(start, grid, stride=2 * cin // LANES), :] = image[r * pitch : r * pitch + grid, m * LANES : (m + 1) * LANES]
            if len(done) == TAPS:
                pltpu.make_async_copy(igrad, igrad_hbm, local_sem.at[8]).start()

        for token in fills[8]:
            if token == "PS":
                forwards[0].wait()
                own_parts[0].wait()
                own_parts[1].wait()
                for give in gives2:
                    give.wait()
                fetch([(ac_hbm.at[0], at_land.at[2]), (ac_hbm.at[1], at_land.at[3])]
                      + [(g2_hbm.at[s], g2r.at[s + 1, pl.ds(LEAD, rows)]) for s in range(3)]
                      + [(own_g2.at[:, part_of(core, half2)], g2r.at[0, pl.ds(LEAD, rows)])], 0)
                for slot, n in enumerate((0, 2, 1, 3)):
                    at_cat[:, slot * rows : (slot + 1) * rows] = at_land[n].astype(BF16)
                sums_next()
            elif token == "PT":
                forwards[1].wait()
                own_parts[2].wait()
                own_parts[3].wait()
                fetch([(ec_hbm.at[0], et_land.at[2]), (ec_hbm.at[1], et_land.at[3])], 0)
                for p in range(4):
                    for slot, n in enumerate((0, 2, 1, 3)):
                        et_cat[p, :, slot * rows : (slot + 1) * rows] = et_land[n, p].astype(BF16)
                for sh, off in enumerate(offsets):
                    own_shift[sh] = own_g[off : off + rows, :].astype(BF16)
                sums_next()
            elif token in ("P0", "P1"):
                h = int(token[1])
                for give in gives0[h]:
                    give.wait()
                fetch([(g0_hbm.at[h, s], g0r.at[h, s + 1, pl.ds(0, rows)]) for s in range(3)]
                      + [(own_g.at[pl.ds(0, rows), part_of(2 * core + h, quarter)], g0r.at[h, 0, pl.ds(0, rows)])], 0)
                for sh, off in enumerate(offsets):
                    for s in range(4):
                        shifted[h, sh, s * rows : (s + 1) * rows, :] = g0r[h, s, off : off + rows, :].astype(BF16)
                sums_next()
            elif token == "I":
                if len(done) < TAPS:
                    image_step()
            elif token in units:
                advance(token, compute)
        while len(done) < TAPS:
            image_step()
        for k in range(n_bits):
            sums_next()
        pltpu.make_async_copy(igrad, igrad_hbm, local_sem.at[8]).wait()

    pl.run_scoped(
        last_phase,
        pltpu.VMEM((4, LEAD + rows + LEAD, half2), F32), pltpu.VMEM((2, 4, rows + LEAD, quarter), F32),
        pltpu.VMEM((4, part, rows), F32), pltpu.VMEM((part, 4 * rows), BF16), pltpu.VMEM((pool["S"], part, width // 2), F32),
        pltpu.VMEM((4, 4, part, rows), F32), pltpu.VMEM((4, part, 4 * rows), BF16),
        pltpu.VMEM((2, 4, 4 * rows, quarter), BF16), pltpu.VMEM((4, rows, width), BF16), pltpu.VMEM((rows, cin), F32),
        pltpu.VMEM((2, cin, width), BF16), pltpu.VMEM((pool["T"], part, width // 2), F32),
        pltpu.VMEM((4 * grid * grid * (cin // LANES), LANES), F32))


def fused(dims, count, size, images, cot, ws, wm, wsd, wr, w2, wt, wmg, aff):
    grid, cin, width, half, n_dp, n_bn = dims
    units, shapes, finals, n_messages, fills, pool = plan(dims)
    rows = -(-grid * (grid + 1) // LANES) * LANES
    share, part = cin // n_dp, cin // 2
    tiles = width // LANES
    n_bits = n_dp.bit_length() - 1
    sd, dma = jax.ShapeDtypeStruct, pltpu.SemaphoreType.DMA
    vm, any_, sm = (pl.BlockSpec(memory_space=space) for space in (pltpu.VMEM, pl.ANY, pltpu.SMEM))
    out = (
        sd((grid * grid * tiles, LANES), F32), sd((4 * grid * grid * (cin // LANES), LANES), F32),
        sd((TAPS, share, width), F32), sd((TAPS, share, half), F32), sd((2 * share, width), F32),
        sd((share, half), F32), sd((share, half), F32), sd((2, 2 * share, half), F32), sd(aff.shape, F32),
        sd((4, part, rows), F32), sd((4, part, rows), F32), sd((2, 4, part, rows), F32),
        sd((part, rows), F32), sd((part, rows), F32), sd((2, part, rows), F32),
        sd((3, rows, half // 2), F32), sd((2, 3, rows, width // 4), F32),
    )
    scratch = [
        [pltpu.VMEM((n,) + shape, F32) for shape, n in shapes.items()],
        [pltpu.VMEM((n,) + shape, F32) for shape, n in finals.items()],
        pltpu.VMEM((rows + LEAD, width), F32), pltpu.VMEM((rows, half), F32),
        pltpu.VMEM((rows, LANES), F32), pltpu.VMEM((4, 8, 8, LANES), F32),
        pltpu.VMEM((8, 3 * tiles, LANES), F32), pltpu.VMEM((8, n_bn, 3 * tiles, LANES), F32),
        pltpu.VMEM(aff.shape, F32), pltpu.VMEM((n_bits,) + aff.shape, F32),
        dma((8 + width // 256,)), dma((8, n_bn - 1)), dma((8, n_bn - 1)), dma((16,)), dma((16,)), dma((16,)),
        dma((n_messages,)), dma((n_messages,)), dma((n_messages,)), dma((n_bits,)), dma((n_bits,)),
    ]
    return pl.pallas_call(
        functools.partial(fused_kernel, dims),
        out_shape=out,
        in_specs=[sm, sm] + [any_] * 9 + [vm],
        out_specs=(any_,) * 8 + (vm,) + (any_,) * 8,
        scratch_shapes=scratch,
        compiler_params=pltpu.CompilerParams(collective_id=0, has_side_effects=True, vmem_limit_bytes=64 * 2**20 - 65536),
        name="section",
    )(count, size, images, cot, ws, wm, wsd, wr, w2, wt, wmg, aff)


def finish_kernel(parts, n, tiles, sums_hbm, *refs):
    ins, outs, affine_hbm = refs[:n], refs[n : n + len(parts)], refs[n + len(parts)]
    held, (sums, affine, sem_a), sems = refs[n + len(parts) + 1 : n + 2 * len(parts) + 1], refs[-5:-2], refs[-2:]
    load_sums = pltpu.make_async_copy(sums_hbm, sums, sem_a.at[0])
    store_affine = pltpu.make_async_copy(affine, affine_hbm, sem_a.at[1])
    load_sums.start()
    steps = []
    for k, (which, row) in enumerate(parts):
        src, dst, by = ins[which] if row is None else ins[which].at[row], outs[k], held[k]
        size = dst.shape[0]
        cuts = 4 if size % 32 == 0 or size >= 2048 else 1
        edge = [size // cuts // 8 * 8 * c for c in range(cuts)] + [size]
        for c in range(cuts):
            r = pl.ds(edge[c], edge[c + 1] - edge[c])
            at = len(steps)
            steps.append((
                pltpu.make_async_copy(src.at[r], by.at[r], sems[0].at[at]),
                pltpu.make_async_copy(by.at[r], dst.at[r], sems[1].at[at])))
    for step in steps:
        step[0].start()
    load_sums.wait()
    first = 2 * tiles * lax.axis_index("dp")
    for t in range(affine.shape[0]):
        for c in range(2):
            affine[t, c : c + 1, :] = sums[pl.ds(first + 2 * t + c, 1), :]
    store_affine.start()
    for step in steps:
        step[0].wait()
        step[1].start()
    for step in steps:
        step[1].wait()
    store_affine.wait()


def finish(sums, tiles, arrays, parts):
    any_ = pl.BlockSpec(memory_space=pl.ANY)
    affine = (max(1, tiles), 2, LANES)
    shapes = [arrays[which].shape if row is None else arrays[which].shape[1:] for which, row in parts]
    return pl.pallas_call(
        functools.partial(finish_kernel, parts, len(arrays), tiles),
        out_shape=tuple(jax.ShapeDtypeStruct(shape, F32) for shape in shapes + [affine]),
        in_specs=[any_] * (len(arrays) + 1),
        out_specs=(any_,) * (len(parts) + 1),
        scratch_shapes=[pltpu.VMEM(shape, F32) for shape in shapes + [sums.shape, affine]] + [pltpu.SemaphoreType.DMA((2,))] + [pltpu.SemaphoreType.DMA((4 * len(parts),))] * 2,
        compiler_params=pltpu.CompilerParams(vmem_limit_bytes=63 * 2**20),
        name="finish",
    )(sums, *arrays)


def local(
    images, image_count, image_size, cotangent, stem_weight, split_main, split_side,
    block_reduce, block_spatial, block_transit, merge_weight, affines,
):
    n_dp, n_bn = lax.axis_size("dp"), lax.axis_size("bn")
    grid, cin = cotangent.shape[1], images.shape[3]
    width, half = merge_weight.shape[0], split_main.shape[1]
    share = cin // n_dp
    dims = (grid, cin, width, half, n_dp, n_bn)
    ws = stem_weight.transpose(1, 2, 0, 3).reshape(9 * cin, width)
    w2 = block_spatial.transpose(1, 2, 0, 3).reshape(9 * half, half)
    aff = affines.reshape(-1, LANES, 2).transpose(0, 2, 1).reshape(-1, LANES)
    act, igrad, stem, spatial, merge, transit, reduce, split, sums, *unused = fused(
        dims, image_count, image_size, images[0], cotangent[0], ws, split_main, split_side,
        block_reduce, w2, block_transit, merge_weight, aff)
    mine = affines.shape[0] // n_dp
    act, igrad, stem, spatial, grad_merge, grad_transit, grad_reduce, grad_main, grad_side, affine = finish(
        sums, mine // LANES, [act, igrad, stem, spatial, merge, transit, reduce, split], [(k, None) for k in range(7)] + [(7, 0), (7, 1)])
    activations = act.reshape(1, grid, grid, width)
    image_grad = igrad.reshape(1, 2 * grid, 2 * grid, cin)
    grad_stem = stem.reshape(3, 3, share, width).transpose(2, 0, 1, 3)
    grad_spatial = spatial.reshape(3, 3, share, half).transpose(2, 0, 1, 3)
    if mine % LANES == 0:
        affine_grad = affine.transpose(0, 2, 1).reshape(mine, 2)
    else:
        whole = sums.reshape(-1, 2, LANES).transpose(0, 2, 1).reshape(-1, 2)
        affine_grad = lax.dynamic_slice_in_dim(whole, lax.axis_index("dp") * mine, mine, axis=0)
    return (activations, image_grad, grad_stem, grad_main, grad_side, grad_reduce, grad_spatial, grad_transit, grad_merge, affine_grad)


def solution(mesh):
    rows = P(("dp", "bn"), None, None, None)
    return jax.shard_map(
        local,
        mesh=mesh,
        in_specs=(rows, P(("dp", "bn")), P(("dp", "bn")), rows) + (P(),) * 8,
        out_specs=(
            rows, rows, P("dp", None, None, None), P("dp", None), P("dp", None), P("dp", None),
            P("dp", None, None, None), P("dp", None), P("dp", None), P("dp", None),
        ),
        check_vma=False,
    )
```
